32 devices in a mesh: az: 16 (over z, y, x), rad: 2 (over core).
Axes of the slice: x: 2, y: 2, z: 4, core: 2. Of those that a mesh axis runs over, the one named last changes fastest.
Arguments:
- density: float32 [2, 2048, 16384], P(None, 'rad', 'az'), may hold values from 0.5 to 2
- mom_r: float32 [2, 2048, 16384], P(None, 'rad', 'az'), may hold values from -1 to 1
- mom_phi: float32 [2, 2048, 16384], P(None, 'rad', 'az'), may hold values from 0.5 to 1.5
- potential_kernel: bfloat16 [64, 2048, 2048], P('az', 'rad'), may hold values from -2 to 2
- force_kernel: bfloat16 [64, 2048, 2048], P('az', 'rad'), may hold values from -2 to 2
Outputs:
- new_density: float32 [2, 2048, 16384], P(None, 'rad', 'az')
- new_mom_r: float32 [2, 2048, 16384], P(None, 'rad', 'az')
- new_mom_phi: float32 [2, 2048, 16384], P(None, 'rad', 'az')
- potential: float32 [2048, 16384], P('rad', 'az')
The draws below stay inside these ranges and needn't reach their ends.
All inputs are finite; a program needn't handle non-finite values.
Results may differ from the reference program's by a relative error of at most 0.0015.
The reference program's roundings to bfloat16 on the way count: a program that leaves them out, or rounds other values in their place, can miss the bound.
Values may be sent and summed in bfloat16 or wider, within the bound.
No kernel may reach another device: no remote copies, remote signals or barrier semaphores. Data moves between devices by JAX's collectives and lax.ppermute only.
A program may use at most 384 MiB of HBM per device.

```python
import math
import jax
import jax.numpy as jnp
from jax import lax

NR = 2048
NAZ = 16384
MODES = 64
LAYERS = 2


def kernel_law(key):
    mode_index = jnp.arange(MODES)
    amplitude = jnp.where(mode_index == 0, 1.0 / LAYERS, math.sqrt(NAZ / (MODES * LAYERS))).astype(jnp.float32)
    entries = jax.random.truncated_normal(key, -4.0, 4.0, (MODES, NR, NR), jnp.float32)
    return (entries * amplitude[:, None, None] / math.sqrt(NR)).astype(jnp.bfloat16)


def draw_potential_kernel(key, part):
    return kernel_law(jax.random.fold_in(key, 11))


def draw_force_kernel(key, part):
    return kernel_law(jax.random.fold_in(key, 23))


def steps_of(rng, shape, shards, low, high):
    level = 1.0
    for axis_at, blocks in shards:
        heights = jax.random.uniform(jax.random.fold_in(jax.random.fold_in(rng, 6), axis_at), (blocks,), jnp.float32, low / len(shards), high / len(shards))
        level = level * jnp.repeat(jnp.exp(heights), shape[axis_at] // blocks).reshape((-1,) + (1,) * (len(shape) - 1 - axis_at))
    return level


def centred(rng, shape, width, most, pieces=(), kind=jnp.bfloat16):
    values = jax.random.normal(rng, shape, jnp.float32) * width
    if len(pieces) > 0:
        values = steps_of(rng, shape, pieces, -0.22, 0.18) * values
    return jnp.clip(values, min=-most, max=most).astype(kind)


def setup_inputs(seed: int = 0) -> dict:
    splits = jax.random.split(jax.random.key(seed), 6)
    density = jnp.clip(0.5 + 1.5 * jax.random.uniform(splits[0], (LAYERS, NR, NAZ), jnp.float32) ** steps_of(splits[0], (LAYERS, NR, NAZ), ((1, 2), (2, 16)), -0.2, 0.2), 0.5, 2.0)
    mom_r = centred(splits[1], (LAYERS, NR, NAZ), 0.2, 1.0, ((1, 2), (2, 16)), jnp.float32)
    mom_phi = jnp.clip(0.5 + 1.0 * jax.random.uniform(splits[2], (LAYERS, NR, NAZ), jnp.float32) ** steps_of(splits[2], (LAYERS, NR, NAZ), ((1, 2), (2, 16)), -0.2, 0.2), 0.5, 1.5)
    potential_kernel = draw_potential_kernel(jax.random.fold_in(splits[5], 71), 0)
    force_kernel = draw_force_kernel(jax.random.fold_in(splits[5], 71), 0)
    return dict(density=density, mom_r=mom_r, mom_phi=mom_phi, potential_kernel=potential_kernel, force_kernel=force_kernel)


aspect_sq = 0.0025

def mode_table(azimuth):
    mode_index = jnp.arange(MODES).astype(jnp.float32)
    angles = azimuth[:, None] * mode_index[None, :]
    basis = jnp.stack([jnp.cos(angles), jnp.sin(angles)], axis=-1).reshape(azimuth.shape[0], 2 * MODES)
    slope = jnp.stack([-mode_index * jnp.sin(angles), mode_index * jnp.cos(angles)], axis=-1).reshape(azimuth.shape[0], 2 * MODES)
    return (basis, slope)

def radial_flux(lower_side, upper_side, sound):

    def physical(fields):
        velocity = fields[1] / fields[0]
        flux = jnp.stack([fields[1], fields[1] * velocity + sound * fields[0], fields[2] * velocity])
        return (flux, velocity)
    flux_lower, vel_lower = physical(lower_side)
    flux_upper, vel_upper = physical(upper_side)
    wave_speed = jnp.maximum(jnp.abs(vel_lower), jnp.abs(vel_upper)) + jnp.sqrt(sound)
    return 0.5 * (flux_lower + flux_upper) - 0.5 * wave_speed * (upper_side - lower_side)

def azimuth_flux(lower_side, upper_side, sound):

    def physical(fields):
        velocity = fields[2] / fields[0]
        flux = jnp.stack([fields[2], fields[1] * velocity, fields[2] * velocity + sound * fields[0]])
        return (flux, velocity)
    flux_lower, vel_lower = physical(lower_side)
    flux_upper, vel_upper = physical(upper_side)
    wave_speed = jnp.maximum(jnp.abs(vel_lower), jnp.abs(vel_upper)) + jnp.sqrt(sound)
    return 0.5 * (flux_lower + flux_upper) - 0.5 * wave_speed * (upper_side - lower_side)

def tendency(fields, radial_ext, azimuth_ext, face_radius, grav_radial, grav_azimuth, cell_step):
    inner_radius = face_radius[:-1]
    outer_radius = face_radius[1:]
    mid_radius = 0.5 * (inner_radius + outer_radius)
    cell_area = 0.5 * (outer_radius * outer_radius - inner_radius * inner_radius)
    sound_face = (aspect_sq / face_radius)[:, None]
    sound_mid = (aspect_sq / mid_radius)[:, None]
    flux_rad = radial_flux(radial_ext[:, :, :-1], radial_ext[:, :, 1:], sound_face)
    flux_azi = azimuth_flux(azimuth_ext[..., :-1], azimuth_ext[..., 1:], sound_mid)
    weighted = flux_rad * face_radius[:, None]
    divergence = (weighted[:, :, 1:] - weighted[:, :, :-1]) / cell_area[:, None]
    divergence = divergence + (flux_azi[..., 1:] - flux_azi[..., :-1]) / (mid_radius[:, None] * cell_step)
    surface_now = fields[0]
    radial_mom = fields[1]
    spin_mom = fields[2]
    centre = mid_radius[:, None]
    source_rad = (spin_mom * spin_mom / surface_now + sound_mid * surface_now) / centre
    source_rad = source_rad + surface_now * (grav_radial / cell_step - 1.0 / (centre * centre))
    source_azi = -radial_mom * spin_mom / (surface_now * centre) + surface_now * (grav_azimuth / cell_step)
    source = jnp.stack([jnp.zeros_like(surface_now), source_rad, source_azi])
    return fields + 0.1 * cell_step * (source - divergence)

def reference(density, mom_r, mom_phi, potential_kernel, force_kernel):
    highest = lax.Precision.HIGHEST
    cell_step = 2.0 * math.pi / NAZ
    azimuth = (jnp.arange(NAZ).astype(jnp.float32) + 0.5) * cell_step
    basis, slope = mode_table(azimuth)
    surface = lax.optimization_barrier(jnp.sum(density, axis=0))
    density_modes = jnp.dot(surface, basis, precision=highest) / NAZ
    rounded = lax.optimization_barrier(density_modes.astype(jnp.bfloat16))
    mode_pairs = rounded.astype(jnp.float32).reshape(NR, MODES, 2)
    pot_modes = jnp.einsum('krs,skc->rkc', potential_kernel.astype(jnp.float32), mode_pairs, precision=highest).reshape(NR, 2 * MODES)
    force_modes = jnp.einsum('krs,skc->rkc', force_kernel.astype(jnp.float32), mode_pairs, precision=highest).reshape(NR, 2 * MODES)
    potential = jnp.dot(pot_modes, basis.T, precision=highest)
    grav_radial = jnp.dot(force_modes, basis.T, precision=highest)
    face_radius = jnp.exp(jnp.arange(NR + 1).astype(jnp.float32) * cell_step)
    mid_radius = 0.5 * (face_radius[:-1] + face_radius[1:])
    grav_azimuth = -jnp.dot(pot_modes, slope.T, precision=highest) / mid_radius[:, None]
    fields = jnp.stack([density, mom_r, mom_phi])
    updated = []
    for layer_index in range(LAYERS):
        column = fields[:, layer_index:layer_index + 1]
        radial_ext = jnp.concatenate([column[:, :, :1], column, column[:, :, -1:]], axis=2)
        azimuth_ext = jnp.concatenate([column[..., -1:], column, column[..., :1]], axis=3)
        updated.append(tendency(column, radial_ext, azimuth_ext, face_radius, grav_radial, grav_azimuth, cell_step))
    result = jnp.concatenate(updated, axis=1)
    return (result[0], result[1], result[2], potential)
```

```python
import math

import jax
import jax.numpy as jnp
from jax import lax
from jax.experimental import pallas as pl
from jax.experimental.pallas import tpu as pltpu
from jax.sharding import PartitionSpec as P

aspect_sq = 0.0025
LANES = 128
SUB = 8
MIB = 1 << 20


def split_bf16(x):
    high = x.astype(jnp.bfloat16)
    low = (x - high.astype(jnp.float32)).astype(jnp.bfloat16)
    return high, low


def modes_kernel(scale, density_ref, basis_ref, out_ref):
    surface = density_ref[0]
    for layer in range(1, density_ref.shape[0]):
        surface = surface + density_ref[layer]
    out_ref[...] = scale * lax.dot_general(
        basis_ref[...],
        surface,
        (((1,), (1,)), ((), ())),
        precision=lax.Precision.HIGHEST,
        preferred_element_type=jnp.float32,
    )


def surface_modes(density, basis, scale):
    layers, rows, cells = density.shape
    cols = basis.shape[0]
    block = min(rows, LANES)
    return pl.pallas_call(
        lambda *refs: modes_kernel(scale, *refs),
        grid=(rows // block,),
        in_specs=[
            pl.BlockSpec((layers, block, cells), lambda i: (0, i, 0)),
            pl.BlockSpec((cols, cells), lambda i: (0, 0)),
        ],
        out_specs=pl.BlockSpec((cols, block), lambda i: (0, i)),
        out_shape=jax.ShapeDtypeStruct((cols, rows), jnp.float32),
        compiler_params=pltpu.CompilerParams(vmem_limit_bytes=16 * MIB),
        cost_estimate=pl.CostEstimate(
            flops=12 * rows * cells * cols, bytes_accessed=4 * density.size, transcendentals=0
        ),
        name="surface_modes",
    )(density, basis)


def response_kernel(mode_count, pairs_ref, pot_ref, force_ref, out_ref):
    pairs = pairs_ref[...]
    row = lax.broadcasted_iota(jnp.int32, out_ref.shape[1:], 0) // 2
    for place, ref in enumerate((pot_ref, force_ref)):
        total = jnp.zeros(out_ref.shape[1:], jnp.float32)
        for mode in range(mode_count):
            part = lax.dot_general(
                pairs, ref[mode], (((1,), (1,)), ((), ())), preferred_element_type=jnp.float32
            )
            total = jnp.where(row == mode, part, total)
        out_ref[place] = total


def responses(pairs, potential_kernel, force_kernel):
    mode_count, rows, count = potential_kernel.shape
    cols = pairs.shape[0]
    block = min(rows, LANES)
    kernel_spec = pl.BlockSpec((mode_count, block, count), lambda i: (0, i, 0))
    return pl.pallas_call(
        lambda *refs: response_kernel(mode_count, *refs),
        grid=(rows // block,),
        in_specs=[pl.BlockSpec((cols, count), lambda i: (0, 0)), kernel_spec, kernel_spec],
        out_specs=pl.BlockSpec((2, cols, block), lambda i: (0, 0, i)),
        out_shape=jax.ShapeDtypeStruct((2, cols, rows), jnp.float32),
        compiler_params=pltpu.CompilerParams(vmem_limit_bytes=16 * MIB),
        cost_estimate=pl.CostEstimate(
            flops=4 * rows * count * cols * mode_count,
            bytes_accessed=4 * potential_kernel.size,
            transcendentals=0,
        ),
        name="responses",
    )(pairs, potential_kernel, force_kernel)


ROOT_FACE, SOUND_FACE, IN, OUT, ROOT_MID, SOUND_MID, AZ, SPIN, PULL = range(9)
COEFS = 16


def row_coefficients(first_row, rows, step):
    face = jnp.exp((first_row + jnp.arange(rows + SUB + 1)).astype(jnp.float32) * step)
    inner, outer = face[:-1], face[1:]
    mid = 0.5 * (inner + outer)
    area = 0.5 * (outer * outer - inner * inner)
    sound_face = aspect_sq / inner
    sound_mid = aspect_sq / mid
    radial = (0.05 * step) / area
    columns = [
        jnp.sqrt(sound_face),
        sound_face,
        radial * inner,
        radial * outer,
        jnp.sqrt(sound_mid),
        sound_mid,
        0.05 / mid,
        (0.1 * step) / mid,
        (0.1 * step) / (mid * mid),
    ]
    columns += [jnp.zeros_like(mid)] * (COEFS - len(columns))
    return jnp.stack(columns, axis=1)


def inverse(x):
    guess = pl.reciprocal(x, approx=True)
    return guess * (2.0 - x * guess)


def flux_kernel(block_count, refs):
    fields = refs[0:3]
    before = refs[3:6]
    after = refs[6:9]
    rim_in, rim_out, ghost_ref, coef_ref, coef_next = refs[9:14]
    outs = refs[-5:-2]
    above, lagged = refs[-2:]
    rows, cells = fields[0].shape
    columns = cells // LANES
    strips = rows // SUB
    index = pl.program_id(0)
    lane = lax.broadcasted_iota(jnp.int32, (SUB, LANES), 1)
    sub = lax.broadcasted_iota(jnp.int32, (SUB, LANES), 0)

    def wide(column):
        return jnp.broadcast_to(column, (SUB, LANES))

    def at(col):
        return pl.ds(col * LANES, LANES)

    def radial_state(state):
        density, mom_r, mom_phi = state
        inv = inverse(density)
        vel = mom_r * inv
        return inv, (density, mom_r, mom_phi, jnp.abs(vel), mom_r * vel, mom_phi * vel)

    def keep_above(col, values):
        for slot, value in enumerate(values):
            above[slot, :, at(col)] = pltpu.roll(value, 1, 0)

    def radial_flux(col, values, root, sound):
        lower = [
            jnp.where(sub == 0, above[slot, :, at(col)], pltpu.roll(value, 1, 0))
            for slot, value in enumerate(values)
        ]
        speed = jnp.maximum(values[3], lower[3]) + root
        return (
            (values[1] + lower[1]) - speed * (values[0] - lower[0]),
            ((values[4] + lower[4]) + sound * (values[0] + lower[0]))
            - speed * (values[1] - lower[1]),
            (values[5] + lower[5]) - speed * (values[2] - lower[2]),
        )

    def finish(rows_before, col, flux, out_coef):
        for comp in range(3):
            up = jnp.where(sub == SUB - 1, pltpu.roll(flux[comp], SUB - 1, 0), lagged[comp, :, at(col)])
            outs[comp][rows_before, at(col)] -= out_coef * up

    def azimuth_flux(values, lower, root):
        speed = jnp.maximum(values[3], lower[3]) + root
        return (
            (values[2] + lower[2]) - speed * (values[0] - lower[0]),
            (values[4] + lower[4]) - speed * (values[1] - lower[1]),
            (values[5] + lower[5]) - speed * (values[2] - lower[2]),
        )

    for col in range(columns):
        state = []
        for comp in range(3):
            row = jnp.where(index == 0, rim_in[comp : comp + 1, at(col)], before[comp][SUB - 1 :, at(col)])
            state.append(jnp.broadcast_to(row, (SUB, LANES)))
        keep_above(col, radial_state(state)[1])

    def strip(place, carry):
        here = pl.ds(pl.multiple_of(place * SUB, SUB), SUB)
        rows_before = pl.ds(pl.multiple_of(jnp.maximum(place - 1, 0) * SUB, SUB), SUB)
        coef = coef_ref[here, :]
        root_face, sound_face, in_coef, root_mid, sound_mid, az, spin, pull = (
            wide(coef[:, k : k + 1])
            for k in (ROOT_FACE, SOUND_FACE, IN, ROOT_MID, SOUND_MID, AZ, SPIN, PULL)
        )
        out_before = wide(coef_ref[rows_before, OUT : OUT + 1])
        ghost = ghost_ref[here, :]

        def azimuth_values(state, inv, cross):
            density, mom_r, mom_phi = state
            vel = mom_phi * inv
            return (
                density, mom_r, mom_phi, jnp.abs(vel), cross, mom_phi * vel + sound_mid * density
            )

        def ghost_values(side):
            state = [wide(ghost[:, 3 * side + k : 3 * side + k + 1]) for k in range(3)]
            inv = inverse(state[0])
            return azimuth_values(state, inv, state[1] * state[2] * inv)

        turned = ghost_values(0)
        held = None
        held_flux = None

        def settle(col, held, held_flux, flux):
            for comp in range(3):
                up = jnp.where(
                    lane == LANES - 1,
                    pltpu.roll(flux[comp], LANES - 1, 1),
                    pltpu.roll(held_flux[comp], LANES - 1, 1),
                )
                outs[comp][here, at(col)] = held[comp] - az * (up - held_flux[comp])

        for col in range(columns):
            state = [ref[here, at(col)] for ref in fields]
            inv, values = radial_state(state)
            flux_r = radial_flux(col, values, root_face, sound_face)
            finish(rows_before, col, flux_r, out_before)
            keep_above(col, values)
            for comp in range(3):
                lagged[comp, :, at(col)] = pltpu.roll(flux_r[comp], SUB - 1, 0)
            values = azimuth_values(state, inv, values[5])
            rolled = [pltpu.roll(value, 1, 1) for value in values]
            lower = [jnp.where(lane == 0, a, b) for a, b in zip(turned, rolled)]
            turned = rolled
            flux = azimuth_flux(values, lower, root_mid)
            if col > 0:
                settle(col - 1, held, held_flux, flux)
            held = (
                state[0] + in_coef * flux_r[0],
                state[1] + in_coef * flux_r[1] + (spin * values[5] - pull * state[0]),
                state[2] + in_coef * flux_r[2] - spin * values[4],
            )
            held_flux = flux
        values = ghost_values(1)
        lower = [wide(a[:, 0:1]) for a in turned]
        settle(columns - 1, held, held_flux, azimuth_flux(values, lower, root_mid))
        return carry

    lax.fori_loop(0, strips, strip, 0)

    last = pl.ds((strips - 1) * SUB, SUB)
    root_face = wide(coef_next[:, ROOT_FACE : ROOT_FACE + 1])
    sound_face = wide(coef_next[:, SOUND_FACE : SOUND_FACE + 1])
    out_coef = wide(coef_ref[last, OUT : OUT + 1])
    for col in range(columns):
        state = []
        for comp in range(3):
            row = jnp.where(
                index == block_count - 1,
                rim_out[comp : comp + 1, at(col)],
                after[comp][0:1, at(col)],
            )
            state.append(jnp.broadcast_to(row, (SUB, LANES)))
        finish(last, col, radial_flux(col, radial_state(state)[1], root_face, sound_face), out_coef)


def flux_layer(layer, fields, rims, ghosts, coefs, so_far):
    layers, rows, cells = fields[0].shape
    block = min(rows, 64)
    count = rows // block
    per = block // SUB
    main = pl.BlockSpec((None, block, cells), lambda i: (layer, i, 0))
    before = pl.BlockSpec((None, SUB, cells), lambda i: (layer, jnp.maximum(i * per - 1, 0), 0))
    after = pl.BlockSpec(
        (None, SUB, cells), lambda i: (layer, jnp.minimum((i + 1) * per, rows // SUB - 1), 0)
    )
    rim = pl.BlockSpec((None, 3, cells), lambda i: (layer, 0, 0))
    operands = [*fields, *fields, *fields, *rims, ghosts, coefs, coefs]
    specs = [main] * 3 + [before] * 3 + [after] * 3 + [
        rim,
        rim,
        pl.BlockSpec((None, block, ghosts.shape[2]), lambda i: (layer, i, 0)),
        pl.BlockSpec((block, COEFS), lambda i: (i, 0)),
        pl.BlockSpec((SUB, COEFS), lambda i: ((i + 1) * per, 0)),
    ]
    aliases = {}
    if so_far is not None:
        for k, array in enumerate(so_far):
            aliases[len(operands)] = k
            operands.append(array)
            specs.append(pl.BlockSpec(memory_space=pl.ANY))
    return pl.pallas_call(
        lambda *refs: flux_kernel(count, refs),
        grid=(count,),
        in_specs=specs,
        out_specs=[main] * 3,
        out_shape=[jax.ShapeDtypeStruct(f.shape, f.dtype) for f in fields],
        scratch_shapes=[
            pltpu.VMEM((6, SUB, cells), jnp.float32),
            pltpu.VMEM((3, SUB, cells), jnp.float32),
        ],
        input_output_aliases=aliases,
        compiler_params=pltpu.CompilerParams(vmem_limit_bytes=16 * MIB),
        cost_estimate=pl.CostEstimate(
            flops=100 * rows * cells, bytes_accessed=24 * rows * cells, transcendentals=rows * cells
        ),
        name="flux_layer",
    )(*operands)


def gravity_kernel(
    pot_ref, force_ref, inverse_ref, table_ref, slope_ref, density_ref, mom_r_ref, mom_phi_ref,
    out_r, out_phi, out_pot,
):
    def left(ref):
        high, low = split_bf16(ref[...])
        return jnp.concatenate([high, low, high], axis=0)

    def product(a, table):
        return lax.dot_general(
            a, table, (((0,), (0,)), ((), ())), preferred_element_type=jnp.float32
        )

    pot, force = left(pot_ref), left(force_ref)
    out_pot[...] = product(pot, table_ref[...])
    radial = product(force, table_ref[...]) * 0.1
    azimuth = product(pot, slope_ref[...]) * inverse_ref[...]
    for layer in range(density_ref.shape[0]):
        density = density_ref[layer]
        out_r[layer] = mom_r_ref[layer] + density * radial
        out_phi[layer] = mom_phi_ref[layer] + density * azimuth


def add_gravity(pot, force, inverse_mid, table, slope, density, mom_r, mom_phi):
    layers, rows, cells = density.shape
    cols = pot.shape[0]
    block = min(rows, LANES)
    modes_spec = pl.BlockSpec((cols, block), lambda i: (0, i))
    table_spec = pl.BlockSpec(table.shape, lambda i: (0, 0))
    field = pl.BlockSpec((layers, block, cells), lambda i: (0, i, 0))
    grid_shape = jax.ShapeDtypeStruct(density.shape, density.dtype)
    return pl.pallas_call(
        gravity_kernel,
        grid=(rows // block,),
        in_specs=[
            modes_spec, modes_spec, pl.BlockSpec((block, 1), lambda i: (i, 0)),
            table_spec, table_spec, field, field, field,
        ],
        out_specs=[field, field, pl.BlockSpec((block, cells), lambda i: (i, 0))],
        out_shape=[grid_shape, grid_shape, jax.ShapeDtypeStruct((rows, cells), jnp.float32)],
        input_output_aliases={6: 0, 7: 1},
        compiler_params=pltpu.CompilerParams(vmem_limit_bytes=24 * MIB),
        cost_estimate=pl.CostEstimate(
            flops=18 * rows * cells * cols, bytes_accessed=44 * rows * cells, transcendentals=0
        ),
        name="add_gravity",
    )(pot, force, inverse_mid, table, slope, density, mom_r, mom_phi)


def exchange_rims(fields, rad_index, rad_count):
    first = jnp.stack([f[:, 0] for f in fields], axis=1)
    last = jnp.stack([f[:, -1] for f in fields], axis=1)
    if rad_count == 1:
        return first, last
    first_out, last_out = first.astype(jnp.bfloat16), last.astype(jnp.bfloat16)
    if rad_count == 2:
        other = lax.ppermute(
            jnp.where(rad_index == 0, last_out, first_out), "rad", [(0, 1), (1, 0)]
        )
        low = high = other
    else:
        up = [(i, i + 1) for i in range(rad_count - 1)]
        low = lax.ppermute(last_out, "rad", up)
        high = lax.ppermute(first_out, "rad", [(b, a) for a, b in up])
    rim_in = jnp.where(rad_index == 0, first, low.astype(first.dtype))
    rim_out = jnp.where(rad_index == rad_count - 1, last, high.astype(last.dtype))
    return rim_in, rim_out


def exchange_edges(fields, az_count):
    right = [(i, (i + 1) % az_count) for i in range(az_count)]
    left = [(b, a) for a, b in right]
    low = lax.ppermute(
        jnp.stack([f[:, :, -1] for f in fields], axis=1).astype(jnp.bfloat16), "az", right
    )
    high = lax.ppermute(
        jnp.stack([f[:, :, 0] for f in fields], axis=1).astype(jnp.bfloat16), "az", left
    )
    both = jnp.concatenate([low, high], axis=1).astype(fields[0].dtype)
    return jnp.swapaxes(both, 1, 2)


def local(az_count, rad_count, density, mom_r, mom_phi, potential_kernel, force_kernel):
    layers, rows, cells = density.shape
    mode_count = potential_kernel.shape[0]
    pair_count = 2 * mode_count
    cols = az_count * pair_count
    step = 2.0 * math.pi / (az_count * cells)
    az_index = lax.axis_index("az")
    rad_index = lax.axis_index("rad")
    fields = (density, mom_r, mom_phi)

    azimuth = ((az_index * cells + jnp.arange(cells)).astype(jnp.float32) + 0.5) * step
    row = lax.broadcasted_iota(jnp.int32, (cols, cells), 0)
    mode = (row // 2).astype(jnp.float32)
    angle = azimuth[None, :] * mode
    cosine, sine = jnp.cos(angle), jnp.sin(angle)
    basis = jnp.where(row % 2 == 0, cosine, sine)
    slope = jnp.where(row % 2 == 0, -mode * sine, mode * cosine)

    rims = exchange_rims(fields, rad_index, rad_count)
    ghosts = exchange_edges(fields, az_count)
    coefs = row_coefficients(rad_index * rows, rows, step)

    partial = surface_modes(density, basis, 1.0 / (az_count * cells))
    pieces = lax.all_to_all(
        partial.reshape(az_count, pair_count, rows), "az", split_axis=0, concat_axis=0, tiled=True
    )
    results = flux_layer(0, fields, rims, ghosts, coefs, None)

    own = jnp.sum(pieces, axis=0).astype(jnp.bfloat16)
    pairs = lax.all_gather(own, "rad", axis=1, tiled=True)
    parts = responses(pairs, potential_kernel, force_kernel)
    every = lax.all_gather(parts, "az", axis=0)
    for layer in range(1, layers):
        results = flux_layer(layer, fields, rims, ghosts, coefs, results)
    pot = every[:, 0].reshape(cols, rows)
    force = every[:, 1].reshape(cols, rows)

    def table_of(x):
        high, low = split_bf16(x)
        return jnp.concatenate([high, high, low], axis=0)

    face = jnp.exp((rad_index * rows + jnp.arange(rows + 1)).astype(jnp.float32) * step)
    inverse_mid = -0.1 / (0.5 * (face[:-1] + face[1:]))
    new_r, new_phi, potential = add_gravity(
        pot, force, inverse_mid[:, None], table_of(basis), table_of(slope), density, results[1], results[2]
    )
    return results[0], new_r, new_phi, potential


def solution(mesh):
    az_count, rad_count = mesh.shape["az"], mesh.shape["rad"]
    field = P(None, "rad", "az")
    kernel = P("az", "rad", None)
    return jax.shard_map(
        lambda *args: local(az_count, rad_count, *args),
        mesh=mesh,
        in_specs=(field, field, field, kernel, kernel),
        out_specs=(field, field, field, P("rad", "az")),
        check_vma=False,
    )
```

```python
import math

import jax
import jax.numpy as jnp
from jax import lax
from jax.experimental import pallas as pl
from jax.experimental.pallas import tpu as pltpu
from jax.sharding import PartitionSpec as P

aspect_sq = 0.0025
LANES = 128
SUB = 8
VMEM_BYTES = 60 << 20


def split_bf16(x):
    high = x.astype(jnp.bfloat16)
    low = (x - high.astype(jnp.float32)).astype(jnp.bfloat16)
    return high, low


def split_outside(x):
    high = lax.reduce_precision(x, 8, 7)
    return high.astype(jnp.bfloat16), (x - high).astype(jnp.bfloat16)


def modes_kernel(scale, density_ref, basis_ref, out_ref):
    surface = density_ref[0]
    for layer in range(1, density_ref.shape[0]):
        surface = surface + density_ref[layer]
    out_ref[...] = scale * lax.dot_general(
        basis_ref[...],
        surface,
        (((1,), (1,)), ((), ())),
        precision=lax.Precision.HIGHEST,
        preferred_element_type=jnp.float32,
    )


def surface_modes(density, basis, scale):
    layers, rows, cells = density.shape
    cols = basis.shape[0]
    block = min(rows, LANES)
    return pl.pallas_call(
        lambda *refs: modes_kernel(scale, *refs),
        grid=(rows // block,),
        in_specs=[
            pl.BlockSpec((layers, block, cells), lambda i: (0, i, 0)),
            pl.BlockSpec((cols, cells), lambda i: (0, 0)),
        ],
        out_specs=pl.BlockSpec((cols, block), lambda i: (0, i)),
        out_shape=jax.ShapeDtypeStruct((cols, rows), jnp.float32),
        compiler_params=pltpu.CompilerParams(vmem_limit_bytes=VMEM_BYTES),
        cost_estimate=pl.CostEstimate(
            flops=12 * rows * cells * cols, bytes_accessed=4 * density.size, transcendentals=0
        ),
        name="surface_modes",
    )(density, basis)


def response_kernel(mode_count, pairs_ref, pot_ref, force_ref, out_ref):
    pairs = pairs_ref[...]
    row = lax.broadcasted_iota(jnp.int32, out_ref.shape[1:], 0) // 2
    for place, ref in enumerate((pot_ref, force_ref)):
        total = jnp.zeros(out_ref.shape[1:], jnp.float32)
        for mode in range(mode_count):
            part = lax.dot_general(
                pairs, ref[mode], (((1,), (1,)), ((), ())), preferred_element_type=jnp.float32
            )
            total = jnp.where(row == mode, part, total)
        out_ref[place] = total


def responses(pairs, potential_kernel, force_kernel):
    mode_count, rows, count = potential_kernel.shape
    cols = pairs.shape[0]
    block = min(rows, LANES)
    kernel_spec = pl.BlockSpec((mode_count, block, count), lambda i: (0, i, 0))
    return pl.pallas_call(
        lambda *refs: response_kernel(mode_count, *refs),
        grid=(rows // block,),
        in_specs=[pl.BlockSpec((cols, count), lambda i: (0, 0)), kernel_spec, kernel_spec],
        out_specs=pl.BlockSpec((2, cols, block), lambda i: (0, 0, i)),
        out_shape=jax.ShapeDtypeStruct((2, cols, rows), jnp.float32),
        compiler_params=pltpu.CompilerParams(vmem_limit_bytes=VMEM_BYTES),
        cost_estimate=pl.CostEstimate(
            flops=4 * rows * count * cols * mode_count,
            bytes_accessed=4 * potential_kernel.size,
            transcendentals=0,
        ),
        name="responses",
    )(pairs, potential_kernel, force_kernel)


ROOT_FACE, SOUND_FACE, FACE, RADIAL, ROOT_MID, SOUND_MID, AZ, SPIN, PULL = range(9)
COEFS = 16


def row_coefficients(first_row, rows, step):
    face = jnp.exp((first_row + jnp.arange(rows + SUB + 1)).astype(jnp.float32) * step)
    inner, outer = face[:-1], face[1:]
    mid = 0.5 * (inner + outer)
    area = 0.5 * (outer * outer - inner * inner)
    sound_face = aspect_sq / inner
    sound_mid = aspect_sq / mid
    columns = [
        jnp.sqrt(sound_face),
        sound_face,
        inner,
        (0.05 * step) / area,
        jnp.sqrt(sound_mid),
        sound_mid,
        0.05 / mid,
        (0.1 * step) / mid,
        (0.1 * step) / (mid * mid),
    ]
    columns += [jnp.zeros_like(mid)] * (COEFS - len(columns))
    return jnp.stack(columns, axis=1)


def inverse(x):
    guess = pl.reciprocal(x, approx=True)
    return guess * (2.0 - x * guess)


def flux_kernel(block_count, refs):
    fields = refs[0:3]
    before = refs[3:6]
    after = refs[6:9]
    rim_in, rim_out, ghost_ref, coef_ref, coef_next = refs[9:14]
    outs = refs[-6:-3]
    cell, face, part = refs[-3:]
    rows, cells = fields[0].shape
    columns = cells // LANES
    strips = rows // SUB
    index = pl.program_id(0)
    lane = lax.broadcasted_iota(jnp.int32, (SUB, LANES), 1)

    def wide(column):
        return jnp.broadcast_to(column, (SUB, LANES))

    def at(col):
        return pl.ds(col * LANES, LANES)

    def rows_at(place):
        return pl.ds(pl.multiple_of(place * SUB, SUB), SUB)

    def radial_state(state):
        density, mom_r, mom_phi = state
        inv = inverse(density)
        vel = mom_r * inv
        return inv, (density, mom_r, mom_phi, jnp.abs(vel), mom_r * vel, mom_phi * vel)

    for col in range(columns):
        for place, edge, rim, near in (
            (0, index == 0, rim_in, [ref[SUB - 1 :, at(col)] for ref in before]),
            (rows + SUB, index == block_count - 1, rim_out, [ref[0:1, at(col)] for ref in after]),
        ):
            state = [
                jnp.broadcast_to(
                    jnp.where(edge, rim[comp : comp + 1, at(col)], near[comp]), (SUB, LANES)
                )
                for comp in range(3)
            ]
            for slot, value in enumerate(radial_state(state)[1]):
                cell[slot, col, pl.ds(place, SUB), :] = value

    def azimuth_flux(values, lower, root):
        speed = jnp.maximum(values[3], lower[3]) + root
        return (
            (values[2] + lower[2]) - speed * (values[0] - lower[0]),
            (values[4] + lower[4]) - speed * (values[1] - lower[1]),
            (values[5] + lower[5]) - speed * (values[2] - lower[2]),
        )

    def first_pass(place, carry):
        here = rows_at(place)
        inside = rows_at(place + 1)
        coef = coef_ref[here, :]
        root_mid, sound_mid, az, spin, pull = (
            wide(coef[:, k : k + 1]) for k in (ROOT_MID, SOUND_MID, AZ, SPIN, PULL)
        )
        ghost = ghost_ref[here, :]

        def azimuth_values(state, inv, cross):
            density, mom_r, mom_phi = state
            vel = mom_phi * inv
            return (
                density, mom_r, mom_phi, jnp.abs(vel), cross, mom_phi * vel + sound_mid * density
            )

        def ghost_values(side):
            state = [wide(ghost[:, 3 * side + k : 3 * side + k + 1]) for k in range(3)]
            inv = inverse(state[0])
            return azimuth_values(state, inv, state[1] * state[2] * inv)

        def settle(col, held, held_flux, flux):
            for comp in range(3):
                up = jnp.where(
                    lane == LANES - 1,
                    pltpu.roll(flux[comp], LANES - 1, 1),
                    pltpu.roll(held_flux[comp], LANES - 1, 1),
                )
                part[comp, here, at(col)] = held[comp] - az * (up - held_flux[comp])

        turned = ghost_values(0)
        held = held_flux = None
        for col in range(columns):
            state = [ref[here, at(col)] for ref in fields]
            inv, values = radial_state(state)
            for slot, value in enumerate(values):
                cell[slot, col, inside, :] = value
            values = azimuth_values(state, inv, values[5])
            rolled = [pltpu.roll(value, 1, 1) for value in values]
            lower = [jnp.where(lane == 0, a, b) for a, b in zip(turned, rolled)]
            turned = rolled
            flux = azimuth_flux(values, lower, root_mid)
            if col > 0:
                settle(col - 1, held, held_flux, flux)
            held = (
                state[0],
                state[1] + (spin * values[5] - pull * state[0]),
                state[2] - spin * values[4],
            )
            held_flux = flux
        values = ghost_values(1)
        lower = [wide(a[:, 0:1]) for a in turned]
        settle(columns - 1, held, held_flux, azimuth_flux(values, lower, root_mid))
        return carry

    lax.fori_loop(0, strips, first_pass, 0)

    def face_flux(place, coef):
        root, sound, radius = (wide(coef[:, k : k + 1]) for k in (ROOT_FACE, SOUND_FACE, FACE))
        start = pl.multiple_of(place * SUB, SUB)
        for col in range(columns):
            upper = [cell[slot, col, pl.ds(start + SUB, SUB), :] for slot in range(6)]
            lower = [cell[slot, col, pl.ds(start + (SUB - 1), SUB), :] for slot in range(6)]
            speed = jnp.maximum(upper[3], lower[3]) + root
            face[0, col, pl.ds(start, SUB), :] = radius * (
                (upper[1] + lower[1]) - speed * (upper[0] - lower[0])
            )
            face[1, col, pl.ds(start, SUB), :] = radius * (
                ((upper[4] + lower[4]) + sound * (upper[0] + lower[0]))
                - speed * (upper[1] - lower[1])
            )
            face[2, col, pl.ds(start, SUB), :] = radius * (
                (upper[5] + lower[5]) - speed * (upper[2] - lower[2])
            )

    def second_pass(place, carry):
        face_flux(place, coef_ref[rows_at(place), :])
        return carry

    lax.fori_loop(0, strips, second_pass, 0)
    face_flux(strips, coef_next[...])

    def third_pass(place, carry):
        here = rows_at(place)
        start = pl.multiple_of(place * SUB, SUB)
        scale = wide(coef_ref[here, RADIAL : RADIAL + 1])
        for col in range(columns):
            for comp in range(3):
                low = face[comp, col, pl.ds(start, SUB), :]
                high = face[comp, col, pl.ds(start + 1, SUB), :]
                outs[comp][here, at(col)] = part[comp, here, at(col)] - scale * (high - low)
        return carry

    lax.fori_loop(0, strips, third_pass, 0)


def flux_layer(layer, fields, rims, ghosts, coefs, so_far):
    layers, rows, cells = fields[0].shape
    block = min(rows, LANES)
    count = rows // block
    per = block // SUB
    main = pl.BlockSpec((None, block, cells), lambda i: (layer, i, 0))
    before = pl.BlockSpec((None, SUB, cells), lambda i: (layer, jnp.maximum(i * per - 1, 0), 0))
    after = pl.BlockSpec(
        (None, SUB, cells), lambda i: (layer, jnp.minimum((i + 1) * per, rows // SUB - 1), 0)
    )
    rim = pl.BlockSpec((None, 3, cells), lambda i: (layer, 0, 0))
    operands = [*fields, *fields, *fields, *rims, ghosts, coefs, coefs]
    specs = [main] * 3 + [before] * 3 + [after] * 3 + [
        rim,
        rim,
        pl.BlockSpec((None, block, ghosts.shape[2]), lambda i: (layer, i, 0)),
        pl.BlockSpec((block, COEFS), lambda i: (i, 0)),
        pl.BlockSpec((SUB, COEFS), lambda i: ((i + 1) * per, 0)),
    ]
    aliases = {}
    if so_far is not None:
        for k, array in enumerate(so_far):
            aliases[len(operands)] = k
            operands.append(array)
            specs.append(pl.BlockSpec(memory_space=pl.ANY))
    return pl.pallas_call(
        lambda *refs: flux_kernel(count, refs),
        grid=(count,),
        in_specs=specs,
        out_specs=[main] * 3,
        out_shape=[jax.ShapeDtypeStruct(f.shape, f.dtype) for f in fields],
        scratch_shapes=[
            pltpu.VMEM((6, cells // LANES, block + 2 * SUB, LANES), jnp.float32),
            pltpu.VMEM((3, cells // LANES, block + SUB, LANES), jnp.float32),
            pltpu.VMEM((3, block, cells), jnp.float32),
        ],
        input_output_aliases=aliases,
        compiler_params=pltpu.CompilerParams(vmem_limit_bytes=VMEM_BYTES),
        cost_estimate=pl.CostEstimate(
            flops=100 * rows * cells, bytes_accessed=24 * rows * cells, transcendentals=rows * cells
        ),
        name="flux_layer",
    )(*operands)


def gravity_kernel(
    pot_ref, force_ref, inverse_ref, table_ref, slope_ref, density_ref, mom_r_ref, mom_phi_ref,
    out_r, out_phi, out_pot,
):
    def left(ref):
        high, low = split_bf16(ref[...])
        return jnp.concatenate([high, low, high], axis=0)

    def product(a, table):
        return lax.dot_general(
            a, table, (((0,), (0,)), ((), ())), preferred_element_type=jnp.float32
        )

    pot, force = left(pot_ref), left(force_ref)
    out_pot[...] = product(pot, table_ref[...])
    radial = product(force, table_ref[...]) * 0.1
    azimuth = product(pot, slope_ref[...]) * inverse_ref[...]
    for layer in range(density_ref.shape[0]):
        density = density_ref[layer]
        out_r[layer] = mom_r_ref[layer] + density * radial
        out_phi[layer] = mom_phi_ref[layer] + density * azimuth


def add_gravity(pot, force, inverse_mid, table, slope, density, mom_r, mom_phi):
    layers, rows, cells = density.shape
    cols = pot.shape[0]
    block = min(rows, LANES)
    modes_spec = pl.BlockSpec((cols, block), lambda i: (0, i))
    table_spec = pl.BlockSpec(table.shape, lambda i: (0, 0))
    field = pl.BlockSpec((layers, block, cells), lambda i: (0, i, 0))
    grid_shape = jax.ShapeDtypeStruct(density.shape, density.dtype)
    return pl.pallas_call(
        gravity_kernel,
        grid=(rows // block,),
        in_specs=[
            modes_spec, modes_spec, pl.BlockSpec((block, 1), lambda i: (i, 0)),
            table_spec, table_spec, field, field, field,
        ],
        out_specs=[field, field, pl.BlockSpec((block, cells), lambda i: (i, 0))],
        out_shape=[grid_shape, grid_shape, jax.ShapeDtypeStruct((rows, cells), jnp.float32)],
        input_output_aliases={6: 0, 7: 1},
        compiler_params=pltpu.CompilerParams(vmem_limit_bytes=VMEM_BYTES),
        cost_estimate=pl.CostEstimate(
            flops=18 * rows * cells * cols, bytes_accessed=44 * rows * cells, transcendentals=0
        ),
        name="add_gravity",
    )(pot, force, inverse_mid, table, slope, density, mom_r, mom_phi)


def exchange_rims(fields, rad_index, rad_count):
    first = jnp.stack([f[:, 0] for f in fields], axis=1)
    last = jnp.stack([f[:, -1] for f in fields], axis=1)
    if rad_count == 1:
        return first, last
    first_out, last_out = first.astype(jnp.bfloat16), last.astype(jnp.bfloat16)
    if rad_count == 2:
        other = lax.ppermute(
            jnp.where(rad_index == 0, last_out, first_out), "rad", [(0, 1), (1, 0)]
        )
        low = high = other
    else:
        up = [(i, i + 1) for i in range(rad_count - 1)]
        low = lax.ppermute(last_out, "rad", up)
        high = lax.ppermute(first_out, "rad", [(b, a) for a, b in up])
    rim_in = jnp.where(rad_index == 0, first, low.astype(first.dtype))
    rim_out = jnp.where(rad_index == rad_count - 1, last, high.astype(last.dtype))
    return rim_in, rim_out


def exchange_edges(fields, az_count):
    right = [(i, (i + 1) % az_count) for i in range(az_count)]
    left = [(b, a) for a, b in right]
    last = lax.optimization_barrier(jnp.stack([f[:, :, -1] for f in fields], axis=1))
    first = lax.optimization_barrier(jnp.stack([f[:, :, 0] for f in fields], axis=1))
    low = lax.ppermute(last.astype(jnp.bfloat16), "az", right)
    high = lax.ppermute(first.astype(jnp.bfloat16), "az", left)
    both = jnp.concatenate([low, high], axis=1).astype(fields[0].dtype)
    return jnp.swapaxes(both, 1, 2)


def local(az_count, rad_count, density, mom_r, mom_phi, potential_kernel, force_kernel):
    layers, rows, cells = density.shape
    mode_count = potential_kernel.shape[0]
    pair_count = 2 * mode_count
    cols = az_count * pair_count
    step = 2.0 * math.pi / (az_count * cells)
    az_index = lax.axis_index("az")
    rad_index = lax.axis_index("rad")
    fields = (density, mom_r, mom_phi)

    azimuth = ((az_index * cells + jnp.arange(cells)).astype(jnp.float32) + 0.5) * step
    row = lax.broadcasted_iota(jnp.int32, (cols, cells), 0)
    mode = (row // 2).astype(jnp.float32)
    angle = azimuth[None, :] * mode
    cosine, sine = jnp.cos(angle), jnp.sin(angle)
    basis = jnp.where(row % 2 == 0, cosine, sine)
    slope = jnp.where(row % 2 == 0, -mode * sine, mode * cosine)

    rims = exchange_rims(fields, rad_index, rad_count)
    ghosts = exchange_edges(fields, az_count)
    coefs = row_coefficients(rad_index * rows, rows, step)

    partial = surface_modes(density, basis, 1.0 / (az_count * cells))
    pieces = lax.all_to_all(
        partial.reshape(az_count, pair_count, rows), "az", split_axis=0, concat_axis=0, tiled=True
    )
    results = flux_layer(0, fields, rims, ghosts, coefs, None)
    pieces, results = lax.optimization_barrier((pieces, results))

    own = jnp.sum(pieces, axis=0).astype(jnp.bfloat16)
    pairs = lax.all_gather(own, "rad", axis=1, tiled=True)
    parts = responses(pairs, potential_kernel, force_kernel)
    every = lax.all_to_all(
        jnp.broadcast_to(parts[None], (az_count, *parts.shape)), "az", split_axis=0, concat_axis=0, tiled=True
    )
    coefs, parts = lax.optimization_barrier((coefs, parts))
    for layer in range(1, layers):
        results = flux_layer(layer, fields, rims, ghosts, coefs, results)
    pot = every[:, 0].reshape(cols, rows)
    force = every[:, 1].reshape(cols, rows)

    def table_of(x):
        high, low = split_outside(x)
        return jnp.concatenate([high, high, low], axis=0)

    face = jnp.exp((rad_index * rows + jnp.arange(rows + 1)).astype(jnp.float32) * step)
    inverse_mid = -0.1 / (0.5 * (face[:-1] + face[1:]))
    new_r, new_phi, potential = add_gravity(
        pot, force, inverse_mid[:, None], table_of(basis), table_of(slope), density, results[1], results[2]
    )
    return results[0], new_r, new_phi, potential


def solution(mesh):
    az_count, rad_count = mesh.shape["az"], mesh.shape["rad"]
    field = P(None, "rad", "az")
    kernel = P("az", "rad", None)
    return jax.shard_map(
        lambda *args: local(az_count, rad_count, *args),
        mesh=mesh,
        in_specs=(field, field, field, kernel, kernel),
        out_specs=(field, field, field, P("rad", "az")),
        check_vma=False,
    )
```

```python
import math

import jax
import jax.numpy as jnp
from jax import lax
from jax.experimental import pallas as pl
from jax.experimental.pallas import tpu as pltpu
from jax.sharding import PartitionSpec as P

aspect_sq = 0.0025
LANES = 128
SUB = 8
VMEM_BYTES = 60 << 20


def split_bf16(x):
    high = x.astype(jnp.bfloat16)
    low = (x - high.astype(jnp.float32)).astype(jnp.bfloat16)
    return high, low


def split_outside(x):
    high = lax.reduce_precision(x, 8, 7)
    return high.astype(jnp.bfloat16), (x - high).astype(jnp.bfloat16)


def modes_kernel(scale, density_ref, basis_ref, out_ref):
    surface = density_ref[0]
    for layer in range(1, density_ref.shape[0]):
        surface = surface + density_ref[layer]
    out_ref[...] = scale * lax.dot_general(
        basis_ref[...],
        surface,
        (((1,), (1,)), ((), ())),
        precision=lax.Precision.HIGHEST,
        preferred_element_type=jnp.float32,
    )


def surface_modes(density, basis, scale):
    layers, rows, cells = density.shape
    cols = basis.shape[0]
    block = min(rows, LANES)
    return pl.pallas_call(
        lambda *refs: modes_kernel(scale, *refs),
        grid=(rows // block,),
        in_specs=[
            pl.BlockSpec((layers, block, cells), lambda i: (0, i, 0)),
            pl.BlockSpec((cols, cells), lambda i: (0, 0)),
        ],
        out_specs=pl.BlockSpec((cols, block), lambda i: (0, i)),
        out_shape=jax.ShapeDtypeStruct((cols, rows), jnp.float32),
        compiler_params=pltpu.CompilerParams(vmem_limit_bytes=VMEM_BYTES),
        cost_estimate=pl.CostEstimate(
            flops=12 * rows * cells * cols, bytes_accessed=4 * density.size, transcendentals=0
        ),
        name="surface_modes",
    )(density, basis)


def response_kernel(mode_count, pairs_ref, pot_ref, force_ref, out_ref):
    pairs = pairs_ref[...]
    cols = pairs.shape[0]
    mode_of = lax.broadcasted_iota(jnp.int32, (pot_ref.shape[1], cols), 1) // 2
    for place, ref in enumerate((pot_ref, force_ref)):
        total = jnp.zeros(mode_of.shape, jnp.float32)
        for mode in range(mode_count):
            part = lax.dot_general(
                ref[mode], pairs, (((1,), (1,)), ((), ())), preferred_element_type=jnp.float32
            )
            total = jnp.where(mode_of == mode, part, total)
        out_ref[place] = total.T


def responses(pairs, potential_kernel, force_kernel):
    mode_count, rows, count = potential_kernel.shape
    cols = pairs.shape[0]
    block = min(rows, LANES)
    kernel_spec = pl.BlockSpec((mode_count, block, count), lambda i: (0, i, 0))
    return pl.pallas_call(
        lambda *refs: response_kernel(mode_count, *refs),
        grid=(rows // block,),
        in_specs=[pl.BlockSpec((cols, count), lambda i: (0, 0)), kernel_spec, kernel_spec],
        out_specs=pl.BlockSpec((2, cols, block), lambda i: (0, 0, i)),
        out_shape=jax.ShapeDtypeStruct((2, cols, rows), jnp.float32),
        compiler_params=pltpu.CompilerParams(vmem_limit_bytes=VMEM_BYTES),
        cost_estimate=pl.CostEstimate(
            flops=4 * rows * count * cols * mode_count,
            bytes_accessed=4 * potential_kernel.size,
            transcendentals=0,
        ),
        name="responses",
    )(pairs, potential_kernel, force_kernel)


ROOT_FACE, SOUND_FACE, IN, OUT, ROOT_MID, SOUND_MID, AZ, SPIN, PULL = range(9)
COEFS = 16


def row_coefficients(first_row, rows, step):
    face = jnp.exp((first_row + jnp.arange(rows + SUB + 1)).astype(jnp.float32) * step)
    inner, outer = face[:-1], face[1:]
    mid = 0.5 * (inner + outer)
    area = 0.5 * (outer * outer - inner * inner)
    sound_face = aspect_sq / inner
    sound_mid = aspect_sq / mid
    radial = (0.05 * step) / area
    columns = [
        jnp.sqrt(sound_face),
        sound_face,
        radial * inner,
        radial * outer,
        jnp.sqrt(sound_mid),
        sound_mid,
        0.05 / mid,
        (0.1 * step) / mid,
        (0.1 * step) / (mid * mid),
    ]
    columns += [jnp.zeros_like(mid)] * (COEFS - len(columns))
    return jnp.stack(columns, axis=1)


def inverse(x):
    guess = pl.reciprocal(x, approx=True)
    return guess * (2.0 - x * guess)


def flux_kernel(first_block, block_count, unroll, refs):
    fields = refs[0:3]
    before = refs[3:6]
    after = refs[6:9]
    rim_in, rim_out, ghost_ref, coef_ref, coef_next = refs[9:14]
    outs = refs[-6:-3]
    above, lagged, pending = refs[-3:]
    layers, rows, cells = fields[0].shape
    columns = cells // LANES
    strips = rows // SUB
    index = pl.program_id(0) + first_block
    lane = lax.broadcasted_iota(jnp.int32, (SUB, LANES), 1)
    sub = lax.broadcasted_iota(jnp.int32, (SUB, LANES), 0)

    def wide(column):
        return jnp.broadcast_to(column, (SUB, LANES))

    def at(col):
        return pl.ds(col * LANES, LANES)

    def rows_at(place):
        return pl.ds(pl.multiple_of(place * SUB, SUB), SUB)

    def radial_state(state):
        density, mom_r, mom_phi = state
        inv = inverse(density)
        vel = mom_r * inv
        return inv, (density, mom_r, mom_phi, jnp.abs(vel), mom_r * vel, mom_phi * vel)

    def radial_flux(values, lower, root, sound):
        speed = jnp.maximum(values[3], lower[3]) + root
        return (
            (values[1] + lower[1]) - speed * (values[0] - lower[0]),
            ((values[4] + lower[4]) + sound * (values[0] + lower[0]))
            - speed * (values[1] - lower[1]),
            (values[5] + lower[5]) - speed * (values[2] - lower[2]),
        )

    def azimuth_flux(values, lower, root):
        speed = jnp.maximum(values[3], lower[3]) + root
        return (
            (values[2] + lower[2]) - speed * (values[0] - lower[0]),
            (values[4] + lower[4]) - speed * (values[1] - lower[1]),
            (values[5] + lower[5]) - speed * (values[2] - lower[2]),
        )

    def finish(slot, rows_before, layer, col, turned_flux, out_coef):
        for comp in range(3):
            up = jnp.where(sub == SUB - 1, turned_flux[comp], lagged[slot, layer, comp, :, at(col)])
            outs[comp][layer, rows_before, at(col)] = (
                pending[slot, layer, comp, :, at(col)] - out_coef * up
            )

    def edge_state(layer, col, edge, rim, near, row):
        state = []
        for comp in range(3):
            value = jnp.where(
                edge, rim[layer, comp : comp + 1, at(col)], near[comp][layer, row : row + 1, at(col)]
            )
            state.append(jnp.broadcast_to(value, (SUB, LANES)))
        return radial_state(state)[1]

    for layer in range(layers):
        for col in range(columns):
            values = edge_state(layer, col, index == 0, rim_in, before, SUB - 1)
            for k, value in enumerate(values):
                above[0, layer, k, :, at(col)] = value

    def strip(place, slot):
        later = (slot + 1) % unroll
        here = rows_at(place)
        rows_before = rows_at(jnp.maximum(place - 1, 0))
        coef = coef_ref[here, :]
        root_face, sound_face, in_coef, root_mid, sound_mid, az, spin, pull = (
            wide(coef[:, k : k + 1])
            for k in (ROOT_FACE, SOUND_FACE, IN, ROOT_MID, SOUND_MID, AZ, SPIN, PULL)
        )
        out_before = wide(coef_ref[rows_before, OUT : OUT + 1])

        def azimuth_values(state, inv, cross):
            density, mom_r, mom_phi = state
            vel = mom_phi * inv
            return (
                density, mom_r, mom_phi, jnp.abs(vel), cross, mom_phi * vel + sound_mid * density
            )

        def ghost_values(layer, side):
            ghost = ghost_ref[layer, here, :]
            state = [wide(ghost[:, 3 * side + k : 3 * side + k + 1]) for k in range(3)]
            inv = inverse(state[0])
            return azimuth_values(state, inv, state[1] * state[2] * inv)

        turned = [ghost_values(layer, 0) for layer in range(layers)]
        held = [None] * layers
        turned_held = [None] * layers

        def settle(layer, col, turned_flux):
            for comp in range(3):
                up = jnp.where(lane == LANES - 1, turned_flux[comp], turned_held[layer][comp])
                pending[later, layer, comp, :, at(col)] = held[layer][comp] - az * up

        for col in range(columns):
            for layer in range(layers):
                state = [ref[layer, here, at(col)] for ref in fields]
                inv, values = radial_state(state)
                rolled = [pltpu.roll(value, 1, 0) for value in values]
                lower = [
                    jnp.where(sub == 0, above[slot, layer, k, :, at(col)], value)
                    for k, value in enumerate(rolled)
                ]
                for k, value in enumerate(rolled):
                    above[later, layer, k, :, at(col)] = value
                flux_r = radial_flux(values, lower, root_face, sound_face)
                turned_r = [pltpu.roll(value, SUB - 1, 0) for value in flux_r]
                finish(slot, rows_before, layer, col, turned_r, out_before)
                for comp in range(3):
                    lagged[later, layer, comp, :, at(col)] = turned_r[comp]
                values = azimuth_values(state, inv, values[5])
                rolled = [pltpu.roll(value, 1, 1) for value in values]
                lower = [jnp.where(lane == 0, a, b) for a, b in zip(turned[layer], rolled)]
                turned[layer] = rolled
                flux = azimuth_flux(values, lower, root_mid)
                turned_flux = [pltpu.roll(value, LANES - 1, 1) for value in flux]
                if col > 0:
                    settle(layer, col - 1, turned_flux)
                held[layer] = (
                    state[0] + in_coef * flux_r[0] + az * flux[0],
                    state[1] + in_coef * flux_r[1] + az * flux[1] + (spin * values[5] - pull * state[0]),
                    state[2] + in_coef * flux_r[2] + az * flux[2] - spin * values[4],
                )
                turned_held[layer] = turned_flux
        for layer in range(layers):
            flux = azimuth_flux(ghost_values(layer, 1), turned[layer], root_mid)
            settle(layer, columns - 1, [pltpu.roll(value, LANES - 1, 1) for value in flux])

    def strip_group(group, carry):
        for slot in range(unroll):
            strip(group * unroll + slot, slot)
        return carry

    lax.fori_loop(0, strips // unroll, strip_group, 0)

    last = pl.ds((strips - 1) * SUB, SUB)
    root_face = wide(coef_next[:, ROOT_FACE : ROOT_FACE + 1])
    sound_face = wide(coef_next[:, SOUND_FACE : SOUND_FACE + 1])
    out_coef = wide(coef_ref[last, OUT : OUT + 1])
    for layer in range(layers):
        for col in range(columns):
            values = edge_state(layer, col, index == block_count - 1, rim_out, after, 0)
            lower = [above[0, layer, k, :, at(col)] for k in range(6)]
            flux_r = radial_flux(values, lower, root_face, sound_face)
            finish(0, last, layer, col, [pltpu.roll(value, SUB - 1, 0) for value in flux_r], out_coef)


def flux_rows(first_block, count, fields, rims, ghosts, coefs, so_far):
    layers, rows, cells = fields[0].shape
    block = flux_block(rows)
    per = block // SUB
    unroll = min(2, per)
    main = pl.BlockSpec((layers, block, cells), lambda i: (0, i + first_block, 0))
    before = pl.BlockSpec(
        (layers, SUB, cells), lambda i: (0, jnp.maximum((i + first_block) * per - 1, 0), 0)
    )
    after = pl.BlockSpec(
        (layers, SUB, cells),
        lambda i: (0, jnp.minimum((i + first_block + 1) * per, rows // SUB - 1), 0),
    )
    rim = pl.BlockSpec((layers, 3, cells), lambda i: (0, 0, 0))
    operands = [*fields, *fields, *fields, *rims, ghosts, coefs, coefs]
    specs = [main] * 3 + [before] * 3 + [after] * 3 + [
        rim,
        rim,
        pl.BlockSpec((layers, block, ghosts.shape[2]), lambda i: (0, i + first_block, 0)),
        pl.BlockSpec((block, COEFS), lambda i: (i + first_block, 0)),
        pl.BlockSpec((SUB, COEFS), lambda i: ((i + first_block + 1) * per, 0)),
    ]
    aliases = {}
    if so_far is not None:
        for k, array in enumerate(so_far):
            aliases[len(operands)] = k
            operands.append(array)
            specs.append(pl.BlockSpec(memory_space=pl.ANY))
    return pl.pallas_call(
        lambda *refs: flux_kernel(first_block, rows // block, unroll, refs),
        grid=(count,),
        in_specs=specs,
        out_specs=[main] * 3,
        out_shape=[jax.ShapeDtypeStruct(f.shape, f.dtype) for f in fields],
        scratch_shapes=[
            pltpu.VMEM((unroll, layers, 6, SUB, cells), jnp.float32),
            pltpu.VMEM((unroll, layers, 3, SUB, cells), jnp.float32),
            pltpu.VMEM((unroll, layers, 3, SUB, cells), jnp.float32),
        ],
        input_output_aliases=aliases,
        compiler_params=pltpu.CompilerParams(vmem_limit_bytes=VMEM_BYTES),
        cost_estimate=pl.CostEstimate(
            flops=100 * layers * count * block * cells,
            bytes_accessed=24 * layers * count * block * cells,
            transcendentals=layers * count * block * cells,
        ),
        name="flux_rows",
    )(*operands)


def flux_block(rows):
    return min(rows, 64)


def gravity_kernel(
    pot_ref, force_ref, inverse_ref, table_ref, slope_ref, density_ref, mom_r_ref, mom_phi_ref,
    out_r, out_phi, out_pot,
):
    def left(ref):
        high, low = split_bf16(ref[...])
        return jnp.concatenate([high, low, high], axis=0)

    def product(a, table):
        return lax.dot_general(
            a, table, (((0,), (0,)), ((), ())), preferred_element_type=jnp.float32
        )

    pot, force = left(pot_ref), left(force_ref)
    out_pot[...] = product(pot, table_ref[...])
    radial = product(force, table_ref[...]) * 0.1
    azimuth = product(pot, slope_ref[...]) * inverse_ref[...]
    for layer in range(density_ref.shape[0]):
        density = density_ref[layer]
        out_r[layer] = mom_r_ref[layer] + density * radial
        out_phi[layer] = mom_phi_ref[layer] + density * azimuth


def add_gravity(pot, force, inverse_mid, table, slope, density, mom_r, mom_phi):
    layers, rows, cells = density.shape
    cols = pot.shape[0]
    block = min(rows, LANES)
    modes_spec = pl.BlockSpec((cols, block), lambda i: (0, i))
    table_spec = pl.BlockSpec(table.shape, lambda i: (0, 0))
    field = pl.BlockSpec((layers, block, cells), lambda i: (0, i, 0))
    grid_shape = jax.ShapeDtypeStruct(density.shape, density.dtype)
    return pl.pallas_call(
        gravity_kernel,
        grid=(rows // block,),
        in_specs=[
            modes_spec, modes_spec, pl.BlockSpec((block, 1), lambda i: (i, 0)),
            table_spec, table_spec, field, field, field,
        ],
        out_specs=[field, field, pl.BlockSpec((block, cells), lambda i: (i, 0))],
        out_shape=[grid_shape, grid_shape, jax.ShapeDtypeStruct((rows, cells), jnp.float32)],
        input_output_aliases={6: 0, 7: 1},
        compiler_params=pltpu.CompilerParams(vmem_limit_bytes=VMEM_BYTES),
        cost_estimate=pl.CostEstimate(
            flops=18 * rows * cells * cols, bytes_accessed=44 * rows * cells, transcendentals=0
        ),
        name="add_gravity",
    )(pot, force, inverse_mid, table, slope, density, mom_r, mom_phi)


def exchange_rims(fields, rad_index, rad_count):
    first = jnp.stack([f[:, 0] for f in fields], axis=1)
    last = jnp.stack([f[:, -1] for f in fields], axis=1)
    if rad_count == 1:
        return first, last
    first_out, last_out = first.astype(jnp.bfloat16), last.astype(jnp.bfloat16)
    if rad_count == 2:
        other = lax.ppermute(
            jnp.where(rad_index == 0, last_out, first_out), "rad", [(0, 1), (1, 0)]
        )
        low = high = other
    else:
        up = [(i, i + 1) for i in range(rad_count - 1)]
        low = lax.ppermute(last_out, "rad", up)
        high = lax.ppermute(first_out, "rad", [(b, a) for a, b in up])
    rim_in = jnp.where(rad_index == 0, first, low.astype(first.dtype))
    rim_out = jnp.where(rad_index == rad_count - 1, last, high.astype(last.dtype))
    return rim_in, rim_out


def exchange_edges(fields, az_count):
    right = [(i, (i + 1) % az_count) for i in range(az_count)]
    left = [(b, a) for a, b in right]
    last = lax.optimization_barrier(jnp.stack([f[:, :, -1] for f in fields], axis=1))
    first = lax.optimization_barrier(jnp.stack([f[:, :, 0] for f in fields], axis=1))
    low = lax.ppermute(last.astype(jnp.bfloat16), "az", right)
    high = lax.ppermute(first.astype(jnp.bfloat16), "az", left)
    both = jnp.concatenate([low, high], axis=1).astype(fields[0].dtype)
    return jnp.swapaxes(both, 1, 2)


def local(az_count, rad_count, density, mom_r, mom_phi, potential_kernel, force_kernel):
    layers, rows, cells = density.shape
    mode_count = potential_kernel.shape[0]
    pair_count = 2 * mode_count
    cols = az_count * pair_count
    step = 2.0 * math.pi / (az_count * cells)
    az_index = lax.axis_index("az")
    rad_index = lax.axis_index("rad")
    fields = (density, mom_r, mom_phi)

    azimuth = ((az_index * cells + jnp.arange(cells)).astype(jnp.float32) + 0.5) * step
    row = lax.broadcasted_iota(jnp.int32, (cols, cells), 0)
    mode = (row // 2).astype(jnp.float32)
    angle = azimuth[None, :] * mode
    cosine, sine = jnp.cos(angle), jnp.sin(angle)
    basis = jnp.where(row % 2 == 0, cosine, sine)
    slope = jnp.where(row % 2 == 0, -mode * sine, mode * cosine)

    rims = exchange_rims(fields, rad_index, rad_count)
    ghosts = exchange_edges(fields, az_count)
    coefs = row_coefficients(rad_index * rows, rows, step)

    partial = surface_modes(density, basis, 1.0 / (az_count * cells))
    pieces = lax.all_to_all(
        partial.reshape(az_count, pair_count, rows), "az", split_axis=0, concat_axis=0, tiled=True
    )
    blocks = rows // flux_block(rows)
    early = blocks // 2
    results = flux_rows(0, early, fields, rims, ghosts, coefs, None) if early else None
    if early:
        pieces, results = lax.optimization_barrier((pieces, results))

    own = jnp.sum(pieces, axis=0).astype(jnp.bfloat16)
    pairs = lax.all_gather(own, "rad", axis=1, tiled=True)
    parts = responses(pairs, potential_kernel, force_kernel)
    every = lax.all_to_all(
        jnp.broadcast_to(parts[None], (az_count, *parts.shape)), "az", split_axis=0, concat_axis=0, tiled=True
    )
    coefs, parts = lax.optimization_barrier((coefs, parts))
    results = flux_rows(early, blocks - early, fields, rims, ghosts, coefs, results)
    pot = every[:, 0].reshape(cols, rows)
    force = every[:, 1].reshape(cols, rows)

    def table_of(x):
        high, low = split_outside(x)
        return jnp.concatenate([high, high, low], axis=0)

    face = jnp.exp((rad_index * rows + jnp.arange(rows + 1)).astype(jnp.float32) * step)
    inverse_mid = -0.1 / (0.5 * (face[:-1] + face[1:]))
    new_r, new_phi, potential = add_gravity(
        pot, force, inverse_mid[:, None], table_of(basis), table_of(slope), density, results[1], results[2]
    )
    return results[0], new_r, new_phi, potential


def solution(mesh):
    az_count, rad_count = mesh.shape["az"], mesh.shape["rad"]
    field = P(None, "rad", "az")
    kernel = P("az", "rad", None)
    return jax.shard_map(
        lambda *args: local(az_count, rad_count, *args),
        mesh=mesh,
        in_specs=(field, field, field, kernel, kernel),
        out_specs=(field, field, field, P("rad", "az")),
        check_vma=False,
    )
```

```python
import math

import jax
import jax.numpy as jnp
from jax import lax
from jax.experimental import pallas as pl
from jax.experimental.pallas import tpu as pltpu
from jax.sharding import PartitionSpec as P

aspect_sq = 0.0025
LANES = 128
SUB = 8
VMEM_BYTES = 60 << 20


def split_bf16(x):
    high = x.astype(jnp.bfloat16)
    low = (x - high.astype(jnp.float32)).astype(jnp.bfloat16)
    return high, low


def split_outside(x):
    high = lax.reduce_precision(x, 8, 7)
    return high.astype(jnp.bfloat16), (x - high).astype(jnp.bfloat16)


def modes_kernel(scale, density_ref, basis_ref, out_ref):
    surface = density_ref[0]
    for layer in range(1, density_ref.shape[0]):
        surface = surface + density_ref[layer]
    out_ref[...] = scale * lax.dot_general(
        basis_ref[...],
        surface,
        (((1,), (1,)), ((), ())),
        precision=lax.Precision.HIGHEST,
        preferred_element_type=jnp.float32,
    )


def surface_modes(density, basis, scale):
    layers, rows, cells = density.shape
    cols = basis.shape[0]
    block = min(rows, LANES)
    return pl.pallas_call(
        lambda *refs: modes_kernel(scale, *refs),
        grid=(rows // block,),
        in_specs=[
            pl.BlockSpec((layers, block, cells), lambda i: (0, i, 0)),
            pl.BlockSpec((cols, cells), lambda i: (0, 0)),
        ],
        out_specs=pl.BlockSpec((cols, block), lambda i: (0, i)),
        out_shape=jax.ShapeDtypeStruct((cols, rows), jnp.float32),
        compiler_params=pltpu.CompilerParams(vmem_limit_bytes=VMEM_BYTES),
        cost_estimate=pl.CostEstimate(
            flops=12 * rows * cells * cols, bytes_accessed=4 * density.size, transcendentals=0
        ),
        name="surface_modes",
    )(density, basis)


def response_kernel(mode_count, pairs_ref, pot_ref, force_ref, out_ref):
    pairs = pairs_ref[...]
    cols = pairs.shape[0]
    mode_of = lax.broadcasted_iota(jnp.int32, (pot_ref.shape[1], cols), 1) // 2
    for place, ref in enumerate((pot_ref, force_ref)):
        total = jnp.zeros(mode_of.shape, jnp.float32)
        for mode in range(mode_count):
            part = lax.dot_general(
                ref[mode], pairs, (((1,), (1,)), ((), ())), preferred_element_type=jnp.float32
            )
            total = jnp.where(mode_of == mode, part, total)
        out_ref[place] = total.T


def responses(pairs, potential_kernel, force_kernel):
    mode_count, rows, count = potential_kernel.shape
    cols = pairs.shape[0]
    block = min(rows, LANES)
    kernel_spec = pl.BlockSpec((mode_count, block, count), lambda i: (0, i, 0))
    return pl.pallas_call(
        lambda *refs: response_kernel(mode_count, *refs),
        grid=(rows // block,),
        in_specs=[pl.BlockSpec((cols, count), lambda i: (0, 0)), kernel_spec, kernel_spec],
        out_specs=pl.BlockSpec((2, cols, block), lambda i: (0, 0, i)),
        out_shape=jax.ShapeDtypeStruct((2, cols, rows), jnp.float32),
        compiler_params=pltpu.CompilerParams(vmem_limit_bytes=VMEM_BYTES),
        cost_estimate=pl.CostEstimate(
            flops=4 * rows * count * cols * mode_count,
            bytes_accessed=4 * potential_kernel.size,
            transcendentals=0,
        ),
        name="responses",
    )(pairs, potential_kernel, force_kernel)


ROOT_FACE, SOUND_FACE, IN, OUT, ROOT_MID, SOUND_MID, AZ, SPIN, PULL = range(9)
COEFS_USED = 9
ROOT_START, SOUND_START = 9, 10
COEFS = 16


def row_coefficients(first_row, rows, step):
    face = jnp.exp((first_row + jnp.arange(rows + 1)).astype(jnp.float32) * step)
    inner, outer = face[:-1], face[1:]
    mid = 0.5 * (inner + outer)
    area = 0.5 * (outer * outer - inner * inner)
    sound_mid = aspect_sq / mid
    radial = (0.05 * step) / area
    columns = [
        jnp.sqrt(aspect_sq / outer),
        aspect_sq / outer,
        radial * inner,
        radial * outer,
        jnp.sqrt(sound_mid),
        sound_mid,
        0.05 / mid,
        (0.1 * step) / mid,
        (0.1 * step) / (mid * mid),
        jnp.sqrt(aspect_sq / inner),
        aspect_sq / inner,
    ]
    columns += [jnp.zeros_like(mid)] * (COEFS - len(columns))
    return jnp.stack(columns, axis=1)


def inverse(x):
    guess = pl.reciprocal(x, approx=True)
    return guess * (2.0 - x * guess)


def flux_kernel(first_block, block_count, tall, refs):
    fields = refs[0:3]
    before = refs[3:6]
    after = refs[6:9]
    rim_in, rim_out, ghost_ref, coef_ref = refs[9:13]
    outs = refs[-4:-1]
    below = refs[-1]
    layers, rows, cells = fields[0].shape
    columns = cells // LANES
    strips = rows // (SUB * tall)
    index = pl.program_id(0) + first_block
    lane = lax.broadcasted_iota(jnp.int32, (SUB, LANES), 1)
    sub = lax.broadcasted_iota(jnp.int32, (SUB, LANES), 0)

    def wide(column):
        return jnp.broadcast_to(column, (SUB, LANES))

    def at(col):
        return pl.ds(col * LANES, LANES)

    def radial_state(state):
        density, mom_r, mom_phi = state
        inv = inverse(density)
        vel = mom_r * inv
        return inv, (density, mom_r, mom_phi, jnp.abs(vel), mom_r * vel, mom_phi * vel)

    def radial_flux(upper, lower, root, sound):
        speed = jnp.maximum(upper[3], lower[3]) + root
        return (
            (upper[1] + lower[1]) - speed * (upper[0] - lower[0]),
            ((upper[4] + lower[4]) + sound * (upper[0] + lower[0]))
            - speed * (upper[1] - lower[1]),
            (upper[5] + lower[5]) - speed * (upper[2] - lower[2]),
        )

    def azimuth_flux(upper, lower, root):
        speed = jnp.maximum(upper[3], lower[3]) + root
        return (
            (upper[2] + lower[2]) - speed * (upper[0] - lower[0]),
            (upper[4] + lower[4]) - speed * (upper[1] - lower[1]),
            (upper[5] + lower[5]) - speed * (upper[2] - lower[2]),
        )

    def face_coefs(coef):
        return wide(coef[:, ROOT_FACE : ROOT_FACE + 1]), wide(coef[:, SOUND_FACE : SOUND_FACE + 1])

    @pl.when(pl.program_id(0) == 0)
    def _():
        for layer in range(layers):
            for col in range(columns):
                pair = []
                for comp in range(3):
                    row = jnp.where(
                        index == 0,
                        rim_in[layer, comp : comp + 1, at(col)],
                        before[comp][layer, SUB - 1 :, at(col)],
                    )
                    pair.append((jnp.broadcast_to(row, (SUB, LANES)), fields[comp][layer, 0:SUB, at(col)]))
                lower = radial_state([p[0] for p in pair])[1]
                upper = radial_state([p[1] for p in pair])[1]
                first = coef_ref[0:SUB, :]
                flux = radial_flux(
                    upper,
                    lower,
                    wide(first[:, ROOT_START : ROOT_START + 1]),
                    wide(first[:, SOUND_START : SOUND_START + 1]),
                )
                for comp in range(3):
                    below[layer, comp, :, at(col)] = flux[comp]

    def strip(layer, start, next_row):
        tiles = [pl.ds(pl.multiple_of(start + SUB * k, SUB), SUB) for k in range(tall)]
        raw = [
            [[ref[layer, tile, at(col)] for ref in fields] for tile in tiles] for col in range(columns)
        ]
        beyond = [next_row(layer, col) for col in range(columns)]
        lowest = [[below[layer, comp, :, at(col)] for comp in range(3)] for col in range(columns)]
        coefs = [coef_ref[tile, :] for tile in tiles]
        ghosts = [ghost_ref[layer, tile, :] for tile in tiles]
        stores = []

        rows_of = [
            [wide(coef[:, k : k + 1]) for k in range(COEFS_USED)] for coef in coefs
        ]

        def azimuth_values(k, state, inv, cross):
            density, mom_r, mom_phi = state
            vel = mom_phi * inv
            return (
                density, mom_r, mom_phi, jnp.abs(vel), cross,
                mom_phi * vel + rows_of[k][SOUND_MID] * density,
            )

        def ghost_values(k, side):
            state = [wide(ghosts[k][:, 3 * side + c : 3 * side + c + 1]) for c in range(3)]
            inv = inverse(state[0])
            return azimuth_values(k, state, inv, state[1] * state[2] * inv)

        turned = [ghost_values(k, 0) for k in range(tall)]
        held = [None] * tall
        turned_held = [None] * tall

        def settle(k, col, turned_flux):
            for comp in range(3):
                up = jnp.where(lane == LANES - 1, turned_flux[comp], turned_held[k][comp])
                stores.append((outs[comp], tiles[k], col, held[k][comp] - rows_of[k][AZ] * up))

        for col in range(columns):
            states = [radial_state(state) for state in raw[col]]
            last = radial_state(beyond[col])[1]
            turned_up = [[pltpu.roll(v, SUB - 1, 0) for v in values] for _, values in states]
            turned_up.append([pltpu.roll(v, SUB - 1, 0) for v in last])
            earlier = lowest[col]
            for k in range(tall):
                c = rows_of[k]
                inv, values = states[k]
                upper = [
                    jnp.where(sub == SUB - 1, b, a) for a, b in zip(turned_up[k], turned_up[k + 1])
                ]
                flux_r = radial_flux(upper, values, c[ROOT_FACE], c[SOUND_FACE])
                turned_r = [pltpu.roll(v, 1, 0) for v in flux_r]
                flux_low = [jnp.where(sub == 0, a, b) for a, b in zip(earlier, turned_r)]
                earlier = turned_r

                azimuthal = azimuth_values(k, raw[col][k], inv, values[5])
                rolled = [pltpu.roll(v, 1, 1) for v in azimuthal]
                lower = [jnp.where(lane == 0, a, b) for a, b in zip(turned[k], rolled)]
                turned[k] = rolled
                flux = azimuth_flux(azimuthal, lower, c[ROOT_MID])
                turned_flux = [pltpu.roll(v, LANES - 1, 1) for v in flux]
                if col > 0:
                    settle(k, col - 1, turned_flux)
                sums = [
                    raw[col][k][comp]
                    + (c[IN] * flux_low[comp] - c[OUT] * flux_r[comp])
                    + c[AZ] * flux[comp]
                    for comp in range(3)
                ]
                held[k] = (
                    sums[0],
                    sums[1] + (c[SPIN] * azimuthal[5] - c[PULL] * raw[col][k][0]),
                    sums[2] - c[SPIN] * azimuthal[4],
                )
                turned_held[k] = turned_flux
            lowest[col] = earlier
        for k in range(tall):
            flux = azimuth_flux(ghost_values(k, 1), turned[k], rows_of[k][ROOT_MID])
            settle(k, columns - 1, [pltpu.roll(v, LANES - 1, 1) for v in flux])

        for ref, tile, col, value in stores:
            ref[layer, tile, at(col)] = value
        for col in range(columns):
            for comp in range(3):
                below[layer, comp, :, at(col)] = lowest[col][comp]

    def inside(place, carry):
        start = place * (SUB * tall)
        following = pl.ds(pl.multiple_of(start + SUB * tall, SUB), SUB)
        for layer in range(layers):
            strip(
                layer,
                start,
                lambda layer, col: [ref[layer, following, at(col)] for ref in fields],
            )
        return carry

    lax.fori_loop(0, strips - 1, inside, 0)

    def row_after(layer, col):
        return [
            jnp.broadcast_to(
                jnp.where(
                    index == block_count - 1,
                    rim_out[layer, comp : comp + 1, at(col)],
                    after[comp][layer, 0:1, at(col)],
                ),
                (SUB, LANES),
            )
            for comp in range(3)
        ]

    for layer in range(layers):
        strip(layer, (strips - 1) * SUB * tall, row_after)


def flux_block(rows):
    return min(rows, LANES)


def flux_rows(first_block, count, fields, rims, ghosts, coefs, so_far):
    layers, rows, cells = fields[0].shape
    block = flux_block(rows)
    per = block // SUB
    tall = min(2, per)
    main = pl.BlockSpec((layers, block, cells), lambda i: (0, i + first_block, 0))
    before = pl.BlockSpec((layers, SUB, cells), lambda i: (0, max(first_block * per - 1, 0), 0))
    after = pl.BlockSpec(
        (layers, SUB, cells),
        lambda i: (0, jnp.minimum((i + first_block + 1) * per, rows // SUB - 1), 0),
    )
    rim = pl.BlockSpec((layers, 3, cells), lambda i: (0, 0, 0))
    operands = [*fields, *fields, *fields, *rims, ghosts, coefs]
    specs = [main] * 3 + [before] * 3 + [after] * 3 + [
        rim,
        rim,
        pl.BlockSpec((layers, block, ghosts.shape[2]), lambda i: (0, i + first_block, 0)),
        pl.BlockSpec((block, COEFS), lambda i: (i + first_block, 0)),
    ]
    aliases = {}
    if so_far is not None:
        for k, array in enumerate(so_far):
            aliases[len(operands)] = k
            operands.append(array)
            specs.append(pl.BlockSpec(memory_space=pl.ANY))
    return pl.pallas_call(
        lambda *refs: flux_kernel(first_block, rows // block, tall, refs),
        grid=(count,),
        in_specs=specs,
        out_specs=[main] * 3,
        out_shape=[jax.ShapeDtypeStruct(f.shape, f.dtype) for f in fields],
        scratch_shapes=[pltpu.VMEM((layers, 3, SUB, cells), jnp.float32)],
        input_output_aliases=aliases,
        compiler_params=pltpu.CompilerParams(vmem_limit_bytes=VMEM_BYTES),
        cost_estimate=pl.CostEstimate(
            flops=100 * layers * count * block * cells,
            bytes_accessed=24 * layers * count * block * cells,
            transcendentals=layers * count * block * cells,
        ),
        name="flux_rows",
    )(*operands)


def gravity_kernel(
    pot_ref, force_ref, inverse_ref, table_ref, slope_ref, density_ref, mom_r_ref, mom_phi_ref,
    out_r, out_phi, out_pot,
):
    def left(ref):
        high, low = split_bf16(ref[...])
        return jnp.concatenate([high, low, high], axis=0)

    def product(a, table):
        return lax.dot_general(
            a, table, (((0,), (0,)), ((), ())), preferred_element_type=jnp.float32
        )

    pot, force = left(pot_ref), left(force_ref)
    out_pot[...] = product(pot, table_ref[...])
    radial = product(force, table_ref[...]) * 0.1
    azimuth = product(pot, slope_ref[...]) * inverse_ref[...]
    for layer in range(density_ref.shape[0]):
        density = density_ref[layer]
        out_r[layer] = mom_r_ref[layer] + density * radial
        out_phi[layer] = mom_phi_ref[layer] + density * azimuth


def add_gravity(pot, force, inverse_mid, table, slope, density, mom_r, mom_phi):
    layers, rows, cells = density.shape
    cols = pot.shape[0]
    block = min(rows, LANES)
    modes_spec = pl.BlockSpec((cols, block), lambda i: (0, i))
    table_spec = pl.BlockSpec(table.shape, lambda i: (0, 0))
    field = pl.BlockSpec((layers, block, cells), lambda i: (0, i, 0))
    grid_shape = jax.ShapeDtypeStruct(density.shape, density.dtype)
    return pl.pallas_call(
        gravity_kernel,
        grid=(rows // block,),
        in_specs=[
            modes_spec, modes_spec, pl.BlockSpec((block, 1), lambda i: (i, 0)),
            table_spec, table_spec, field, field, field,
        ],
        out_specs=[field, field, pl.BlockSpec((block, cells), lambda i: (i, 0))],
        out_shape=[grid_shape, grid_shape, jax.ShapeDtypeStruct((rows, cells), jnp.float32)],
        input_output_aliases={6: 0, 7: 1},
        compiler_params=pltpu.CompilerParams(vmem_limit_bytes=VMEM_BYTES),
        cost_estimate=pl.CostEstimate(
            flops=18 * rows * cells * cols, bytes_accessed=44 * rows * cells, transcendentals=0
        ),
        name="add_gravity",
    )(pot, force, inverse_mid, table, slope, density, mom_r, mom_phi)


def exchange_rims(fields, rad_index, rad_count):
    first = jnp.stack([f[:, 0] for f in fields], axis=1)
    last = jnp.stack([f[:, -1] for f in fields], axis=1)
    if rad_count == 1:
        return first, last
    first_out, last_out = first.astype(jnp.bfloat16), last.astype(jnp.bfloat16)
    if rad_count == 2:
        other = lax.ppermute(
            jnp.where(rad_index == 0, last_out, first_out), "rad", [(0, 1), (1, 0)]
        )
        low = high = other
    else:
        up = [(i, i + 1) for i in range(rad_count - 1)]
        low = lax.ppermute(last_out, "rad", up)
        high = lax.ppermute(first_out, "rad", [(b, a) for a, b in up])
    rim_in = jnp.where(rad_index == 0, first, low.astype(first.dtype))
    rim_out = jnp.where(rad_index == rad_count - 1, last, high.astype(last.dtype))
    return rim_in, rim_out


def exchange_edges(fields, az_count):
    right = [(i, (i + 1) % az_count) for i in range(az_count)]
    left = [(b, a) for a, b in right]
    last = lax.optimization_barrier(jnp.stack([f[:, :, -1] for f in fields], axis=1))
    first = lax.optimization_barrier(jnp.stack([f[:, :, 0] for f in fields], axis=1))
    low = lax.ppermute(last.astype(jnp.bfloat16), "az", right)
    high = lax.ppermute(first.astype(jnp.bfloat16), "az", left)
    both = jnp.concatenate([low, high], axis=1).astype(fields[0].dtype)
    return jnp.swapaxes(both, 1, 2)


def local(az_count, rad_count, density, mom_r, mom_phi, potential_kernel, force_kernel):
    layers, rows, cells = density.shape
    mode_count = potential_kernel.shape[0]
    pair_count = 2 * mode_count
    cols = az_count * pair_count
    step = 2.0 * math.pi / (az_count * cells)
    az_index = lax.axis_index("az")
    rad_index = lax.axis_index("rad")
    fields = (density, mom_r, mom_phi)

    azimuth = ((az_index * cells + jnp.arange(cells)).astype(jnp.float32) + 0.5) * step
    row = lax.broadcasted_iota(jnp.int32, (cols, cells), 0)
    mode = (row // 2).astype(jnp.float32)
    angle = azimuth[None, :] * mode
    cosine, sine = jnp.cos(angle), jnp.sin(angle)
    basis = jnp.where(row % 2 == 0, cosine, sine)
    slope = jnp.where(row % 2 == 0, -mode * sine, mode * cosine)

    rims = exchange_rims(fields, rad_index, rad_count)
    ghosts = exchange_edges(fields, az_count)
    coefs = row_coefficients(rad_index * rows, rows, step)

    partial = surface_modes(density, basis, 1.0 / (az_count * cells))
    pieces = lax.all_to_all(
        partial.reshape(az_count, pair_count, rows), "az", split_axis=0, concat_axis=0, tiled=True
    )
    blocks = rows // flux_block(rows)
    early = blocks // 2
    results = flux_rows(0, early, fields, rims, ghosts, coefs, None) if early else None
    if early:
        pieces, results = lax.optimization_barrier((pieces, results))

    own = jnp.sum(pieces, axis=0).astype(jnp.bfloat16)
    pairs = lax.all_gather(own, "rad", axis=1, tiled=True)
    parts = responses(pairs, potential_kernel, force_kernel)
    every = lax.all_to_all(
        jnp.broadcast_to(parts[None], (az_count, *parts.shape)), "az", split_axis=0, concat_axis=0, tiled=True
    )
    coefs, parts = lax.optimization_barrier((coefs, parts))
    results = flux_rows(early, blocks - early, fields, rims, ghosts, coefs, results)
    pot = every[:, 0].reshape(cols, rows)
    force = every[:, 1].reshape(cols, rows)

    def table_of(x):
        high, low = split_outside(x)
        return jnp.concatenate([high, high, low], axis=0)

    face = jnp.exp((rad_index * rows + jnp.arange(rows + 1)).astype(jnp.float32) * step)
    inverse_mid = -0.1 / (0.5 * (face[:-1] + face[1:]))
    new_r, new_phi, potential = add_gravity(
        pot, force, inverse_mid[:, None], table_of(basis), table_of(slope), density, results[1], results[2]
    )
    return results[0], new_r, new_phi, potential


def solution(mesh):
    az_count, rad_count = mesh.shape["az"], mesh.shape["rad"]
    field = P(None, "rad", "az")
    kernel = P("az", "rad", None)
    return jax.shard_map(
        lambda *args: local(az_count, rad_count, *args),
        mesh=mesh,
        in_specs=(field, field, field, kernel, kernel),
        out_specs=(field, field, field, P("rad", "az")),
        check_vma=False,
    )
```

```python
import math

import jax
import jax.numpy as jnp
from jax import lax
from jax.experimental import pallas as pl
from jax.experimental.pallas import tpu as pltpu
from jax.sharding import PartitionSpec as P

aspect_sq = 0.0025
LANES = 128
SUB = 8
VMEM_BYTES = 60 << 20


def split_bf16(x):
    high = x.astype(jnp.bfloat16)
    low = (x - high.astype(jnp.float32)).astype(jnp.bfloat16)
    return high, low


def pieces_of(x, count):
    out = []
    for _ in range(count - 1):
        high = lax.reduce_precision(x, 8, 7)
        out.append(high.astype(jnp.bfloat16))
        x = x - high
    return out + [x.astype(jnp.bfloat16)]


EDGE_ROWS = 16


def modes_kernel(scale, layers, streams, refs):
    density = [refs[layer * streams : (layer + 1) * streams] for layer in range(layers)]
    firsts, lasts = refs[layers * streams : layers * streams + 2], refs[layers * streams + 2 : layers * streams + 4]
    wide_ref, thin_ref, out_ref, first_ref, last_ref = refs[layers * streams + 4 :]
    cols = thin_ref.shape[0] // 2
    total = None
    for stream in range(streams):
        x = density[0][stream][...]
        width = x.shape[1]
        for layer in range(1, layers):
            x = x + density[layer][stream][...]
        here = pl.ds(stream * width, width)
        high = x.astype(jnp.bfloat16)
        x = x - high.astype(jnp.float32)
        mid = x.astype(jnp.bfloat16)
        low = (x - mid.astype(jnp.float32)).astype(jnp.bfloat16)

        def product(a, table):
            return lax.dot_general(
                a, table, (((1,), (1,)), ((), ())), preferred_element_type=jnp.float32
            )

        both = wide_ref[:, here]
        major = product(high, both)
        minor = product(mid, both)
        small = product(low, both[:cols]) + product(high, thin_ref[:cols, here])
        part = major[:, :cols] + (major[:, cols:] + minor[:, :cols] + (minor[:, cols:] + small))
        total = part if total is None else total + part
    out_ref[...] = (scale * total).T

    block = out_ref.shape[1]
    lane = lax.broadcasted_iota(jnp.int32, (block, LANES), 1)
    edges = jnp.zeros((block, LANES), jnp.float32)
    for layer in range(layers):
        sides = (
            (0, 0, (density[layer][0][:, :LANES], firsts[0][layer], firsts[1][layer])),
            (EDGE_ROWS, LANES - 1, (density[layer][-1][:, -LANES:], lasts[0][layer], lasts[1][layer])),
        )
        for base, place, tiles in sides:
            for comp, tile in enumerate(tiles):
                edges = jnp.where(
                    lane == base + 3 * layer + comp,
                    jnp.broadcast_to(tile[:, place : place + 1], (block, LANES)),
                    edges,
                )
    edges = edges.T
    first_ref[...] = edges[:EDGE_ROWS].astype(jnp.bfloat16)
    last_ref[...] = edges[EDGE_ROWS : 2 * EDGE_ROWS].astype(jnp.bfloat16)


def surface_modes(fields, table, thin, scale):
    layers, rows, cells = fields[0].shape
    cols = table.shape[0] // 2
    block = min(rows, LANES)
    streams = min(4, cells // LANES)
    width = cells // streams

    def stream(layer, place):
        return pl.BlockSpec((None, block, width), lambda i: (layer, i, place))

    first = pl.BlockSpec((layers, block, LANES), lambda i: (0, i, 0))
    last = pl.BlockSpec((layers, block, LANES), lambda i: (0, i, cells // LANES - 1))
    table_spec = pl.BlockSpec((2 * cols, cells), lambda i: (0, 0))
    edge_spec = pl.BlockSpec((EDGE_ROWS, block), lambda i: (0, i))
    edge_shape = jax.ShapeDtypeStruct((EDGE_ROWS, rows), jnp.bfloat16)
    return pl.pallas_call(
        lambda *refs: modes_kernel(scale, layers, streams, refs),
        grid=(rows // block,),
        in_specs=[stream(layer, place) for layer in range(layers) for place in range(streams)]
        + [first, first, last, last, table_spec, table_spec],
        out_specs=[pl.BlockSpec((cols, block), lambda i: (0, i)), edge_spec, edge_spec],
        out_shape=[jax.ShapeDtypeStruct((cols, rows), jnp.float32), edge_shape, edge_shape],
        compiler_params=pltpu.CompilerParams(vmem_limit_bytes=VMEM_BYTES),
        cost_estimate=pl.CostEstimate(
            flops=12 * rows * cells * cols, bytes_accessed=4 * fields[0].size, transcendentals=0
        ),
        name="surface_modes",
    )(*[fields[0]] * (layers * streams), fields[1], fields[2], fields[1], fields[2], table, thin)


def response_kernel(mode_count, refs):
    pairs = refs[0][...]
    out_ref = refs[-1]
    cols = pairs.shape[0]
    mode_of = lax.broadcasted_iota(jnp.int32, (refs[1].shape[0], cols), 1) // 2
    for place in range(2):
        total = jnp.zeros(mode_of.shape, jnp.float32)
        for mode in range(mode_count):
            part = lax.dot_general(
                refs[1 + place * mode_count + mode][...],
                pairs,
                (((1,), (1,)), ((), ())),
                preferred_element_type=jnp.float32,
            )
            total = jnp.where(mode_of == mode, part, total)
        out_ref[place] = total.T


def responses(pairs, potential_kernel, force_kernel):
    mode_count, rows, count = potential_kernel.shape
    cols = pairs.shape[0]
    block = min(rows, LANES)

    def stream(mode):
        return pl.BlockSpec((None, block, count), lambda i: (mode, i, 0))

    return pl.pallas_call(
        lambda *refs: response_kernel(mode_count, refs),
        grid=(rows // block,),
        in_specs=[pl.BlockSpec((cols, count), lambda i: (0, 0))]
        + [stream(mode) for mode in range(mode_count)] * 2,
        out_specs=pl.BlockSpec((2, cols, block), lambda i: (0, 0, i)),
        out_shape=jax.ShapeDtypeStruct((2, cols, rows), jnp.float32),
        compiler_params=pltpu.CompilerParams(vmem_limit_bytes=VMEM_BYTES),
        cost_estimate=pl.CostEstimate(
            flops=4 * rows * count * cols * mode_count,
            bytes_accessed=4 * potential_kernel.size,
            transcendentals=0,
        ),
        name="responses",
    )(pairs, *[potential_kernel] * mode_count, *[force_kernel] * mode_count)


ROOT_FACE, SOUND_FACE, IN, OUT, ROOT_MID, SOUND_MID, AZ, SPIN, PULL = range(9)
COEFS_USED = 9
ROOT_START, SOUND_START = 9, 10
COEFS = 16


def row_coefficients(first_row, rows, step):
    face = jnp.exp((first_row + jnp.arange(rows + 1)).astype(jnp.float32) * step)
    inner, outer = face[:-1], face[1:]
    mid = 0.5 * (inner + outer)
    area = 0.5 * (outer * outer - inner * inner)
    sound_mid = aspect_sq / mid
    radial = (0.05 * step) / area
    columns = [
        jnp.sqrt(aspect_sq / outer),
        aspect_sq / outer,
        radial * inner,
        radial * outer,
        jnp.sqrt(sound_mid),
        sound_mid,
        0.05 / mid,
        (0.1 * step) / mid,
        (0.1 * step) / (mid * mid),
        jnp.sqrt(aspect_sq / inner),
        aspect_sq / inner,
    ]
    columns += [jnp.zeros_like(mid)] * (COEFS - len(columns))
    return jnp.stack(columns, axis=0), (-0.1 / mid)[None]


def inverse(x):
    guess = pl.reciprocal(x, approx=True)
    return guess * (2.0 - x * guess)


def flux_kernel(first_block, block_count, tall, refs):
    fields = refs[0:3]
    before = refs[3:6]
    after = refs[6:9]
    rim_in, rim_out, coef_rows, low_rows, high_rows = refs[9:14]
    outs = refs[-5:-2]
    below, side_ref = refs[-2:]
    layers, rows, cells = fields[0].shape
    columns = cells // LANES
    strips = rows // (SUB * tall)
    index = pl.program_id(0) + first_block
    lane = lax.broadcasted_iota(jnp.int32, (SUB, LANES), 1)
    sub = lax.broadcasted_iota(jnp.int32, (SUB, LANES), 0)

    def wide(column):
        return jnp.broadcast_to(column, (SUB, LANES))

    def at(col):
        return pl.ds(col * LANES, LANES)

    def radial_state(state):
        density, mom_r, mom_phi = state
        inv = inverse(density)
        vel = mom_r * inv
        return inv, (density, mom_r, mom_phi, jnp.abs(vel), mom_r * vel, mom_phi * vel)

    def radial_flux(upper, lower, root, sound):
        speed = jnp.maximum(upper[3], lower[3]) + root
        return (
            (upper[1] + lower[1]) - speed * (upper[0] - lower[0]),
            ((upper[4] + lower[4]) + sound * (upper[0] + lower[0]))
            - speed * (upper[1] - lower[1]),
            (upper[5] + lower[5]) - speed * (upper[2] - lower[2]),
        )

    def azimuth_flux(upper, lower, root):
        speed = jnp.maximum(upper[3], lower[3]) + root
        return (
            (upper[2] + lower[2]) - speed * (upper[0] - lower[0]),
            (upper[4] + lower[4]) - speed * (upper[1] - lower[1]),
            (upper[5] + lower[5]) - speed * (upper[2] - lower[2]),
        )

    def face_coefs(coef):
        return wide(coef[:, ROOT_FACE : ROOT_FACE + 1]), wide(coef[:, SOUND_FACE : SOUND_FACE + 1])

    side_rows = jnp.concatenate(
        [coef_rows[...], low_rows[...].astype(jnp.float32), high_rows[...].astype(jnp.float32)], axis=0
    )
    filler = jnp.zeros((LANES - side_rows.shape[0], rows), jnp.float32)
    side_ref[...] = jnp.concatenate([side_rows, filler], axis=0).T

    @pl.when(pl.program_id(0) == 0)
    def _():
        for layer in range(layers):
            for col in range(columns):
                pair = []
                for comp in range(3):
                    row = jnp.where(
                        index == 0,
                        rim_in[layer, comp : comp + 1, at(col)],
                        before[comp][layer, SUB - 1 :, at(col)],
                    )
                    pair.append((jnp.broadcast_to(row, (SUB, LANES)), fields[comp][layer, 0:SUB, at(col)]))
                lower = radial_state([p[0] for p in pair])[1]
                upper = radial_state([p[1] for p in pair])[1]
                first = side_ref[0:SUB, :]
                flux = radial_flux(
                    upper,
                    lower,
                    wide(first[:, ROOT_START : ROOT_START + 1]),
                    wide(first[:, SOUND_START : SOUND_START + 1]),
                )
                for comp in range(3):
                    below[layer, comp, :, at(col)] = flux[comp]

    def strip(layer, start, next_row):
        tiles = [pl.ds(pl.multiple_of(start + SUB * k, SUB), SUB) for k in range(tall)]
        raw = [
            [[ref[layer, tile, at(col)] for ref in fields] for tile in tiles] for col in range(columns)
        ]
        beyond = [next_row(layer, col) for col in range(columns)]
        lowest = [[below[layer, comp, :, at(col)] for comp in range(3)] for col in range(columns)]
        coefs = [side_ref[tile, :] for tile in tiles]
        stores = []

        rows_of = [
            [wide(coef[:, k : k + 1]) for k in range(COEFS_USED)] for coef in coefs
        ]

        def azimuth_values(k, state, inv, cross):
            density, mom_r, mom_phi = state
            vel = mom_phi * inv
            return (
                density, mom_r, mom_phi, jnp.abs(vel), cross,
                mom_phi * vel + rows_of[k][SOUND_MID] * density,
            )

        def ghost_values(k, side):
            base = COEFS + side * EDGE_ROWS + 3 * layer
            state = [wide(coefs[k][:, base + c : base + c + 1]) for c in range(3)]
            inv = inverse(state[0])
            return azimuth_values(k, state, inv, state[1] * state[2] * inv)

        turned = [ghost_values(k, 0) for k in range(tall)]
        held = [None] * tall
        turned_held = [None] * tall

        def settle(k, col, turned_flux):
            for comp in range(3):
                up = jnp.where(lane == LANES - 1, turned_flux[comp], turned_held[k][comp])
                stores.append((outs[comp], tiles[k], col, held[k][comp] - rows_of[k][AZ] * up))

        for col in range(columns):
            states = [radial_state(state) for state in raw[col]]
            last = radial_state(beyond[col])[1]
            turned_up = [[pltpu.roll(v, SUB - 1, 0) for v in values] for _, values in states]
            turned_up.append([pltpu.roll(v, SUB - 1, 0) for v in last])
            earlier = lowest[col]
            for k in range(tall):
                c = rows_of[k]
                inv, values = states[k]
                upper = [
                    jnp.where(sub == SUB - 1, b, a) for a, b in zip(turned_up[k], turned_up[k + 1])
                ]
                flux_r = radial_flux(upper, values, c[ROOT_FACE], c[SOUND_FACE])
                turned_r = [pltpu.roll(v, 1, 0) for v in flux_r]
                flux_low = [jnp.where(sub == 0, a, b) for a, b in zip(earlier, turned_r)]
                earlier = turned_r

                azimuthal = azimuth_values(k, raw[col][k], inv, values[5])
                rolled = [pltpu.roll(v, 1, 1) for v in azimuthal]
                lower = [jnp.where(lane == 0, a, b) for a, b in zip(turned[k], rolled)]
                turned[k] = rolled
                flux = azimuth_flux(azimuthal, lower, c[ROOT_MID])
                turned_flux = [pltpu.roll(v, LANES - 1, 1) for v in flux]
                if col > 0:
                    settle(k, col - 1, turned_flux)
                sums = [
                    raw[col][k][comp]
                    + (c[IN] * flux_low[comp] - c[OUT] * flux_r[comp])
                    + c[AZ] * flux[comp]
                    for comp in range(3)
                ]
                held[k] = (
                    sums[0],
                    sums[1] + (c[SPIN] * azimuthal[5] - c[PULL] * raw[col][k][0]),
                    sums[2] - c[SPIN] * azimuthal[4],
                )
                turned_held[k] = turned_flux
            lowest[col] = earlier
        for k in range(tall):
            flux = azimuth_flux(ghost_values(k, 1), turned[k], rows_of[k][ROOT_MID])
            settle(k, columns - 1, [pltpu.roll(v, LANES - 1, 1) for v in flux])

        for ref, tile, col, value in stores:
            ref[layer, tile, at(col)] = value
        for col in range(columns):
            for comp in range(3):
                below[layer, comp, :, at(col)] = lowest[col][comp]

    def inside(place, carry):
        start = place * (SUB * tall)
        following = pl.ds(pl.multiple_of(start + SUB * tall, SUB), SUB)
        for layer in range(layers):
            strip(
                layer,
                start,
                lambda layer, col: [ref[layer, following, at(col)] for ref in fields],
            )
        return carry

    lax.fori_loop(0, strips - 1, inside, 0)

    def row_after(layer, col):
        return [
            jnp.broadcast_to(
                jnp.where(
                    index == block_count - 1,
                    rim_out[layer, comp : comp + 1, at(col)],
                    after[comp][layer, 0:1, at(col)],
                ),
                (SUB, LANES),
            )
            for comp in range(3)
        ]

    for layer in range(layers):
        strip(layer, (strips - 1) * SUB * tall, row_after)


def flux_block(rows):
    return min(rows, LANES)


def flux_rows(first_block, count, fields, rims, edges, coefs, so_far):
    layers, rows, cells = fields[0].shape
    block = flux_block(rows)
    per = block // SUB
    tall = min(2, per)
    main = pl.BlockSpec((layers, block, cells), lambda i: (0, i + first_block, 0))
    before = pl.BlockSpec((layers, SUB, cells), lambda i: (0, max(first_block * per - 1, 0), 0))
    after = pl.BlockSpec(
        (layers, SUB, cells),
        lambda i: (0, jnp.minimum((i + first_block + 1) * per, rows // SUB - 1), 0),
    )
    rim = pl.BlockSpec((layers, 3, cells), lambda i: (0, 0, 0))
    operands = [*fields, *fields, *fields, *rims, coefs, *edges]
    specs = [main] * 3 + [before] * 3 + [after] * 3 + [
        rim,
        rim,
        pl.BlockSpec((COEFS, block), lambda i: (0, i + first_block)),
        pl.BlockSpec((EDGE_ROWS, block), lambda i: (0, i + first_block)),
        pl.BlockSpec((EDGE_ROWS, block), lambda i: (0, i + first_block)),
    ]
    aliases = {}
    if so_far is not None:
        for k, array in enumerate(so_far):
            aliases[len(operands)] = k
            operands.append(array)
            specs.append(pl.BlockSpec(memory_space=pl.ANY))
    return pl.pallas_call(
        lambda *refs: flux_kernel(first_block, rows // block, tall, refs),
        grid=(count,),
        in_specs=specs,
        out_specs=[main] * 3,
        out_shape=[jax.ShapeDtypeStruct(f.shape, f.dtype) for f in fields],
        scratch_shapes=[
            pltpu.VMEM((layers, 3, SUB, cells), jnp.float32),
            pltpu.VMEM((block, LANES), jnp.float32),
        ],
        input_output_aliases=aliases,
        compiler_params=pltpu.CompilerParams(vmem_limit_bytes=VMEM_BYTES),
        cost_estimate=pl.CostEstimate(
            flops=100 * layers * count * block * cells,
            bytes_accessed=24 * layers * count * block * cells,
            transcendentals=layers * count * block * cells,
        ),
        name="flux_rows",
    )(*operands)


def gravity_kernel(layers, refs):
    pot_ref, force_ref, inverse_ref, table_ref, slope_ref = refs[:5]
    density, mom_r, mom_phi = (refs[5 + k * layers : 5 + (k + 1) * layers] for k in range(3))
    out_r, out_phi, out_pot = refs[5 + 3 * layers :]

    def product(a, table):
        high, low = split_bf16(a)
        return lax.dot_general(
            jnp.concatenate([high, low, high], axis=0),
            table,
            (((0,), (0,)), ((), ())),
            preferred_element_type=jnp.float32,
        )

    pot = pot_ref[...]
    out_pot[...] = product(pot, table_ref[...])
    radial = product(force_ref[...] * 0.1, table_ref[...])
    azimuth = product(pot * inverse_ref[...], slope_ref[...])
    for layer in range(layers):
        here = density[layer][...]
        out_r[layer] = mom_r[layer][...] + here * radial
        out_phi[layer] = mom_phi[layer][...] + here * azimuth


def add_gravity(pot, force, inverse_mid, table, slope, density, mom_r, mom_phi):
    layers, rows, cells = density.shape
    cols = pot.shape[0]
    block = min(rows, LANES)
    modes_spec = pl.BlockSpec((cols, block), lambda i: (0, i))
    table_spec = pl.BlockSpec(table.shape, lambda i: (0, 0))

    def stream(layer):
        return pl.BlockSpec((None, block, cells), lambda i: (layer, i, 0))

    field = pl.BlockSpec((layers, block, cells), lambda i: (0, i, 0))
    grid_shape = jax.ShapeDtypeStruct(density.shape, density.dtype)
    return pl.pallas_call(
        lambda *refs: gravity_kernel(layers, refs),
        grid=(rows // block,),
        in_specs=[
            modes_spec, modes_spec, pl.BlockSpec((1, block), lambda i: (0, i)), table_spec, table_spec,
        ] + [stream(layer) for layer in range(layers)] * 3,
        out_specs=[field, field, pl.BlockSpec((block, cells), lambda i: (i, 0))],
        out_shape=[grid_shape, grid_shape, jax.ShapeDtypeStruct((rows, cells), jnp.float32)],
        input_output_aliases={5 + layers: 0, 5 + 2 * layers: 1} if layers == 1 else {},
        compiler_params=pltpu.CompilerParams(vmem_limit_bytes=VMEM_BYTES),
        cost_estimate=pl.CostEstimate(
            flops=18 * rows * cells * cols, bytes_accessed=44 * rows * cells, transcendentals=0
        ),
        name="add_gravity",
    )(
        pot, force, inverse_mid, table, slope,
        *[density] * layers, *[mom_r] * layers, *[mom_phi] * layers,
    )


def exchange_rims(fields, rad_index, rad_count):
    first = jnp.stack([f[:, 0] for f in fields], axis=1)
    last = jnp.stack([f[:, -1] for f in fields], axis=1)
    if rad_count == 1:
        return first, last
    first_out, last_out = first.astype(jnp.bfloat16), last.astype(jnp.bfloat16)
    if rad_count == 2:
        other = lax.ppermute(
            jnp.where(rad_index == 0, last_out, first_out), "rad", [(0, 1), (1, 0)]
        )
        low = high = other
    else:
        up = [(i, i + 1) for i in range(rad_count - 1)]
        low = lax.ppermute(last_out, "rad", up)
        high = lax.ppermute(first_out, "rad", [(b, a) for a, b in up])
    rim_in = jnp.where(rad_index == 0, first, low.astype(first.dtype))
    rim_out = jnp.where(rad_index == rad_count - 1, last, high.astype(last.dtype))
    return rim_in, rim_out


def exchange_edges(first, last, az_count):
    right = [(i, (i + 1) % az_count) for i in range(az_count)]
    left = [(b, a) for a, b in right]
    return lax.ppermute(last, "az", right), lax.ppermute(first, "az", left)


def local(az_count, rad_count, density, mom_r, mom_phi, potential_kernel, force_kernel):
    layers, rows, cells = density.shape
    mode_count = potential_kernel.shape[0]
    pair_count = 2 * mode_count
    cols = az_count * pair_count
    step = 2.0 * math.pi / (az_count * cells)
    az_index = lax.axis_index("az")
    rad_index = lax.axis_index("rad")
    fields = (density, mom_r, mom_phi)

    azimuth = ((az_index * cells + jnp.arange(cells)).astype(jnp.float32) + 0.5) * step
    row = lax.broadcasted_iota(jnp.int32, (cols, cells), 0)
    mode = (row // 2).astype(jnp.float32)
    angle = azimuth[None, :] * mode
    cosine, sine = jnp.cos(angle), jnp.sin(angle)
    basis = pieces_of(jnp.where(row % 2 == 0, cosine, sine), 3)
    slope = pieces_of(jnp.where(row % 2 == 0, -mode * sine, mode * cosine), 2)
    wide = jnp.concatenate([basis[0], basis[1]], axis=0)
    thin = jnp.concatenate([basis[2], basis[2]], axis=0)

    rims = exchange_rims(fields, rad_index, rad_count)
    coefs, inverse_mid = row_coefficients(rad_index * rows, rows, step)

    partial, first, last = surface_modes(fields, wide, thin, 1.0 / (az_count * cells))
    edges = exchange_edges(first, last, az_count)
    pieces = lax.all_to_all(
        partial.reshape(az_count, pair_count, rows), "az", split_axis=0, concat_axis=0, tiled=True
    )
    blocks = rows // flux_block(rows)
    early = blocks // 2
    results = flux_rows(0, early, fields, rims, edges, coefs, None) if early else None
    if early:
        pieces, results = lax.optimization_barrier((pieces, results))

    own = jnp.sum(pieces, axis=0).astype(jnp.bfloat16)
    pairs = lax.all_gather(own, "rad", axis=1, tiled=True)
    parts = responses(pairs, potential_kernel, force_kernel)
    every = lax.all_to_all(
        jnp.broadcast_to(parts[None], (az_count, *parts.shape)), "az", split_axis=0, concat_axis=0, tiled=True
    )
    coefs, parts = lax.optimization_barrier((coefs, parts))
    results = flux_rows(early, blocks - early, fields, rims, edges, coefs, results)
    pot = every[:, 0].reshape(cols, rows)
    force = every[:, 1].reshape(cols, rows)

    new_r, new_phi, potential = add_gravity(
        pot,
        force,
        inverse_mid,
        jnp.concatenate([basis[0], basis[0], basis[1]], axis=0),
        jnp.concatenate([slope[0], slope[0], slope[1]], axis=0),
        density,
        results[1],
        results[2],
    )
    return results[0], new_r, new_phi, potential


def solution(mesh):
    az_count, rad_count = mesh.shape["az"], mesh.shape["rad"]
    field = P(None, "rad", "az")
    kernel = P("az", "rad", None)
    return jax.shard_map(
        lambda *args: local(az_count, rad_count, *args),
        mesh=mesh,
        in_specs=(field, field, field, kernel, kernel),
        out_specs=(field, field, field, P("rad", "az")),
        check_vma=False,
    )
```

```python
import math

import jax
import jax.numpy as jnp
from jax import lax
from jax.experimental import pallas as pl
from jax.experimental.pallas import tpu as pltpu
from jax.sharding import PartitionSpec as P

aspect_sq = 0.0025
LANES = 128
SUB = 8
VMEM_BYTES = 60 << 20


def fetch_rows(refs, buffers, sems, steps):
    block = refs[0].shape[1] // steps

    def copy(k, place):
        if isinstance(place, int):
            rows = pl.ds(place * block, block)
        else:
            rows = pl.ds(pl.multiple_of(place * block, block), block)
        return pltpu.make_async_copy(refs[k].at[:, rows], buffers[k].at[:, rows], sems.at[k, place])

    @pl.when(pl.program_id(0) == 0)
    def _():
        for place in range(steps):
            for k in range(len(refs)):
                copy(k, place).start()

    for k in range(len(refs)):
        copy(k, pl.program_id(0)).wait()
    return pl.ds(pl.multiple_of(pl.program_id(0) * block, block), block)


def split_bf16(x):
    high = x.astype(jnp.bfloat16)
    low = (x - high.astype(jnp.float32)).astype(jnp.bfloat16)
    return high, low


def pieces_of(x, count):
    out = []
    for _ in range(count - 1):
        high = lax.reduce_precision(x, 8, 7)
        out.append(high.astype(jnp.bfloat16))
        x = x - high
    return out + [x.astype(jnp.bfloat16)]


EDGE_ROWS = 16


def modes_kernel(scale, steps, refs):
    firsts, lasts = refs[1:3], refs[3:5]
    *tables, out_ref, first_ref, last_ref, wide_ref, density, sems = refs[5:]
    thin_ref = tables[2]
    layers, _, cells = density.shape
    streams = min(4, cells // LANES)
    width = cells // streams
    rows_here = fetch_rows(refs[:1], [density], sems, steps)
    cols = thin_ref.shape[0]

    @pl.when(pl.program_id(0) == 0)
    def _():
        wide_ref[:cols] = tables[0][...]
        wide_ref[cols:] = tables[1][...]

    total = None
    for stream in range(streams):
        here = pl.ds(stream * width, width)
        x = density[0, rows_here, here]
        for layer in range(1, layers):
            x = x + density[layer, rows_here, here]
        high = x.astype(jnp.bfloat16)
        x = x - high.astype(jnp.float32)
        mid = x.astype(jnp.bfloat16)
        low = (x - mid.astype(jnp.float32)).astype(jnp.bfloat16)

        def product(a, table):
            return lax.dot_general(
                a, table, (((1,), (1,)), ((), ())), preferred_element_type=jnp.float32
            )

        both = wide_ref[:, here]
        major = product(high, both)
        minor = product(mid, both)
        small = product(low, both[:cols]) + product(high, thin_ref[:, here])
        part = major[:, :cols] + (major[:, cols:] + minor[:, :cols] + (minor[:, cols:] + small))
        total = part if total is None else total + part
    out_ref[...] = (scale * total).T

    block = out_ref.shape[1]
    lane = lax.broadcasted_iota(jnp.int32, (block, LANES), 1)
    edges = jnp.zeros((block, LANES), jnp.float32)
    for layer in range(layers):
        sides = (
            (0, 0, (density[layer, rows_here, :LANES], firsts[0][layer], firsts[1][layer])),
            (
                EDGE_ROWS,
                LANES - 1,
                (density[layer, rows_here, cells - LANES :], lasts[0][layer], lasts[1][layer]),
            ),
        )
        for base, place, tiles in sides:
            for comp, tile in enumerate(tiles):
                edges = jnp.where(
                    lane == base + 3 * layer + comp,
                    jnp.broadcast_to(tile[:, place : place + 1], (block, LANES)),
                    edges,
                )
    edges = edges.T
    first_ref[...] = edges[:EDGE_ROWS].astype(jnp.bfloat16)
    last_ref[...] = edges[EDGE_ROWS : 2 * EDGE_ROWS].astype(jnp.bfloat16)


def surface_modes(fields, tables, scale):
    layers, rows, cells = fields[0].shape
    cols = tables[0].shape[0]
    block = min(rows, LANES)
    first = pl.BlockSpec((layers, block, LANES), lambda i: (0, i, 0))
    last = pl.BlockSpec((layers, block, LANES), lambda i: (0, i, cells // LANES - 1))
    table_spec = pl.BlockSpec((cols, cells), lambda i: (0, 0))
    edge_spec = pl.BlockSpec((EDGE_ROWS, block), lambda i: (0, i))
    edge_shape = jax.ShapeDtypeStruct((EDGE_ROWS, rows), jnp.bfloat16)
    return pl.pallas_call(
        lambda *refs: modes_kernel(scale, rows // block, refs),
        grid=(rows // block,),
        in_specs=[pl.BlockSpec(memory_space=pl.ANY)]
        + [first, first, last, last] + [table_spec] * 3,
        out_specs=[pl.BlockSpec((cols, block), lambda i: (0, i)), edge_spec, edge_spec],
        out_shape=[jax.ShapeDtypeStruct((cols, rows), jnp.float32), edge_shape, edge_shape],
        scratch_shapes=[
            pltpu.VMEM((2 * cols, cells), jnp.bfloat16),
            pltpu.VMEM(fields[0].shape, jnp.float32),
            pltpu.SemaphoreType.DMA((1, rows // block)),
        ],
        compiler_params=pltpu.CompilerParams(vmem_limit_bytes=VMEM_BYTES),
        cost_estimate=pl.CostEstimate(
            flops=12 * rows * cells * cols, bytes_accessed=4 * fields[0].size, transcendentals=0
        ),
        name="surface_modes",
    )(*fields, fields[1], fields[2], *tables)


def response_kernel(steps, refs):
    pairs_ref, pot_ref, force_ref, out_ref, pot_buffer, force_buffer, sems = refs
    pairs = pairs_ref[...]
    buffers = (pot_buffer, force_buffer)
    rows_here = fetch_rows((pot_ref, force_ref), buffers, sems, steps)
    block, cols = out_ref.shape[3], pairs.shape[0]
    mode_of = lax.broadcasted_iota(jnp.int32, (block, cols), 1) // 2
    for place, buffer in enumerate(buffers):
        total = jnp.zeros(mode_of.shape, jnp.float32)
        for mode in range(buffer.shape[0]):
            part = lax.dot_general(
                buffer[mode, rows_here, :],
                pairs,
                (((1,), (1,)), ((), ())),
                preferred_element_type=jnp.float32,
            )
            total = jnp.where(mode_of == mode, part, total)
        out_ref[:, place] = jnp.broadcast_to(total.T[None], (out_ref.shape[0], cols, block))


def responses(pairs, potential_kernel, force_kernel, copies):
    mode_count, rows, count = potential_kernel.shape
    cols = pairs.shape[0]
    block = min(rows, LANES)
    steps = rows // block
    whole = pl.BlockSpec(memory_space=pl.ANY)
    return pl.pallas_call(
        lambda *refs: response_kernel(steps, refs),
        grid=(steps,),
        in_specs=[pl.BlockSpec((cols, count), lambda i: (0, 0)), whole, whole],
        out_specs=pl.BlockSpec((copies, 2, cols, block), lambda i: (0, 0, 0, i)),
        out_shape=jax.ShapeDtypeStruct((copies, 2, cols, rows), jnp.float32),
        scratch_shapes=[
            pltpu.VMEM(potential_kernel.shape, potential_kernel.dtype),
            pltpu.VMEM(force_kernel.shape, force_kernel.dtype),
            pltpu.SemaphoreType.DMA((2, steps)),
        ],
        compiler_params=pltpu.CompilerParams(vmem_limit_bytes=VMEM_BYTES),
        cost_estimate=pl.CostEstimate(
            flops=4 * rows * count * cols * mode_count,
            bytes_accessed=4 * potential_kernel.size,
            transcendentals=0,
        ),
        name="responses",
    )(pairs, potential_kernel, force_kernel)


ROOT_FACE, SOUND_FACE, IN, OUT, ROOT_MID, SOUND_MID, AZ, SPIN, PULL = range(9)
COEFS = 16


def row_coefficients(first_row, rows, step):
    face = jnp.exp((first_row + jnp.arange(rows + LANES + 1)).astype(jnp.float32) * step)
    inner, outer = face[:-1], face[1:]
    mid = 0.5 * (inner + outer)
    area = 0.5 * (outer * outer - inner * inner)
    sound_face = aspect_sq / inner
    sound_mid = aspect_sq / mid
    radial = (0.05 * step) / area
    columns = [
        jnp.sqrt(sound_face),
        sound_face,
        radial * inner,
        radial * outer,
        jnp.sqrt(sound_mid),
        sound_mid,
        0.05 / mid,
        (0.1 * step) / mid,
        (0.1 * step) / (mid * mid),
    ]
    columns += [jnp.zeros_like(mid)] * (COEFS - len(columns))
    return jnp.stack(columns, axis=0), (-0.1 / mid)[None, :rows]


def inverse(x):
    guess = pl.reciprocal(x, approx=True)
    return guess * (2.0 - x * guess)


class FluxBlock:
    def __init__(self, block_count, refs):
        self.fields = refs[0:3]
        self.before = refs[3:6]
        self.after = refs[6:9]
        self.rim_in, self.rim_out, coef_rows, low_rows, high_rows, coef_after = refs[9:15]
        self.block_count = block_count
        self.rows, cells = self.fields[0].shape
        self.columns = cells // LANES
        self.strips = self.rows // SUB
        self.index = pl.program_id(0)
        self.lane = lax.broadcasted_iota(jnp.int32, (SUB, LANES), 1)
        self.sub = lax.broadcasted_iota(jnp.int32, (SUB, LANES), 0)
        side_rows = jnp.concatenate(
            [coef_rows[...], low_rows[...].astype(jnp.float32), high_rows[...].astype(jnp.float32)], axis=0
        )
        filler = jnp.zeros((LANES - side_rows.shape[0], self.rows), jnp.float32)
        self.side = jnp.concatenate([side_rows, filler], axis=0).T
        self.coef_after = coef_after

    def wide(self, column):
        return jnp.broadcast_to(column, (SUB, LANES))

    def at(self, col):
        return pl.ds(col * LANES, LANES)

    def rows_at(self, place):
        return pl.ds(pl.multiple_of(place * SUB, SUB), SUB)

    def radial_state(self, state):
        density, mom_r, mom_phi = state
        inv = inverse(density)
        vel = mom_r * inv
        return inv, (density, mom_r, mom_phi, jnp.abs(vel), mom_r * vel, mom_phi * vel)

    def radial_flux(self, upper, lower, root, sound):
        speed = jnp.maximum(upper[3], lower[3]) + root
        return (
            (upper[1] + lower[1]) - speed * (upper[0] - lower[0]),
            ((upper[4] + lower[4]) + sound * (upper[0] + lower[0]))
            - speed * (upper[1] - lower[1]),
            (upper[5] + lower[5]) - speed * (upper[2] - lower[2]),
        )

    def azimuth_flux(self, upper, lower, root):
        speed = jnp.maximum(upper[3], lower[3]) + root
        return (
            (upper[2] + lower[2]) - speed * (upper[0] - lower[0]),
            (upper[4] + lower[4]) - speed * (upper[1] - lower[1]),
            (upper[5] + lower[5]) - speed * (upper[2] - lower[2]),
        )

    def azimuth_values(self, state, inv, cross, sound):
        density, mom_r, mom_phi = state
        vel = mom_phi * inv
        return density, mom_r, mom_phi, jnp.abs(vel), cross, mom_phi * vel + sound * density

    def ghost_values(self, layer, coef, side, sound):
        base = COEFS + side * EDGE_ROWS + 3 * layer
        state = [self.wide(coef[:, base + c : base + c + 1]) for c in range(3)]
        inv = inverse(state[0])
        return self.azimuth_values(state, inv, state[1] * state[2] * inv, sound)

    def row_before(self, col):
        return self.edge_row(col, self.index == 0, self.rim_in, self.before, SUB - 1)

    def row_after(self, col):
        return self.edge_row(col, self.index == self.block_count - 1, self.rim_out, self.after, 0)

    def edge_row(self, col, edge, rim, near, row):
        state = []
        for comp in range(3):
            value = jnp.where(
                edge, rim[comp : comp + 1, self.at(col)], near[comp][row : row + 1, self.at(col)]
            )
            state.append(jnp.broadcast_to(value, (SUB, LANES)))
        return self.radial_state(state)[1]

    def columns_of(self, coef, names):
        return [self.wide(coef[:, k : k + 1]) for k in names]


def joint_flux(layer, block_count, refs):
    block = FluxBlock(block_count, refs)
    outs = refs[-6:-3]
    above, lagged, side = refs[-3:]
    side[...] = block.side
    lane, sub, at, fields = block.lane, block.sub, block.at, block.fields
    columns = block.columns

    def keep_above(col, rolled):
        for slot, value in enumerate(rolled):
            above[slot, :, at(col)] = value

    def finish(rows_before, col, turned, out_coef):
        for comp in range(3):
            up = jnp.where(sub == SUB - 1, turned[comp], lagged[comp, :, at(col)])
            outs[comp][rows_before, at(col)] -= out_coef * up

    for col in range(columns):
        keep_above(col, block.row_before(col))

    def strip(place, carry):
        here = block.rows_at(place)
        rows_before = block.rows_at(jnp.maximum(place - 1, 0))
        coef = side[here, :]
        root_face, sound_face, in_coef, root_mid, sound_mid, az, spin, pull = block.columns_of(
            coef, (ROOT_FACE, SOUND_FACE, IN, ROOT_MID, SOUND_MID, AZ, SPIN, PULL)
        )
        (out_before,) = block.columns_of(side[rows_before, :], (OUT,))
        turned = block.ghost_values(layer, coef, 0, sound_mid)
        held = held_flux = None

        def settle(col, held, held_flux, flux):
            for comp in range(3):
                up = jnp.where(
                    lane == LANES - 1,
                    pltpu.roll(flux[comp], LANES - 1, 1),
                    pltpu.roll(held_flux[comp], LANES - 1, 1),
                )
                outs[comp][here, at(col)] = held[comp] - az * (up - held_flux[comp])

        for col in range(columns):
            state = [ref[here, at(col)] for ref in fields]
            inv, values = block.radial_state(state)
            rolled = [pltpu.roll(value, 1, 0) for value in values]
            lower = [
                jnp.where(sub == 0, above[slot, :, at(col)], value)
                for slot, value in enumerate(rolled)
            ]
            flux_r = block.radial_flux(values, lower, root_face, sound_face)
            turned_r = [pltpu.roll(value, SUB - 1, 0) for value in flux_r]
            finish(rows_before, col, turned_r, out_before)
            keep_above(col, rolled)
            for comp in range(3):
                lagged[comp, :, at(col)] = turned_r[comp]
            values = block.azimuth_values(state, inv, values[5], sound_mid)
            rolled = [pltpu.roll(value, 1, 1) for value in values]
            lower = [jnp.where(lane == 0, a, b) for a, b in zip(turned, rolled)]
            turned = rolled
            flux = block.azimuth_flux(values, lower, root_mid)
            if col > 0:
                settle(col - 1, held, held_flux, flux)
            held = (
                state[0] + in_coef * flux_r[0],
                state[1] + in_coef * flux_r[1] + (spin * values[5] - pull * state[0]),
                state[2] + in_coef * flux_r[2] - spin * values[4],
            )
            held_flux = flux
        values = block.ghost_values(layer, coef, 1, sound_mid)
        settle(columns - 1, held, held_flux, block.azimuth_flux(values, turned, root_mid))
        return carry

    lax.fori_loop(0, block.strips, strip, 0)

    last = pl.ds((block.strips - 1) * SUB, SUB)
    after = block.coef_after[...].T
    root_face, sound_face = block.columns_of(after[:SUB], (ROOT_FACE, SOUND_FACE))
    (out_coef,) = block.columns_of(side[last, :], (OUT,))
    for col in range(columns):
        lower = [above[slot, :, at(col)] for slot in range(6)]
        flux_r = block.radial_flux(block.row_after(col), lower, root_face, sound_face)
        finish(last, col, [pltpu.roll(value, SUB - 1, 0) for value in flux_r], out_coef)


def split_flux(layer, block_count, refs):
    block = FluxBlock(block_count, refs)
    outs = refs[-7:-4]
    above, lagged, side, part = refs[-4:]
    side[...] = block.side
    lane, sub, at, fields = block.lane, block.sub, block.at, block.fields
    columns = block.columns

    def azimuth_strip(place, carry):
        here = block.rows_at(place)
        coef = side[here, :]
        root_mid, sound_mid, az, spin, pull = block.columns_of(
            coef, (ROOT_MID, SOUND_MID, AZ, SPIN, PULL)
        )
        turned = block.ghost_values(layer, coef, 0, sound_mid)
        held = turned_held = None

        def settle(col, turned_flux):
            for comp in range(3):
                up = jnp.where(lane == LANES - 1, turned_flux[comp], turned_held[comp])
                part[comp, here, at(col)] = held[comp] - az * up

        for col in range(columns):
            state = [ref[here, at(col)] for ref in fields]
            inv = inverse(state[0])
            vel = state[2] * inv
            values = (
                *state, jnp.abs(vel), state[1] * vel, state[2] * vel + sound_mid * state[0]
            )
            rolled = [pltpu.roll(value, 1, 1) for value in values]
            lower = [jnp.where(lane == 0, a, b) for a, b in zip(turned, rolled)]
            turned = rolled
            flux = block.azimuth_flux(values, lower, root_mid)
            turned_flux = [pltpu.roll(value, LANES - 1, 1) for value in flux]
            if col > 0:
                settle(col - 1, turned_flux)
            held = (
                state[0] + az * flux[0],
                state[1] + az * flux[1] + (spin * values[5] - pull * state[0]),
                state[2] + az * flux[2] - spin * values[4],
            )
            turned_held = turned_flux
        flux = block.azimuth_flux(block.ghost_values(layer, coef, 1, sound_mid), turned, root_mid)
        settle(columns - 1, [pltpu.roll(value, LANES - 1, 1) for value in flux])
        return carry

    lax.fori_loop(0, block.strips, azimuth_strip, 0)

    for col in range(columns):
        for slot, value in enumerate(block.row_before(col)):
            above[slot, :, at(col)] = value

    def finish(place, col, turned, in_coef, out_coef):
        here = block.rows_at(place)
        for comp in range(3):
            low = lagged[comp, :, at(col)]
            up = jnp.where(sub == SUB - 1, turned[comp], pltpu.roll(low, SUB - 1, 0))
            outs[comp][here, at(col)] = part[comp, here, at(col)] + (in_coef * low - out_coef * up)

    def radial_strip(place, carry):
        here = block.rows_at(place)
        earlier = jnp.maximum(place - 1, 0)
        root_face, sound_face = block.columns_of(side[here, :], (ROOT_FACE, SOUND_FACE))
        in_coef, out_coef = block.columns_of(side[block.rows_at(earlier), :], (IN, OUT))
        for col in range(columns):
            values = block.radial_state([ref[here, at(col)] for ref in fields])[1]
            rolled = [pltpu.roll(value, 1, 0) for value in values]
            lower = [
                jnp.where(sub == 0, above[slot, :, at(col)], value)
                for slot, value in enumerate(rolled)
            ]
            for slot, value in enumerate(rolled):
                above[slot, :, at(col)] = value
            flux = block.radial_flux(values, lower, root_face, sound_face)
            finish(earlier, col, [pltpu.roll(value, SUB - 1, 0) for value in flux], in_coef, out_coef)
            for comp in range(3):
                lagged[comp, :, at(col)] = flux[comp]
        return carry

    lax.fori_loop(0, block.strips, radial_strip, 0)

    after = block.coef_after[...].T
    root_face, sound_face = block.columns_of(after[:SUB], (ROOT_FACE, SOUND_FACE))
    in_coef, out_coef = block.columns_of(
        side[(block.strips - 1) * SUB : block.strips * SUB, :], (IN, OUT)
    )
    for col in range(columns):
        lower = [above[slot, :, at(col)] for slot in range(6)]
        flux = block.radial_flux(block.row_after(col), lower, root_face, sound_face)
        turned = [pltpu.roll(value, SUB - 1, 0) for value in flux]
        finish(block.strips - 1, col, turned, in_coef, out_coef)


def flux_layer(layer, kernel, fields, rims, edges, coefs, so_far):
    layers, rows, cells = fields[0].shape
    block = min(rows, LANES)
    count = rows // block
    per = block // SUB
    main = pl.BlockSpec((None, block, cells), lambda i: (layer, i, 0))
    before = pl.BlockSpec((None, SUB, cells), lambda i: (layer, jnp.maximum(i * per - 1, 0), 0))
    after = pl.BlockSpec(
        (None, SUB, cells), lambda i: (layer, jnp.minimum((i + 1) * per, rows // SUB - 1), 0)
    )
    rim = pl.BlockSpec((None, 3, cells), lambda i: (layer, 0, 0))
    operands = [*fields, *fields, *fields, *rims, coefs, *edges, coefs]
    specs = [main] * 3 + [before] * 3 + [after] * 3 + [
        rim,
        rim,
        pl.BlockSpec((COEFS, block), lambda i: (0, i)),
        pl.BlockSpec((EDGE_ROWS, block), lambda i: (0, i)),
        pl.BlockSpec((EDGE_ROWS, block), lambda i: (0, i)),
        pl.BlockSpec((COEFS, LANES), lambda i: (0, (i + 1) * (block // LANES))),
    ]
    aliases = {}
    if so_far is not None:
        for k, array in enumerate(so_far):
            aliases[len(operands)] = k
            operands.append(array)
            specs.append(pl.BlockSpec(memory_space=pl.ANY))
    scratch = [
        pltpu.VMEM((6, SUB, cells), jnp.float32),
        pltpu.VMEM((3, SUB, cells), jnp.float32),
        pltpu.VMEM((block, LANES), jnp.float32),
    ]
    if kernel is split_flux:
        scratch.append(pltpu.VMEM((3, block, cells), jnp.float32))
    return pl.pallas_call(
        lambda *refs: kernel(layer, count, refs),
        grid=(count,),
        in_specs=specs,
        out_specs=[main] * 3,
        out_shape=[jax.ShapeDtypeStruct(f.shape, f.dtype) for f in fields],
        scratch_shapes=scratch,
        input_output_aliases=aliases,
        compiler_params=pltpu.CompilerParams(vmem_limit_bytes=VMEM_BYTES),
        cost_estimate=pl.CostEstimate(
            flops=100 * rows * cells, bytes_accessed=24 * rows * cells, transcendentals=rows * cells
        ),
        name=kernel.__name__,
    )(*operands)


def gravity_kernel(steps, refs):
    pot_ref, force_ref, inverse_ref = refs[:3]
    halves = refs[3:7]
    out_r, out_phi, out_pot, table_ref, slope_ref, *buffers, sems = refs[10:]
    density, mom_r, mom_phi = buffers
    rows_here = fetch_rows(refs[7:10], buffers, sems, steps)
    cols = pot_ref.shape[0]

    @pl.when(pl.program_id(0) == 0)
    def _():
        for ref, (high, low) in ((table_ref, halves[:2]), (slope_ref, halves[2:])):
            ref[:cols] = high[...]
            ref[cols : 2 * cols] = high[...]
            ref[2 * cols :] = low[...]


    def product(a, table):
        high, low = split_bf16(a)
        return lax.dot_general(
            jnp.concatenate([high, low, high], axis=0),
            table,
            (((0,), (0,)), ((), ())),
            preferred_element_type=jnp.float32,
        )

    pot = pot_ref[...]
    out_pot[...] = product(pot, table_ref[...])
    radial = product(force_ref[...] * 0.1, table_ref[...])
    azimuth = product(pot * inverse_ref[...], slope_ref[...])
    for layer in range(density.shape[0]):
        here = density[layer, rows_here, :]
        out_r[layer] = mom_r[layer, rows_here, :] + here * radial
        out_phi[layer] = mom_phi[layer, rows_here, :] + here * azimuth


def add_gravity(pot, force, inverse_mid, tables, density, mom_r, mom_phi):
    layers, rows, cells = density.shape
    cols = pot.shape[0]
    block = min(rows, LANES)
    modes_spec = pl.BlockSpec((cols, block), lambda i: (0, i))
    table_spec = pl.BlockSpec((cols, cells), lambda i: (0, 0))

    field = pl.BlockSpec((layers, block, cells), lambda i: (0, i, 0))
    grid_shape = jax.ShapeDtypeStruct(density.shape, density.dtype)
    return pl.pallas_call(
        lambda *refs: gravity_kernel(rows // block, refs),
        grid=(rows // block,),
        in_specs=[
            modes_spec, modes_spec, pl.BlockSpec((1, block), lambda i: (0, i)),
        ] + [table_spec] * 4 + [pl.BlockSpec(memory_space=pl.ANY)] * 3,
        out_specs=[field, field, pl.BlockSpec((block, cells), lambda i: (i, 0))],
        out_shape=[grid_shape, grid_shape, jax.ShapeDtypeStruct((rows, cells), jnp.float32)],
        scratch_shapes=[pltpu.VMEM((3 * cols, cells), jnp.bfloat16)] * 2
        + [pltpu.VMEM(density.shape, density.dtype)] * 3
        + [pltpu.SemaphoreType.DMA((3, rows // block))],
        compiler_params=pltpu.CompilerParams(vmem_limit_bytes=VMEM_BYTES),
        cost_estimate=pl.CostEstimate(
            flops=18 * rows * cells * cols, bytes_accessed=44 * rows * cells, transcendentals=0
        ),
        name="add_gravity",
    )(
        pot, force, inverse_mid, *tables,
        density, mom_r, mom_phi,
    )


def exchange_rims(fields, rad_index, rad_count):
    first = jnp.stack([f[:, 0] for f in fields], axis=1)
    last = jnp.stack([f[:, -1] for f in fields], axis=1)
    if rad_count == 1:
        return first, last
    first_out, last_out = first.astype(jnp.bfloat16), last.astype(jnp.bfloat16)
    if rad_count == 2:
        other = lax.ppermute(
            jnp.where(rad_index == 0, last_out, first_out), "rad", [(0, 1), (1, 0)]
        )
        low = high = other
    else:
        up = [(i, i + 1) for i in range(rad_count - 1)]
        low = lax.ppermute(last_out, "rad", up)
        high = lax.ppermute(first_out, "rad", [(b, a) for a, b in up])
    rim_in = jnp.where(rad_index == 0, first, low.astype(first.dtype))
    rim_out = jnp.where(rad_index == rad_count - 1, last, high.astype(last.dtype))
    return rim_in, rim_out


def exchange_edges(first, last, az_count):
    right = [(i, (i + 1) % az_count) for i in range(az_count)]
    left = [(b, a) for a, b in right]
    return lax.ppermute(last, "az", right), lax.ppermute(first, "az", left)


def local(az_count, rad_count, density, mom_r, mom_phi, potential_kernel, force_kernel):
    layers, rows, cells = density.shape
    mode_count = potential_kernel.shape[0]
    pair_count = 2 * mode_count
    cols = az_count * pair_count
    step = 2.0 * math.pi / (az_count * cells)
    az_index = lax.axis_index("az")
    rad_index = lax.axis_index("rad")
    fields = (density, mom_r, mom_phi)

    azimuth = ((az_index * cells + jnp.arange(cells)).astype(jnp.float32) + 0.5) * step
    row = lax.broadcasted_iota(jnp.int32, (cols, cells), 0)
    mode = (row // 2).astype(jnp.float32)
    angle = azimuth[None, :] * mode
    cosine, sine = jnp.cos(angle), jnp.sin(angle)
    basis = pieces_of(jnp.where(row % 2 == 0, cosine, sine), 3)
    slope = pieces_of(jnp.where(row % 2 == 0, -mode * sine, mode * cosine), 2)

    rims = exchange_rims(fields, rad_index, rad_count)
    coefs, inverse_mid = row_coefficients(rad_index * rows, rows, step)

    partial, first, last = surface_modes(fields, basis, 1.0 / (az_count * cells))
    edges = exchange_edges(first, last, az_count)
    pieces = lax.all_to_all(
        partial.reshape(az_count, pair_count, rows), "az", split_axis=0, concat_axis=0, tiled=True
    )
    results = flux_layer(0, joint_flux, fields, rims, edges, coefs, None)
    pieces, results = lax.optimization_barrier((pieces, results))

    own = jnp.sum(pieces, axis=0).astype(jnp.bfloat16)
    pairs = lax.all_gather(own, "rad", axis=1, tiled=True)
    parts = responses(pairs, potential_kernel, force_kernel, az_count)
    every = lax.all_to_all(parts, "az", split_axis=0, concat_axis=0, tiled=True)
    coefs, parts = lax.optimization_barrier((coefs, parts))
    for layer in range(1, layers):
        results = flux_layer(layer, split_flux, fields, rims, edges, coefs, results)
    pot = every[:, 0].reshape(cols, rows)
    force = every[:, 1].reshape(cols, rows)

    new_r, new_phi, potential = add_gravity(
        pot,
        force,
        inverse_mid,
        (basis[0], basis[1], *slope),
        density,
        results[1],
        results[2],
    )
    return results[0], new_r, new_phi, potential


def solution(mesh):
    az_count, rad_count = mesh.shape["az"], mesh.shape["rad"]
    field = P(None, "rad", "az")
    kernel = P("az", "rad", None)
    return jax.shard_map(
        lambda *args: local(az_count, rad_count, *args),
        mesh=mesh,
        in_specs=(field, field, field, kernel, kernel),
        out_specs=(field, field, field, P("rad", "az")),
        check_vma=False,
    )
```

```python
import math

import jax
import jax.numpy as jnp
from jax import lax
from jax.experimental import pallas as pl
from jax.experimental.pallas import tpu as pltpu
from jax.sharding import PartitionSpec as P

aspect_sq = 0.0025
LANES = 128
SUB = 8
VMEM_BYTES = 60 << 20


def fetch_rows(refs, buffers, sems, steps):
    block = refs[0].shape[1] // steps

    def copy(k, place):
        if isinstance(place, int):
            rows = pl.ds(place * block, block)
        else:
            rows = pl.ds(pl.multiple_of(place * block, block), block)
        return pltpu.make_async_copy(refs[k].at[:, rows], buffers[k].at[:, rows], sems.at[k, place])

    @pl.when(pl.program_id(0) == 0)
    def _():
        for place in range(steps):
            for k in range(len(refs)):
                copy(k, place).start()

    for k in range(len(refs)):
        copy(k, pl.program_id(0)).wait()
    return pl.ds(pl.multiple_of(pl.program_id(0) * block, block), block)


def split_bf16(x):
    high = x.astype(jnp.bfloat16)
    low = (x - high.astype(jnp.float32)).astype(jnp.bfloat16)
    return high, low


def pieces_of(x, count):
    out = []
    for _ in range(count - 1):
        high = lax.reduce_precision(x, 8, 7)
        out.append(high.astype(jnp.bfloat16))
        x = x - high
    return out + [x.astype(jnp.bfloat16)]


EDGE_ROWS = 16


def modes_kernel(scale, steps, refs):
    firsts, lasts = refs[1:3], refs[3:5]
    *tables, out_ref, first_ref, last_ref, wide_ref, density, sems = refs[5:]
    thin_ref = tables[2]
    layers, _, cells = density.shape
    rows_here = fetch_rows(refs[:1], [density], sems, steps)
    cols = thin_ref.shape[0]

    @pl.when(pl.program_id(0) == 0)
    def _():
        wide_ref[:cols] = tables[0][...]
        wide_ref[cols:] = tables[1][...]

    x = density[0, rows_here, :]
    for layer in range(1, layers):
        x = x + density[layer, rows_here, :]
    high = x.astype(jnp.bfloat16)
    x = x - high.astype(jnp.float32)
    mid = x.astype(jnp.bfloat16)
    low = (x - mid.astype(jnp.float32)).astype(jnp.bfloat16)

    def product(a, table):
        return lax.dot_general(
            a, table, (((1,), (1,)), ((), ())), preferred_element_type=jnp.float32
        )

    rows = high.shape[0]
    major = product(jnp.concatenate([high, mid, low], axis=0), wide_ref[...])
    small = major[2 * rows :, :cols] + product(high, thin_ref[...])
    total = major[:rows, :cols] + (
        major[:rows, cols:] + major[rows : 2 * rows, :cols] + (major[rows : 2 * rows, cols:] + small)
    )
    out_ref[...] = (scale * total).T

    block = out_ref.shape[1]
    lane = lax.broadcasted_iota(jnp.int32, (block, LANES), 1)
    edges = jnp.zeros((block, LANES), jnp.float32)
    for layer in range(layers):
        sides = (
            (0, 0, (density[layer, rows_here, :LANES], firsts[0][layer], firsts[1][layer])),
            (
                EDGE_ROWS,
                LANES - 1,
                (density[layer, rows_here, cells - LANES :], lasts[0][layer], lasts[1][layer]),
            ),
        )
        for base, place, tiles in sides:
            for comp, tile in enumerate(tiles):
                edges = jnp.where(
                    lane == base + 3 * layer + comp,
                    jnp.broadcast_to(tile[:, place : place + 1], (block, LANES)),
                    edges,
                )
    edges = edges.T
    first_ref[...] = edges[:EDGE_ROWS].astype(jnp.bfloat16)
    last_ref[...] = edges[EDGE_ROWS : 2 * EDGE_ROWS].astype(jnp.bfloat16)


def surface_modes(fields, tables, scale):
    layers, rows, cells = fields[0].shape
    cols = tables[0].shape[0]
    block = min(rows, 2 * LANES)
    first = pl.BlockSpec((layers, block, LANES), lambda i: (0, i, 0))
    last = pl.BlockSpec((layers, block, LANES), lambda i: (0, i, cells // LANES - 1))
    table_spec = pl.BlockSpec((cols, cells), lambda i: (0, 0))
    edge_spec = pl.BlockSpec((EDGE_ROWS, block), lambda i: (0, i))
    edge_shape = jax.ShapeDtypeStruct((EDGE_ROWS, rows), jnp.bfloat16)
    return pl.pallas_call(
        lambda *refs: modes_kernel(scale, rows // block, refs),
        grid=(rows // block,),
        in_specs=[pl.BlockSpec(memory_space=pl.ANY)]
        + [first, first, last, last] + [table_spec] * 3,
        out_specs=[pl.BlockSpec((cols, block), lambda i: (0, i)), edge_spec, edge_spec],
        out_shape=[jax.ShapeDtypeStruct((cols, rows), jnp.float32), edge_shape, edge_shape],
        scratch_shapes=[
            pltpu.VMEM((2 * cols, cells), jnp.bfloat16),
            pltpu.VMEM(fields[0].shape, jnp.float32),
            pltpu.SemaphoreType.DMA((1, rows // block)),
        ],
        compiler_params=pltpu.CompilerParams(vmem_limit_bytes=VMEM_BYTES),
        cost_estimate=pl.CostEstimate(
            flops=12 * rows * cells * cols, bytes_accessed=4 * fields[0].size, transcendentals=0
        ),
        name="surface_modes",
    )(*fields, fields[1], fields[2], *tables)


def response_kernel(steps, refs):
    pairs_ref, pot_ref, force_ref, out_ref, pot_buffer, force_buffer, sems = refs
    pairs = pairs_ref[...]
    buffers = (pot_buffer, force_buffer)
    rows_here = fetch_rows((pot_ref, force_ref), buffers, sems, steps)
    block, cols = out_ref.shape[3], pairs.shape[0]
    mode_of = lax.broadcasted_iota(jnp.int32, (block, cols), 1) // 2
    for place, buffer in enumerate(buffers):
        total = jnp.zeros(mode_of.shape, jnp.float32)
        for mode in range(buffer.shape[0]):
            part = lax.dot_general(
                buffer[mode, rows_here, :],
                pairs,
                (((1,), (1,)), ((), ())),
                preferred_element_type=jnp.float32,
            )
            total = jnp.where(mode_of == mode, part, total)
        out_ref[:, place] = jnp.broadcast_to(total.T[None], (out_ref.shape[0], cols, block))


def responses(pairs, potential_kernel, force_kernel, copies):
    mode_count, rows, count = potential_kernel.shape
    cols = pairs.shape[0]
    block = min(rows, LANES)
    steps = rows // block
    whole = pl.BlockSpec(memory_space=pl.ANY)
    return pl.pallas_call(
        lambda *refs: response_kernel(steps, refs),
        grid=(steps,),
        in_specs=[pl.BlockSpec((cols, count), lambda i: (0, 0)), whole, whole],
        out_specs=pl.BlockSpec((copies, 2, cols, block), lambda i: (0, 0, 0, i)),
        out_shape=jax.ShapeDtypeStruct((copies, 2, cols, rows), jnp.float32),
        scratch_shapes=[
            pltpu.VMEM(potential_kernel.shape, potential_kernel.dtype),
            pltpu.VMEM(force_kernel.shape, force_kernel.dtype),
            pltpu.SemaphoreType.DMA((2, steps)),
        ],
        compiler_params=pltpu.CompilerParams(vmem_limit_bytes=VMEM_BYTES),
        cost_estimate=pl.CostEstimate(
            flops=4 * rows * count * cols * mode_count,
            bytes_accessed=4 * potential_kernel.size,
            transcendentals=0,
        ),
        name="responses",
    )(pairs, potential_kernel, force_kernel)


ROOT_FACE, SOUND_FACE, IN, OUT, ROOT_MID, SOUND_MID, AZ, SPIN, PULL = range(9)
COEFS = 16


def row_coefficients(first_row, rows, step):
    face = jnp.exp((first_row + jnp.arange(rows + LANES + 1)).astype(jnp.float32) * step)
    inner, outer = face[:-1], face[1:]
    mid = 0.5 * (inner + outer)
    area = 0.5 * (outer * outer - inner * inner)
    sound_face = aspect_sq / inner
    sound_mid = aspect_sq / mid
    radial = (0.05 * step) / area
    columns = [
        jnp.sqrt(sound_face),
        sound_face,
        radial * inner,
        radial * outer,
        jnp.sqrt(sound_mid),
        sound_mid,
        0.05 / mid,
        (0.1 * step) / mid,
        (0.1 * step) / (mid * mid),
    ]
    columns += [jnp.zeros_like(mid)] * (COEFS - len(columns))
    return jnp.stack(columns, axis=0), (-0.1 / mid)[None, :rows]


def inverse(x):
    guess = pl.reciprocal(x, approx=True)
    return guess * (2.0 - x * guess)


class FluxBlock:
    def __init__(self, block_count, refs):
        self.fields = refs[0:3]
        self.before = refs[3:6]
        self.after = refs[6:9]
        self.rim_in, self.rim_out, coef_rows, low_rows, high_rows, coef_after = refs[9:15]
        self.block_count = block_count
        self.rows, cells = self.fields[0].shape
        self.columns = cells // LANES
        self.strips = self.rows // SUB
        self.index = pl.program_id(0)
        self.lane = lax.broadcasted_iota(jnp.int32, (SUB, LANES), 1)
        self.sub = lax.broadcasted_iota(jnp.int32, (SUB, LANES), 0)
        side_rows = jnp.concatenate(
            [coef_rows[...], low_rows[...].astype(jnp.float32), high_rows[...].astype(jnp.float32)], axis=0
        )
        filler = jnp.zeros((LANES - side_rows.shape[0], self.rows), jnp.float32)
        self.side = jnp.concatenate([side_rows, filler], axis=0).T
        self.coef_after = coef_after

    def wide(self, column):
        return jnp.broadcast_to(column, (SUB, LANES))

    def at(self, col):
        return pl.ds(col * LANES, LANES)

    def rows_at(self, place):
        return pl.ds(pl.multiple_of(place * SUB, SUB), SUB)

    def radial_state(self, state):
        density, mom_r, mom_phi = state
        inv = inverse(density)
        vel = mom_r * inv
        return inv, (density, mom_r, mom_phi, jnp.abs(vel), mom_r * vel, mom_phi * vel)

    def radial_flux(self, upper, lower, root, sound):
        speed = jnp.maximum(upper[3], lower[3]) + root
        return (
            (upper[1] + lower[1]) - speed * (upper[0] - lower[0]),
            ((upper[4] + lower[4]) + sound * (upper[0] + lower[0]))
            - speed * (upper[1] - lower[1]),
            (upper[5] + lower[5]) - speed * (upper[2] - lower[2]),
        )

    def azimuth_flux(self, upper, lower, root):
        speed = jnp.maximum(upper[3], lower[3]) + root
        return (
            (upper[2] + lower[2]) - speed * (upper[0] - lower[0]),
            (upper[4] + lower[4]) - speed * (upper[1] - lower[1]),
            (upper[5] + lower[5]) - speed * (upper[2] - lower[2]),
        )

    def azimuth_values(self, state, inv, cross, sound):
        density, mom_r, mom_phi = state
        vel = mom_phi * inv
        return density, mom_r, mom_phi, jnp.abs(vel), cross, mom_phi * vel + sound * density

    def ghost_values(self, layer, coef, side, sound):
        base = COEFS + side * EDGE_ROWS + 3 * layer
        state = [self.wide(coef[:, base + c : base + c + 1]) for c in range(3)]
        inv = inverse(state[0])
        return self.azimuth_values(state, inv, state[1] * state[2] * inv, sound)

    def row_before(self, col):
        return self.edge_row(col, self.index == 0, self.rim_in, self.before, SUB - 1)

    def row_after(self, col):
        return self.edge_row(col, self.index == self.block_count - 1, self.rim_out, self.after, 0)

    def edge_row(self, col, edge, rim, near, row):
        state = []
        for comp in range(3):
            value = jnp.where(
                edge, rim[comp : comp + 1, self.at(col)], near[comp][row : row + 1, self.at(col)]
            )
            state.append(jnp.broadcast_to(value, (SUB, LANES)))
        return self.radial_state(state)[1]

    def columns_of(self, coef, names):
        return [self.wide(coef[:, k : k + 1]) for k in names]


def joint_flux(group, layer, block_count, refs):
    block = FluxBlock(block_count, refs)
    outs = refs[-6:-3]
    above, lagged, side = refs[-3:]
    side[...] = block.side
    lane, sub, at, fields = block.lane, block.sub, block.at, block.fields
    columns = block.columns

    def keep_above(col, rolled):
        for slot, value in enumerate(rolled):
            above[slot, :, at(col)] = value

    def finish(rows_before, col, turned, out_coef):
        for comp in range(3):
            up = jnp.where(sub == SUB - 1, turned[comp], lagged[comp, :, at(col)])
            outs[comp][rows_before, at(col)] -= out_coef * up

    for col in range(columns):
        keep_above(col, block.row_before(col))

    def strip(place, carry):
        here = block.rows_at(place)
        rows_before = block.rows_at(jnp.maximum(place - 1, 0))
        coef = side[here, :]
        root_face, sound_face, in_coef, root_mid, sound_mid, az, spin, pull = block.columns_of(
            coef, (ROOT_FACE, SOUND_FACE, IN, ROOT_MID, SOUND_MID, AZ, SPIN, PULL)
        )
        (out_before,) = block.columns_of(side[rows_before, :], (OUT,))
        zero = jnp.zeros((SUB, LANES), jnp.float32)

        def settle(col, held, turned_held, turned_flux):
            for comp in range(3):
                up = jnp.where(lane == LANES - 1, turned_flux[comp], turned_held[comp])
                outs[comp][here, col] = held[comp] - az * up

        def some_columns(place, carry):
            turned, held, turned_held = carry
            for k in range(group):
                first = place * (group * LANES) + k * LANES
                col = pl.ds(pl.multiple_of(first, LANES), LANES)
                before = pl.ds(pl.multiple_of(jnp.maximum(first - LANES, 0), LANES), LANES)
                state = [ref[here, col] for ref in fields]
                inv, values = block.radial_state(state)
                rolled = [pltpu.roll(value, 1, 0) for value in values]
                lower = [
                    jnp.where(sub == 0, above[slot, :, col], value) for slot, value in enumerate(rolled)
                ]
                flux_r = block.radial_flux(values, lower, root_face, sound_face)
                turned_r = [pltpu.roll(value, SUB - 1, 0) for value in flux_r]
                for comp in range(3):
                    up = jnp.where(sub == SUB - 1, turned_r[comp], lagged[comp, :, col])
                    outs[comp][rows_before, col] -= out_before * up
                for slot, value in enumerate(rolled):
                    above[slot, :, col] = value
                for comp in range(3):
                    lagged[comp, :, col] = turned_r[comp]
                values = block.azimuth_values(state, inv, values[5], sound_mid)
                rolled = [pltpu.roll(value, 1, 1) for value in values]
                lower = [jnp.where(lane == 0, a, b) for a, b in zip(turned, rolled)]
                turned = rolled
                flux = block.azimuth_flux(values, lower, root_mid)
                turned_flux = [pltpu.roll(value, LANES - 1, 1) for value in flux]
                settle(before, held, turned_held, turned_flux)
                held = (
                    state[0] + in_coef * flux_r[0] + az * flux[0],
                    state[1] + in_coef * flux_r[1] + az * flux[1] + (spin * values[5] - pull * state[0]),
                    state[2] + in_coef * flux_r[2] + az * flux[2] - spin * values[4],
                )
                turned_held = turned_flux
            return tuple(turned), held, tuple(turned_held)

        turned, held, turned_held = lax.fori_loop(
            0,
            columns // group,
            some_columns,
            (block.ghost_values(layer, coef, 0, sound_mid), (zero,) * 3, (zero,) * 3),
        )
        flux = block.azimuth_flux(block.ghost_values(layer, coef, 1, sound_mid), turned, root_mid)
        settle(
            at(columns - 1), held, turned_held, [pltpu.roll(value, LANES - 1, 1) for value in flux]
        )
        return carry

    lax.fori_loop(0, block.strips, strip, 0)

    last = pl.ds((block.strips - 1) * SUB, SUB)
    after = block.coef_after[...].T
    root_face, sound_face = block.columns_of(after[:SUB], (ROOT_FACE, SOUND_FACE))
    (out_coef,) = block.columns_of(side[last, :], (OUT,))
    for col in range(columns):
        lower = [above[slot, :, at(col)] for slot in range(6)]
        flux_r = block.radial_flux(block.row_after(col), lower, root_face, sound_face)
        finish(last, col, [pltpu.roll(value, SUB - 1, 0) for value in flux_r], out_coef)


def flux_layer(layer, group, fields, rims, edges, coefs, so_far):
    layers, rows, cells = fields[0].shape
    block = min(rows, LANES)
    count = rows // block
    per = block // SUB
    main = pl.BlockSpec((None, block, cells), lambda i: (layer, i, 0))
    before = pl.BlockSpec((None, SUB, cells), lambda i: (layer, jnp.maximum(i * per - 1, 0), 0))
    after = pl.BlockSpec(
        (None, SUB, cells), lambda i: (layer, jnp.minimum((i + 1) * per, rows // SUB - 1), 0)
    )
    rim = pl.BlockSpec((None, 3, cells), lambda i: (layer, 0, 0))
    operands = [*fields, *fields, *fields, *rims, coefs, *edges, coefs]
    specs = [main] * 3 + [before] * 3 + [after] * 3 + [
        rim,
        rim,
        pl.BlockSpec((COEFS, block), lambda i: (0, i)),
        pl.BlockSpec((EDGE_ROWS, block), lambda i: (0, i)),
        pl.BlockSpec((EDGE_ROWS, block), lambda i: (0, i)),
        pl.BlockSpec((COEFS, LANES), lambda i: (0, (i + 1) * (block // LANES))),
    ]
    aliases = {}
    if so_far is not None:
        for k, array in enumerate(so_far):
            aliases[len(operands)] = k
            operands.append(array)
            specs.append(pl.BlockSpec(memory_space=pl.ANY))
    scratch = [
        pltpu.VMEM((6, SUB, cells), jnp.float32),
        pltpu.VMEM((3, SUB, cells), jnp.float32),
        pltpu.VMEM((block, LANES), jnp.float32),
    ]
    group = min(group, cells // LANES)
    return pl.pallas_call(
        lambda *refs: joint_flux(group, layer, count, refs),
        grid=(count,),
        in_specs=specs,
        out_specs=[main] * 3,
        out_shape=[jax.ShapeDtypeStruct(f.shape, f.dtype) for f in fields],
        scratch_shapes=scratch,
        input_output_aliases=aliases,
        compiler_params=pltpu.CompilerParams(vmem_limit_bytes=VMEM_BYTES),
        cost_estimate=pl.CostEstimate(
            flops=100 * rows * cells, bytes_accessed=24 * rows * cells, transcendentals=rows * cells
        ),
        name="joint_flux",
    )(*operands)


def gravity_kernel(steps, refs):
    pot_ref, force_ref, inverse_ref = refs[:3]
    halves = refs[3:5]
    out_r, out_phi, out_pot, table_ref, *buffers, sems = refs[8:]
    density, mom_r, mom_phi = buffers
    rows_here = fetch_rows(refs[5:8], buffers, sems, steps)
    cols, block = pot_ref.shape

    @pl.when(pl.program_id(0) == 0)
    def _():
        table_ref[:cols] = halves[0][...]
        table_ref[cols : 2 * cols] = halves[0][...]
        table_ref[2 * cols :] = halves[1][...]

    pot = pot_ref[...]
    row = lax.broadcasted_iota(jnp.int32, pot.shape, 0)
    even = row % 2 == 0
    mode = (row // 2).astype(jnp.float32)
    swapped = jnp.where(even, pltpu.roll(pot, cols - 1, 0), -pltpu.roll(pot, 1, 0))
    left = jnp.concatenate(
        [pot, 0.1 * force_ref[...], swapped * (mode * inverse_ref[...])], axis=1
    )
    high, low = split_bf16(left)
    grid = lax.dot_general(
        jnp.concatenate([high, low, high], axis=0),
        table_ref[...],
        (((0,), (0,)), ((), ())),
        preferred_element_type=jnp.float32,
    )
    out_pot[...] = grid[:block]
    for layer in range(density.shape[0]):
        here = density[layer, rows_here, :]
        out_r[layer] = mom_r[layer, rows_here, :] + here * grid[block : 2 * block]
        out_phi[layer] = mom_phi[layer, rows_here, :] + here * grid[2 * block :]


def add_gravity(pot, force, inverse_mid, tables, density, mom_r, mom_phi):
    layers, rows, cells = density.shape
    cols = pot.shape[0]
    block = min(rows, 2 * LANES)
    modes_spec = pl.BlockSpec((cols, block), lambda i: (0, i))
    table_spec = pl.BlockSpec((cols, cells), lambda i: (0, 0))

    field = pl.BlockSpec((layers, block, cells), lambda i: (0, i, 0))
    grid_shape = jax.ShapeDtypeStruct(density.shape, density.dtype)
    return pl.pallas_call(
        lambda *refs: gravity_kernel(rows // block, refs),
        grid=(rows // block,),
        in_specs=[
            modes_spec, modes_spec, pl.BlockSpec((1, block), lambda i: (0, i)),
        ] + [table_spec] * 2 + [pl.BlockSpec(memory_space=pl.ANY)] * 3,
        out_specs=[field, field, pl.BlockSpec((block, cells), lambda i: (i, 0))],
        out_shape=[grid_shape, grid_shape, jax.ShapeDtypeStruct((rows, cells), jnp.float32)],
        scratch_shapes=[pltpu.VMEM((3 * cols, cells), jnp.bfloat16)]
        + [pltpu.VMEM(density.shape, density.dtype)] * 3
        + [pltpu.SemaphoreType.DMA((3, rows // block))],
        compiler_params=pltpu.CompilerParams(vmem_limit_bytes=VMEM_BYTES),
        cost_estimate=pl.CostEstimate(
            flops=18 * rows * cells * cols, bytes_accessed=44 * rows * cells, transcendentals=0
        ),
        name="add_gravity",
    )(
        pot, force, inverse_mid, *tables,
        density, mom_r, mom_phi,
    )


def exchange_rims(fields, rad_index, rad_count):
    first = jnp.stack([f[:, 0] for f in fields], axis=1)
    last = jnp.stack([f[:, -1] for f in fields], axis=1)
    if rad_count == 1:
        return first, last
    first_out, last_out = first.astype(jnp.bfloat16), last.astype(jnp.bfloat16)
    if rad_count == 2:
        other = lax.ppermute(
            jnp.where(rad_index == 0, last_out, first_out), "rad", [(0, 1), (1, 0)]
        )
        low = high = other
    else:
        up = [(i, i + 1) for i in range(rad_count - 1)]
        low = lax.ppermute(last_out, "rad", up)
        high = lax.ppermute(first_out, "rad", [(b, a) for a, b in up])
    rim_in = jnp.where(rad_index == 0, first, low.astype(first.dtype))
    rim_out = jnp.where(rad_index == rad_count - 1, last, high.astype(last.dtype))
    return rim_in, rim_out


def exchange_edges(first, last, az_count):
    right = [(i, (i + 1) % az_count) for i in range(az_count)]
    left = [(b, a) for a, b in right]
    return lax.ppermute(last, "az", right), lax.ppermute(first, "az", left)


def local(az_count, rad_count, density, mom_r, mom_phi, potential_kernel, force_kernel):
    layers, rows, cells = density.shape
    mode_count = potential_kernel.shape[0]
    pair_count = 2 * mode_count
    cols = az_count * pair_count
    step = 2.0 * math.pi / (az_count * cells)
    az_index = lax.axis_index("az")
    rad_index = lax.axis_index("rad")
    fields = (density, mom_r, mom_phi)

    azimuth = ((az_index * cells + jnp.arange(cells)).astype(jnp.float32) + 0.5) * step
    row = lax.broadcasted_iota(jnp.int32, (cols, cells), 0)
    mode = (row // 2).astype(jnp.float32)
    angle = azimuth[None, :] * mode
    cosine, sine = jnp.cos(angle), jnp.sin(angle)
    basis = pieces_of(jnp.where(row % 2 == 0, cosine, sine), 3)

    rims = exchange_rims(fields, rad_index, rad_count)
    coefs, inverse_mid = row_coefficients(rad_index * rows, rows, step)

    partial, first, last = surface_modes(fields, basis, 1.0 / (az_count * cells))
    edges = exchange_edges(first, last, az_count)
    partial, edges, rims = lax.optimization_barrier((partial, edges, rims))
    pieces = lax.all_to_all(
        partial.reshape(az_count, pair_count, rows), "az", split_axis=0, concat_axis=0, tiled=True
    )
    results = flux_layer(0, 4, fields, rims, edges, coefs, None)
    pieces, results = lax.optimization_barrier((pieces, results))

    own = jnp.sum(pieces, axis=0).astype(jnp.bfloat16)
    pairs = lax.all_gather(own, "rad", axis=1, tiled=True)
    parts = responses(pairs, potential_kernel, force_kernel, az_count)
    every = lax.all_to_all(parts, "az", split_axis=0, concat_axis=0, tiled=True)
    coefs, parts = lax.optimization_barrier((coefs, parts))
    for layer in range(1, layers):
        results = flux_layer(layer, 2, fields, rims, edges, coefs, results)
    pot = every[:, 0].reshape(cols, rows)
    force = every[:, 1].reshape(cols, rows)

    new_r, new_phi, potential = add_gravity(
        pot,
        force,
        inverse_mid,
        basis[:2],
        density,
        results[1],
        results[2],
    )
    return results[0], new_r, new_phi, potential


def solution(mesh):
    az_count, rad_count = mesh.shape["az"], mesh.shape["rad"]
    field = P(None, "rad", "az")
    kernel = P("az", "rad", None)
    return jax.shard_map(
        lambda *args: local(az_count, rad_count, *args),
        mesh=mesh,
        in_specs=(field, field, field, kernel, kernel),
        out_specs=(field, field, field, P("rad", "az")),
        check_vma=False,
    )
```

```python
import math

import jax
import jax.numpy as jnp
from jax import lax
from jax.experimental import pallas as pl
from jax.experimental.pallas import tpu as pltpu
from jax.sharding import PartitionSpec as P

aspect_sq = 0.0025
LANES = 128
SUB = 8
VMEM_BYTES = 60 << 20


def fetch_rows(refs, buffers, sems, steps):
    block = refs[0].shape[1] // steps

    def copy(k, place):
        if isinstance(place, int):
            rows = pl.ds(place * block, block)
        else:
            rows = pl.ds(pl.multiple_of(place * block, block), block)
        return pltpu.make_async_copy(refs[k].at[:, rows], buffers[k].at[:, rows], sems.at[k, place])

    @pl.when(pl.program_id(0) == 0)
    def _():
        for place in range(steps):
            for k in range(len(refs)):
                copy(k, place).start()

    for k in range(len(refs)):
        copy(k, pl.program_id(0)).wait()
    return pl.ds(pl.multiple_of(pl.program_id(0) * block, block), block)


def split_bf16(x):
    high = x.astype(jnp.bfloat16)
    low = (x - high.astype(jnp.float32)).astype(jnp.bfloat16)
    return high, low


def pieces_of(x, count):
    out = []
    for _ in range(count - 1):
        high = lax.reduce_precision(x, 8, 7)
        out.append(high.astype(jnp.bfloat16))
        x = x - high
    return out + [x.astype(jnp.bfloat16)]


EDGE_ROWS = 16


def modes_kernel(scale, steps, refs):
    firsts, lasts = refs[1:3], refs[3:5]
    *tables, out_ref, first_ref, last_ref, wide_ref, density, sems = refs[5:]
    thin_ref = tables[2]
    layers, _, cells = density.shape
    rows_here = fetch_rows(refs[:1], [density], sems, steps)
    cols = thin_ref.shape[0]

    @pl.when(pl.program_id(0) == 0)
    def _():
        wide_ref[:cols] = tables[0][...]
        wide_ref[cols:] = tables[1][...]

    x = density[0, rows_here, :]
    for layer in range(1, layers):
        x = x + density[layer, rows_here, :]
    high = x.astype(jnp.bfloat16)
    x = x - high.astype(jnp.float32)
    mid = x.astype(jnp.bfloat16)
    low = (x - mid.astype(jnp.float32)).astype(jnp.bfloat16)

    def product(a, table):
        return lax.dot_general(
            a, table, (((1,), (1,)), ((), ())), preferred_element_type=jnp.float32
        )

    rows = high.shape[0]
    major = product(jnp.concatenate([high, mid, low], axis=0), wide_ref[...])
    small = major[2 * rows :, :cols] + product(high, thin_ref[...])
    total = major[:rows, :cols] + (
        major[:rows, cols:] + major[rows : 2 * rows, :cols] + (major[rows : 2 * rows, cols:] + small)
    )
    out_ref[...] = (scale * total).T

    block = out_ref.shape[1]
    lane = lax.broadcasted_iota(jnp.int32, (block, LANES), 1)
    edges = jnp.zeros((block, LANES), jnp.float32)
    for layer in range(layers):
        sides = (
            (0, 0, (density[layer, rows_here, :LANES], firsts[0][layer], firsts[1][layer])),
            (
                EDGE_ROWS,
                LANES - 1,
                (density[layer, rows_here, cells - LANES :], lasts[0][layer], lasts[1][layer]),
            ),
        )
        for base, place, tiles in sides:
            for comp, tile in enumerate(tiles):
                edges = jnp.where(
                    lane == base + 3 * layer + comp,
                    jnp.broadcast_to(tile[:, place : place + 1], (block, LANES)),
                    edges,
                )
    edges = edges.T
    first_ref[...] = edges[:EDGE_ROWS].astype(jnp.bfloat16)
    last_ref[...] = edges[EDGE_ROWS : 2 * EDGE_ROWS].astype(jnp.bfloat16)


def surface_modes(fields, tables, scale):
    layers, rows, cells = fields[0].shape
    cols = tables[0].shape[0]
    block = min(rows, 2 * LANES)
    first = pl.BlockSpec((layers, block, LANES), lambda i: (0, i, 0))
    last = pl.BlockSpec((layers, block, LANES), lambda i: (0, i, cells // LANES - 1))
    table_spec = pl.BlockSpec((cols, cells), lambda i: (0, 0))
    edge_spec = pl.BlockSpec((EDGE_ROWS, block), lambda i: (0, i))
    edge_shape = jax.ShapeDtypeStruct((EDGE_ROWS, rows), jnp.bfloat16)
    return pl.pallas_call(
        lambda *refs: modes_kernel(scale, rows // block, refs),
        grid=(rows // block,),
        in_specs=[pl.BlockSpec(memory_space=pl.ANY)]
        + [first, first, last, last] + [table_spec] * 3,
        out_specs=[pl.BlockSpec((cols, block), lambda i: (0, i)), edge_spec, edge_spec],
        out_shape=[jax.ShapeDtypeStruct((cols, rows), jnp.float32), edge_shape, edge_shape],
        scratch_shapes=[
            pltpu.VMEM((2 * cols, cells), jnp.bfloat16),
            pltpu.VMEM(fields[0].shape, jnp.float32),
            pltpu.SemaphoreType.DMA((1, rows // block)),
        ],
        compiler_params=pltpu.CompilerParams(vmem_limit_bytes=VMEM_BYTES),
        cost_estimate=pl.CostEstimate(
            flops=12 * rows * cells * cols, bytes_accessed=4 * fields[0].size, transcendentals=0
        ),
        name="surface_modes",
    )(*fields, fields[1], fields[2], *tables)


def response_kernel(steps, refs):
    pairs_ref, pot_ref, force_ref, out_ref, pot_buffer, force_buffer, sems = refs
    pairs = pairs_ref[...]
    buffers = (pot_buffer, force_buffer)
    rows_here = fetch_rows((pot_ref, force_ref), buffers, sems, steps)
    block, cols = out_ref.shape[3], pairs.shape[0]
    mode_of = lax.broadcasted_iota(jnp.int32, (block, cols), 1) // 2
    for place, buffer in enumerate(buffers):
        total = jnp.zeros(mode_of.shape, jnp.float32)
        for mode in range(buffer.shape[0]):
            part = lax.dot_general(
                buffer[mode, rows_here, :],
                pairs,
                (((1,), (1,)), ((), ())),
                preferred_element_type=jnp.float32,
            )
            total = jnp.where(mode_of == mode, part, total)
        out_ref[:, place] = jnp.broadcast_to(total.T[None], (out_ref.shape[0], cols, block))


def responses(pairs, potential_kernel, force_kernel, copies):
    mode_count, rows, count = potential_kernel.shape
    cols = pairs.shape[0]
    block = min(rows, LANES)
    steps = rows // block
    whole = pl.BlockSpec(memory_space=pl.ANY)
    return pl.pallas_call(
        lambda *refs: response_kernel(steps, refs),
        grid=(steps,),
        in_specs=[pl.BlockSpec((cols, count), lambda i: (0, 0)), whole, whole],
        out_specs=pl.BlockSpec((copies, 2, cols, block), lambda i: (0, 0, 0, i)),
        out_shape=jax.ShapeDtypeStruct((copies, 2, cols, rows), jnp.float32),
        scratch_shapes=[
            pltpu.VMEM(potential_kernel.shape, potential_kernel.dtype),
            pltpu.VMEM(force_kernel.shape, force_kernel.dtype),
            pltpu.SemaphoreType.DMA((2, steps)),
        ],
        compiler_params=pltpu.CompilerParams(vmem_limit_bytes=VMEM_BYTES),
        cost_estimate=pl.CostEstimate(
            flops=4 * rows * count * cols * mode_count,
            bytes_accessed=4 * potential_kernel.size,
            transcendentals=0,
        ),
        name="responses",
    )(pairs, potential_kernel, force_kernel)


ROOT_FACE, SOUND_FACE, IN, OUT, ROOT_MID, SOUND_MID, AZ, SPIN, PULL = range(9)
COEFS = 16


def row_coefficients(first_row, rows, step):
    face = jnp.exp((first_row + jnp.arange(rows + LANES + 1)).astype(jnp.float32) * step)
    inner, outer = face[:-1], face[1:]
    mid = 0.5 * (inner + outer)
    area = 0.5 * (outer * outer - inner * inner)
    sound_face = aspect_sq / inner
    sound_mid = aspect_sq / mid
    radial = (0.05 * step) / area
    columns = [
        jnp.sqrt(sound_face),
        sound_face,
        radial * inner,
        radial * outer,
        jnp.sqrt(sound_mid),
        sound_mid,
        0.05 / mid,
        (0.1 * step) / mid,
        (0.1 * step) / (mid * mid),
    ]
    columns += [jnp.zeros_like(mid)] * (COEFS - len(columns))
    return jnp.stack(columns, axis=0), (-0.1 / mid)[None, :rows]


def inverse(x):
    guess = pl.reciprocal(x, approx=True)
    return guess * (2.0 - x * guess)


class FluxBlock:
    def __init__(self, block_count, refs):
        self.fields = refs[0:3]
        self.before = refs[3:6]
        self.after = refs[6:9]
        self.rim_in, self.rim_out, coef_rows, low_rows, high_rows, coef_after = refs[9:15]
        self.block_count = block_count
        self.rows, cells = self.fields[0].shape
        self.columns = cells // LANES
        self.strips = self.rows // SUB
        self.index = pl.program_id(0)
        self.lane = lax.broadcasted_iota(jnp.int32, (SUB, LANES), 1)
        self.sub = lax.broadcasted_iota(jnp.int32, (SUB, LANES), 0)
        side_rows = jnp.concatenate(
            [coef_rows[...], low_rows[...].astype(jnp.float32), high_rows[...].astype(jnp.float32)], axis=0
        )
        filler = jnp.zeros((LANES - side_rows.shape[0], self.rows), jnp.float32)
        self.side = jnp.concatenate([side_rows, filler], axis=0).T
        self.coef_after = coef_after

    def wide(self, column):
        return jnp.broadcast_to(column, (SUB, LANES))

    def at(self, col):
        return pl.ds(col * LANES, LANES)

    def rows_at(self, place):
        return pl.ds(pl.multiple_of(place * SUB, SUB), SUB)

    def radial_state(self, state):
        density, mom_r, mom_phi = state
        inv = inverse(density)
        vel = mom_r * inv
        return inv, (density, mom_r, mom_phi, jnp.abs(vel), mom_r * vel, mom_phi * vel)

    def radial_flux(self, upper, lower, root, sound):
        speed = jnp.maximum(upper[3], lower[3]) + root
        return (
            (upper[1] + lower[1]) - speed * (upper[0] - lower[0]),
            ((upper[4] + lower[4]) + sound * (upper[0] + lower[0]))
            - speed * (upper[1] - lower[1]),
            (upper[5] + lower[5]) - speed * (upper[2] - lower[2]),
        )

    def azimuth_flux(self, upper, lower, root):
        speed = jnp.maximum(upper[3], lower[3]) + root
        return (
            (upper[2] + lower[2]) - speed * (upper[0] - lower[0]),
            (upper[4] + lower[4]) - speed * (upper[1] - lower[1]),
            (upper[5] + lower[5]) - speed * (upper[2] - lower[2]),
        )

    def azimuth_values(self, state, inv, cross, sound):
        density, mom_r, mom_phi = state
        vel = mom_phi * inv
        return density, mom_r, mom_phi, jnp.abs(vel), cross, mom_phi * vel + sound * density

    def ghost_values(self, layer, coef, side, sound):
        base = COEFS + side * EDGE_ROWS + 3 * layer
        state = [self.wide(coef[:, base + c : base + c + 1]) for c in range(3)]
        inv = inverse(state[0])
        return self.azimuth_values(state, inv, state[1] * state[2] * inv, sound)

    def row_before(self, col):
        return self.edge_row(col, self.index == 0, self.rim_in, self.before, SUB - 1)

    def row_after(self, col):
        return self.edge_row(col, self.index == self.block_count - 1, self.rim_out, self.after, 0)

    def edge_row(self, col, edge, rim, near, row):
        state = []
        for comp in range(3):
            value = jnp.where(
                edge, rim[comp : comp + 1, self.at(col)], near[comp][row : row + 1, self.at(col)]
            )
            state.append(jnp.broadcast_to(value, (SUB, LANES)))
        return self.radial_state(state)[1]

    def columns_of(self, coef, names):
        return [self.wide(coef[:, k : k + 1]) for k in names]


CELL_VALUES = 8


def flux_kernel(layer, block_count, refs):
    block = FluxBlock(block_count, refs)
    outs = refs[-8:-5]
    side, cell, faces, sides, held = refs[-5:]
    side[...] = block.side
    lane, sub, at, fields, rows_at = block.lane, block.sub, block.at, block.fields, block.rows_at
    columns, strips, rows = block.columns, block.strips, block.rows

    after = block.coef_after[...].T
    root_face, sound_face = block.columns_of(after[:SUB], (ROOT_FACE, SOUND_FACE))
    for col in range(columns):
        for slot, value in enumerate(block.row_before(col)):
            cell[slot, 0:SUB, at(col)] = value
        last = [
            jnp.broadcast_to(ref[rows - 1 : rows, at(col)], (SUB, LANES)) for ref in fields
        ]
        flux = block.radial_flux(
            block.row_after(col), block.radial_state(last)[1], root_face, sound_face
        )
        for comp in range(3):
            faces[comp, rows : rows + SUB, at(col)] = flux[comp]

    def update(place):
        here, above = rows_at(place), rows_at(place + 1)
        out_coef, az = block.columns_of(side[here, :], (OUT, AZ))
        for col in range(columns):
            for comp in range(3):
                face = jnp.where(sub == 0, faces[comp, above, at(col)], faces[comp, here, at(col)])
                edge = jnp.where(lane == 0, sides[comp, here, at(col + 1)], sides[comp, here, at(col)])
                outs[comp][here, at(col)] = held[comp, here, at(col)] - (
                    out_coef * pltpu.roll(face, SUB - 1, 0) + az * pltpu.roll(edge, LANES - 1, 1)
                )

    def face_fluxes(place):
        here, inside = rows_at(place), rows_at(place + 1)
        coef = side[here, :]
        root_face, sound_face, in_coef, root_mid, sound_mid, az, spin, pull = block.columns_of(
            coef, (ROOT_FACE, SOUND_FACE, IN, ROOT_MID, SOUND_MID, AZ, SPIN, PULL)
        )
        left = block.ghost_values(layer, coef, 0, sound_mid)
        for col in range(columns):
            now = [cell[slot, inside, at(col)] for slot in range(CELL_VALUES)]
            lower = [
                pltpu.roll(jnp.where(sub == SUB - 1, cell[slot, here, at(col)], now[slot]), 1, 0)
                for slot in range(6)
            ]
            flux_r = block.radial_flux(now[:6], lower, root_face, sound_face)
            values = (*now[:3], now[6], now[5], now[7])
            lower = [
                pltpu.roll(jnp.where(lane == LANES - 1, a, b), 1, 1) for a, b in zip(left, values)
            ]
            left = values
            flux = block.azimuth_flux(values, lower, root_mid)
            for comp in range(3):
                faces[comp, here, at(col)] = flux_r[comp]
                sides[comp, here, at(col)] = flux[comp]
            held[0, here, at(col)] = now[0] + (in_coef * flux_r[0] + az * flux[0])
            held[1, here, at(col)] = (now[1] + (in_coef * flux_r[1] + az * flux[1])) + (
                spin * now[7] - pull * now[0]
            )
            held[2, here, at(col)] = (now[2] + (in_coef * flux_r[2] + az * flux[2])) - spin * now[5]
        values = block.ghost_values(layer, coef, 1, sound_mid)
        lower = [pltpu.roll(a, 1, 1) for a in left]
        for comp, value in enumerate(block.azimuth_flux(values, lower, root_mid)):
            sides[comp, here, at(columns)] = value

    def cell_values(place):
        here, inside = rows_at(place), rows_at(place + 1)
        (sound_mid,) = block.columns_of(side[here, :], (SOUND_MID,))
        for col in range(columns):
            state = [ref[here, at(col)] for ref in fields]
            inv, values = block.radial_state(state)
            vel = state[2] * inv
            values = (*values, jnp.abs(vel), state[2] * vel + sound_mid * state[0])
            for slot, value in enumerate(values):
                cell[slot, inside, at(col)] = value

    def iteration(place, carry):
        def clamped(late):
            return jnp.clip(place - late, 0, strips - 1)

        update(clamped(3))
        face_fluxes(clamped(1))
        cell_values(clamped(0))
        return carry

    lax.fori_loop(0, strips + 3, iteration, 0)


def flux_layer(layer, fields, rims, edges, coefs, so_far):
    layers, rows, cells = fields[0].shape
    block = min(rows, 2 * LANES)
    count = rows // block
    per = block // SUB
    main = pl.BlockSpec((None, block, cells), lambda i: (layer, i, 0))
    before = pl.BlockSpec((None, SUB, cells), lambda i: (layer, jnp.maximum(i * per - 1, 0), 0))
    after = pl.BlockSpec(
        (None, SUB, cells), lambda i: (layer, jnp.minimum((i + 1) * per, rows // SUB - 1), 0)
    )
    rim = pl.BlockSpec((None, 3, cells), lambda i: (layer, 0, 0))
    operands = [*fields, *fields, *fields, *rims, coefs, *edges, coefs]
    specs = [main] * 3 + [before] * 3 + [after] * 3 + [
        rim,
        rim,
        pl.BlockSpec((COEFS, block), lambda i: (0, i)),
        pl.BlockSpec((EDGE_ROWS, block), lambda i: (0, i)),
        pl.BlockSpec((EDGE_ROWS, block), lambda i: (0, i)),
        pl.BlockSpec((COEFS, LANES), lambda i: (0, (i + 1) * (block // LANES))),
    ]
    aliases = {}
    if so_far is not None:
        for k, array in enumerate(so_far):
            aliases[len(operands)] = k
            operands.append(array)
            specs.append(pl.BlockSpec(memory_space=pl.ANY))
    scratch = [
        pltpu.VMEM((block, LANES), jnp.float32),
        pltpu.VMEM((CELL_VALUES, block + SUB, cells), jnp.float32),
        pltpu.VMEM((3, block + SUB, cells), jnp.float32),
        pltpu.VMEM((3, block, cells + LANES), jnp.float32),
        pltpu.VMEM((3, block, cells), jnp.float32),
    ]
    return pl.pallas_call(
        lambda *refs: flux_kernel(layer, count, refs),
        grid=(count,),
        in_specs=specs,
        out_specs=[main] * 3,
        out_shape=[jax.ShapeDtypeStruct(f.shape, f.dtype) for f in fields],
        scratch_shapes=scratch,
        input_output_aliases=aliases,
        compiler_params=pltpu.CompilerParams(vmem_limit_bytes=VMEM_BYTES),
        cost_estimate=pl.CostEstimate(
            flops=100 * rows * cells, bytes_accessed=24 * rows * cells, transcendentals=rows * cells
        ),
        name="flux_layer",
    )(*operands)


def gravity_kernel(steps, refs):
    pot_ref, force_ref, inverse_ref = refs[:3]
    halves = refs[3:5]
    out_r, out_phi, out_pot, table_ref, *buffers, sems = refs[8:]
    density, mom_r, mom_phi = buffers
    rows_here = fetch_rows(refs[5:8], buffers, sems, steps)
    cols, block = pot_ref.shape

    @pl.when(pl.program_id(0) == 0)
    def _():
        table_ref[:cols] = halves[0][...]
        table_ref[cols : 2 * cols] = halves[0][...]
        table_ref[2 * cols :] = halves[1][...]

    pot = pot_ref[...]
    row = lax.broadcasted_iota(jnp.int32, pot.shape, 0)
    even = row % 2 == 0
    mode = (row // 2).astype(jnp.float32)
    swapped = jnp.where(even, pltpu.roll(pot, cols - 1, 0), -pltpu.roll(pot, 1, 0))
    left = jnp.concatenate(
        [pot, 0.1 * force_ref[...], swapped * (mode * inverse_ref[...])], axis=1
    )
    high, low = split_bf16(left)
    grid = lax.dot_general(
        jnp.concatenate([high, low, high], axis=0),
        table_ref[...],
        (((0,), (0,)), ((), ())),
        preferred_element_type=jnp.float32,
    )
    out_pot[...] = grid[:block]
    for layer in range(density.shape[0]):
        here = density[layer, rows_here, :]
        out_r[layer] = mom_r[layer, rows_here, :] + here * grid[block : 2 * block]
        out_phi[layer] = mom_phi[layer, rows_here, :] + here * grid[2 * block :]


def add_gravity(pot, force, inverse_mid, tables, density, mom_r, mom_phi):
    layers, rows, cells = density.shape
    cols = pot.shape[0]
    block = min(rows, 2 * LANES)
    modes_spec = pl.BlockSpec((cols, block), lambda i: (0, i))
    table_spec = pl.BlockSpec((cols, cells), lambda i: (0, 0))

    field = pl.BlockSpec((layers, block, cells), lambda i: (0, i, 0))
    grid_shape = jax.ShapeDtypeStruct(density.shape, density.dtype)
    return pl.pallas_call(
        lambda *refs: gravity_kernel(rows // block, refs),
        grid=(rows // block,),
        in_specs=[
            modes_spec, modes_spec, pl.BlockSpec((1, block), lambda i: (0, i)),
        ] + [table_spec] * 2 + [pl.BlockSpec(memory_space=pl.ANY)] * 3,
        out_specs=[field, field, pl.BlockSpec((block, cells), lambda i: (i, 0))],
        out_shape=[grid_shape, grid_shape, jax.ShapeDtypeStruct((rows, cells), jnp.float32)],
        scratch_shapes=[pltpu.VMEM((3 * cols, cells), jnp.bfloat16)]
        + [pltpu.VMEM(density.shape, density.dtype)] * 3
        + [pltpu.SemaphoreType.DMA((3, rows // block))],
        compiler_params=pltpu.CompilerParams(vmem_limit_bytes=VMEM_BYTES),
        cost_estimate=pl.CostEstimate(
            flops=18 * rows * cells * cols, bytes_accessed=44 * rows * cells, transcendentals=0
        ),
        name="add_gravity",
    )(
        pot, force, inverse_mid, *tables,
        density, mom_r, mom_phi,
    )


def exchange_rims(fields, rad_index, rad_count):
    first = jnp.stack([f[:, 0] for f in fields], axis=1)
    last = jnp.stack([f[:, -1] for f in fields], axis=1)
    if rad_count == 1:
        return first, last
    first_out, last_out = first.astype(jnp.bfloat16), last.astype(jnp.bfloat16)
    if rad_count == 2:
        other = lax.ppermute(
            jnp.where(rad_index == 0, last_out, first_out), "rad", [(0, 1), (1, 0)]
        )
        low = high = other
    else:
        up = [(i, i + 1) for i in range(rad_count - 1)]
        low = lax.ppermute(last_out, "rad", up)
        high = lax.ppermute(first_out, "rad", [(b, a) for a, b in up])
    rim_in = jnp.where(rad_index == 0, first, low.astype(first.dtype))
    rim_out = jnp.where(rad_index == rad_count - 1, last, high.astype(last.dtype))
    return rim_in, rim_out


def exchange_edges(first, last, az_count):
    right = [(i, (i + 1) % az_count) for i in range(az_count)]
    left = [(b, a) for a, b in right]
    return lax.ppermute(last, "az", right), lax.ppermute(first, "az", left)


def local(az_count, rad_count, density, mom_r, mom_phi, potential_kernel, force_kernel):
    layers, rows, cells = density.shape
    mode_count = potential_kernel.shape[0]
    pair_count = 2 * mode_count
    cols = az_count * pair_count
    step = 2.0 * math.pi / (az_count * cells)
    az_index = lax.axis_index("az")
    rad_index = lax.axis_index("rad")
    fields = (density, mom_r, mom_phi)

    azimuth = ((az_index * cells + jnp.arange(cells)).astype(jnp.float32) + 0.5) * step
    row = lax.broadcasted_iota(jnp.int32, (cols, cells), 0)
    mode = (row // 2).astype(jnp.float32)
    angle = azimuth[None, :] * mode
    cosine, sine = jnp.cos(angle), jnp.sin(angle)
    basis = pieces_of(jnp.where(row % 2 == 0, cosine, sine), 3)

    rims = exchange_rims(fields, rad_index, rad_count)
    coefs, inverse_mid = row_coefficients(rad_index * rows, rows, step)

    partial, first, last = surface_modes(fields, basis, 1.0 / (az_count * cells))
    edges = exchange_edges(first, last, az_count)
    partial, edges, rims = lax.optimization_barrier((partial, edges, rims))
    pieces = lax.all_to_all(
        partial.reshape(az_count, pair_count, rows), "az", split_axis=0, concat_axis=0, tiled=True
    )
    results = flux_layer(0, fields, rims, edges, coefs, None)
    pieces, results = lax.optimization_barrier((pieces, results))

    own = jnp.sum(pieces, axis=0).astype(jnp.bfloat16)
    pairs = lax.all_gather(own, "rad", axis=1, tiled=True)
    parts = responses(pairs, potential_kernel, force_kernel, az_count)
    every = lax.all_to_all(parts, "az", split_axis=0, concat_axis=0, tiled=True)
    coefs, parts = lax.optimization_barrier((coefs, parts))
    for layer in range(1, layers):
        results = flux_layer(layer, fields, rims, edges, coefs, results)
    pot = every[:, 0].reshape(cols, rows)
    force = every[:, 1].reshape(cols, rows)

    new_r, new_phi, potential = add_gravity(
        pot,
        force,
        inverse_mid,
        basis[:2],
        density,
        results[1],
        results[2],
    )
    return results[0], new_r, new_phi, potential


def solution(mesh):
    az_count, rad_count = mesh.shape["az"], mesh.shape["rad"]
    field = P(None, "rad", "az")
    kernel = P("az", "rad", None)
    return jax.shard_map(
        lambda *args: local(az_count, rad_count, *args),
        mesh=mesh,
        in_specs=(field, field, field, kernel, kernel),
        out_specs=(field, field, field, P("rad", "az")),
        check_vma=False,
    )
```

```python
import math

import jax
import jax.numpy as jnp
from jax import lax
from jax.experimental import pallas as pl
from jax.experimental.pallas import tpu as pltpu
from jax.sharding import PartitionSpec as P

aspect_sq = 0.0025
LANES = 128
SUB = 8
VMEM_BYTES = 60 << 20


def fetch_rows(refs, buffers, sems, steps):
    block = refs[0].shape[1] // steps

    def copy(k, place):
        if isinstance(place, int):
            rows = pl.ds(place * block, block)
        else:
            rows = pl.ds(pl.multiple_of(place * block, block), block)
        return pltpu.make_async_copy(refs[k].at[:, rows], buffers[k].at[:, rows], sems.at[k, place])

    @pl.when(pl.program_id(0) == 0)
    def _():
        for place in range(steps):
            for k in range(len(refs)):
                copy(k, place).start()

    for k in range(len(refs)):
        copy(k, pl.program_id(0)).wait()
    return pl.ds(pl.multiple_of(pl.program_id(0) * block, block), block)


def split_bf16(x):
    high = x.astype(jnp.bfloat16)
    low = (x - high.astype(jnp.float32)).astype(jnp.bfloat16)
    return high, low


def pieces_of(x, count):
    out = []
    for _ in range(count - 1):
        high = lax.reduce_precision(x, 8, 7)
        out.append(high.astype(jnp.bfloat16))
        x = x - high
    return out + [x.astype(jnp.bfloat16)]


EDGE_ROWS = 16


def modes_kernel(scale, steps, refs):
    firsts, lasts = refs[1:3], refs[3:5]
    *tables, out_ref, first_ref, last_ref, wide_ref, density, sems = refs[5:]
    thin_ref = tables[2]
    layers, _, cells = density.shape
    rows_here = fetch_rows(refs[:1], [density], sems, steps)
    cols = thin_ref.shape[0]

    @pl.when(pl.program_id(0) == 0)
    def _():
        wide_ref[:cols] = tables[0][...]
        wide_ref[cols:] = tables[1][...]

    x = density[0, rows_here, :]
    for layer in range(1, layers):
        x = x + density[layer, rows_here, :]
    high = x.astype(jnp.bfloat16)
    x = x - high.astype(jnp.float32)
    mid = x.astype(jnp.bfloat16)
    low = (x - mid.astype(jnp.float32)).astype(jnp.bfloat16)

    def product(a, table):
        return lax.dot_general(
            a, table, (((1,), (1,)), ((), ())), preferred_element_type=jnp.float32
        )

    rows = high.shape[0]
    major = product(jnp.concatenate([high, mid, low], axis=0), wide_ref[...])
    small = major[2 * rows :, :cols] + product(high, thin_ref[...])
    total = major[:rows, :cols] + (
        major[:rows, cols:] + major[rows : 2 * rows, :cols] + (major[rows : 2 * rows, cols:] + small)
    )
    out_ref[...] = (scale * total).T

    block = out_ref.shape[1]
    lane = lax.broadcasted_iota(jnp.int32, (block, LANES), 1)
    edges = jnp.zeros((block, LANES), jnp.float32)
    for layer in range(layers):
        sides = (
            (0, 0, (density[layer, rows_here, :LANES], firsts[0][layer], firsts[1][layer])),
            (
                EDGE_ROWS,
                LANES - 1,
                (density[layer, rows_here, cells - LANES :], lasts[0][layer], lasts[1][layer]),
            ),
        )
        for base, place, tiles in sides:
            for comp, tile in enumerate(tiles):
                edges = jnp.where(
                    lane == base + 3 * layer + comp,
                    jnp.broadcast_to(tile[:, place : place + 1], (block, LANES)),
                    edges,
                )
    edges = edges.T
    first_ref[...] = edges[:EDGE_ROWS].astype(jnp.bfloat16)
    last_ref[...] = edges[EDGE_ROWS : 2 * EDGE_ROWS].astype(jnp.bfloat16)


def surface_modes(fields, tables, scale):
    layers, rows, cells = fields[0].shape
    cols = tables[0].shape[0]
    block = min(rows, 2 * LANES)
    first = pl.BlockSpec((layers, block, LANES), lambda i: (0, i, 0))
    last = pl.BlockSpec((layers, block, LANES), lambda i: (0, i, cells // LANES - 1))
    table_spec = pl.BlockSpec((cols, cells), lambda i: (0, 0))
    edge_spec = pl.BlockSpec((EDGE_ROWS, block), lambda i: (0, i))
    edge_shape = jax.ShapeDtypeStruct((EDGE_ROWS, rows), jnp.bfloat16)
    return pl.pallas_call(
        lambda *refs: modes_kernel(scale, rows // block, refs),
        grid=(rows // block,),
        in_specs=[pl.BlockSpec(memory_space=pl.ANY)]
        + [first, first, last, last] + [table_spec] * 3,
        out_specs=[pl.BlockSpec((cols, block), lambda i: (0, i)), edge_spec, edge_spec],
        out_shape=[jax.ShapeDtypeStruct((cols, rows), jnp.float32), edge_shape, edge_shape],
        scratch_shapes=[
            pltpu.VMEM((2 * cols, cells), jnp.bfloat16),
            pltpu.VMEM(fields[0].shape, jnp.float32),
            pltpu.SemaphoreType.DMA((1, rows // block)),
        ],
        compiler_params=pltpu.CompilerParams(vmem_limit_bytes=VMEM_BYTES),
        cost_estimate=pl.CostEstimate(
            flops=12 * rows * cells * cols, bytes_accessed=4 * fields[0].size, transcendentals=0
        ),
        name="surface_modes",
    )(*fields, fields[1], fields[2], *tables)


def response_kernel(steps, refs):
    pairs_ref, pot_ref, force_ref, out_ref, pot_buffer, force_buffer, sems = refs
    pairs = pairs_ref[...]
    buffers = (pot_buffer, force_buffer)
    rows_here = fetch_rows((pot_ref, force_ref), buffers, sems, steps)
    block, cols = out_ref.shape[3], pairs.shape[0]
    mode_of = lax.broadcasted_iota(jnp.int32, (block, cols), 1) // 2
    for place, buffer in enumerate(buffers):
        total = jnp.zeros(mode_of.shape, jnp.float32)
        for mode in range(buffer.shape[0]):
            part = lax.dot_general(
                buffer[mode, rows_here, :],
                pairs,
                (((1,), (1,)), ((), ())),
                preferred_element_type=jnp.float32,
            )
            total = jnp.where(mode_of == mode, part, total)
        out_ref[:, place] = jnp.broadcast_to(total.T[None], (out_ref.shape[0], cols, block))


def responses(pairs, potential_kernel, force_kernel, copies):
    mode_count, rows, count = potential_kernel.shape
    cols = pairs.shape[0]
    block = min(rows, LANES)
    steps = rows // block
    whole = pl.BlockSpec(memory_space=pl.ANY)
    return pl.pallas_call(
        lambda *refs: response_kernel(steps, refs),
        grid=(steps,),
        in_specs=[pl.BlockSpec((cols, count), lambda i: (0, 0)), whole, whole],
        out_specs=pl.BlockSpec((copies, 2, cols, block), lambda i: (0, 0, 0, i)),
        out_shape=jax.ShapeDtypeStruct((copies, 2, cols, rows), jnp.float32),
        scratch_shapes=[
            pltpu.VMEM(potential_kernel.shape, potential_kernel.dtype),
            pltpu.VMEM(force_kernel.shape, force_kernel.dtype),
            pltpu.SemaphoreType.DMA((2, steps)),
        ],
        compiler_params=pltpu.CompilerParams(vmem_limit_bytes=VMEM_BYTES),
        cost_estimate=pl.CostEstimate(
            flops=4 * rows * count * cols * mode_count,
            bytes_accessed=4 * potential_kernel.size,
            transcendentals=0,
        ),
        name="responses",
    )(pairs, potential_kernel, force_kernel)


ROOT_FACE, SOUND_FACE, IN, OUT, ROOT_MID, SOUND_MID, AZ, SPIN, PULL = range(9)
COEFS = 16


def row_coefficients(first_row, rows, step):
    face = jnp.exp((first_row + jnp.arange(rows + LANES + 1)).astype(jnp.float32) * step)
    inner, outer = face[:-1], face[1:]
    mid = 0.5 * (inner + outer)
    area = 0.5 * (outer * outer - inner * inner)
    sound_face = aspect_sq / inner
    sound_mid = aspect_sq / mid
    radial = (0.05 * step) / area
    columns = [
        jnp.sqrt(sound_face),
        sound_face,
        radial * inner,
        radial * outer,
        jnp.sqrt(sound_mid),
        sound_mid,
        0.05 / mid,
        (0.1 * step) / mid,
        (0.1 * step) / (mid * mid),
    ]
    columns += [jnp.zeros_like(mid)] * (COEFS - len(columns))
    return jnp.stack(columns, axis=0), (-0.1 / mid)[None, :rows]


def inverse(x):
    guess = pl.reciprocal(x, approx=True)
    return guess * (2.0 - x * guess)


class FluxBlock:
    def __init__(self, block_count, refs):
        self.fields = refs[0:3]
        self.before = refs[3:6]
        self.after = refs[6:9]
        self.rim_in, self.rim_out, coef_rows, low_rows, high_rows, coef_after = refs[9:15]
        self.block_count = block_count
        self.rows, cells = self.fields[0].shape
        self.columns = cells // LANES
        self.strips = self.rows // SUB
        self.index = pl.program_id(0)
        self.lane = lax.broadcasted_iota(jnp.int32, (SUB, LANES), 1)
        side_rows = jnp.concatenate(
            [coef_rows[...], low_rows[...].astype(jnp.float32), high_rows[...].astype(jnp.float32)], axis=0
        )
        filler = jnp.zeros((LANES - side_rows.shape[0], self.rows), jnp.float32)
        self.side = jnp.concatenate([side_rows, filler], axis=0).T
        self.coef_after = coef_after

    def wide(self, column):
        return jnp.broadcast_to(column, (SUB, LANES))

    def at(self, col):
        return pl.ds(col * LANES, LANES)

    def rows_at(self, place):
        return pl.ds(pl.multiple_of(place * SUB, SUB), SUB)

    def radial_state(self, state):
        density, mom_r, mom_phi = state
        inv = inverse(density)
        vel = mom_r * inv
        return inv, (density, mom_r, mom_phi, jnp.abs(vel), mom_r * vel, mom_phi * vel)

    def radial_flux(self, upper, lower, root, sound):
        speed = jnp.maximum(upper[3], lower[3]) + root
        return (
            (upper[1] + lower[1]) - speed * (upper[0] - lower[0]),
            ((upper[4] + lower[4]) + sound * (upper[0] + lower[0]))
            - speed * (upper[1] - lower[1]),
            (upper[5] + lower[5]) - speed * (upper[2] - lower[2]),
        )

    def azimuth_flux(self, upper, lower, root):
        speed = jnp.maximum(upper[3], lower[3]) + root
        return (
            (upper[2] + lower[2]) - speed * (upper[0] - lower[0]),
            (upper[4] + lower[4]) - speed * (upper[1] - lower[1]),
            (upper[5] + lower[5]) - speed * (upper[2] - lower[2]),
        )

    def azimuth_values(self, state, inv, cross, sound):
        density, mom_r, mom_phi = state
        vel = mom_phi * inv
        return density, mom_r, mom_phi, jnp.abs(vel), cross, mom_phi * vel + sound * density

    def ghost_values(self, layer, coef, side, sound):
        base = COEFS + side * EDGE_ROWS + 3 * layer
        state = [self.wide(coef[:, base + c : base + c + 1]) for c in range(3)]
        inv = inverse(state[0])
        return self.azimuth_values(state, inv, state[1] * state[2] * inv, sound)

    def row_before(self, col):
        return self.edge_row(col, self.index == 0, self.rim_in, self.before, SUB - 1)

    def row_after(self, col):
        return self.edge_row(col, self.index == self.block_count - 1, self.rim_out, self.after, 0)

    def edge_row(self, col, edge, rim, near, row):
        state = []
        for comp in range(3):
            value = jnp.where(
                edge, rim[comp : comp + 1, self.at(col)], near[comp][row : row + 1, self.at(col)]
            )
            state.append(jnp.broadcast_to(value, (SUB, LANES)))
        return self.radial_state(state)[1]

    def columns_of(self, coef, names):
        return [self.wide(coef[:, k : k + 1]) for k in names]


CELL_VALUES = 8


def flux_kernel(layer, block_count, refs):
    block = FluxBlock(block_count, refs)
    outs = refs[-8:-5]
    side, cell, faces, sides, held = refs[-5:]
    side[...] = block.side
    lane, at, fields, rows_at = block.lane, block.at, block.fields, block.rows_at
    columns, strips, rows = block.columns, block.strips, block.rows

    after = block.coef_after[...].T
    root_face, sound_face = block.columns_of(after[:SUB], (ROOT_FACE, SOUND_FACE))
    for col in range(columns):
        for slot, value in enumerate(block.row_before(col)):
            cell[slot, col, 0:SUB, :] = value
        last = [
            jnp.broadcast_to(ref[rows - 1 : rows, at(col)], (SUB, LANES)) for ref in fields
        ]
        flux = block.radial_flux(
            block.row_after(col), block.radial_state(last)[1], root_face, sound_face
        )
        for comp in range(3):
            faces[comp, col, rows : rows + SUB, :] = flux[comp]

    def shifted(place, by):
        return pl.ds(pl.multiple_of(place * SUB, SUB) + by, SUB)

    def update(place):
        here, above = rows_at(place), shifted(place, 1)
        out_coef, az = block.columns_of(side[here, :], (OUT, AZ))
        for col in range(columns):
            for comp in range(3):
                edge = jnp.where(lane == 0, sides[comp, here, at(col + 1)], sides[comp, here, at(col)])
                outs[comp][here, at(col)] = held[comp, here, at(col)] - (
                    out_coef * faces[comp, col, above, :] + az * pltpu.roll(edge, LANES - 1, 1)
                )

    def face_fluxes(place):
        here, inside, below = rows_at(place), rows_at(place + 1), shifted(place, SUB - 1)
        coef = side[here, :]
        root_face, sound_face, in_coef, root_mid, sound_mid, az, spin, pull = block.columns_of(
            coef, (ROOT_FACE, SOUND_FACE, IN, ROOT_MID, SOUND_MID, AZ, SPIN, PULL)
        )
        left = block.ghost_values(layer, coef, 0, sound_mid)
        for col in range(columns):
            now = [cell[slot, col, inside, :] for slot in range(CELL_VALUES)]
            lower = [cell[slot, col, below, :] for slot in range(6)]
            flux_r = block.radial_flux(now[:6], lower, root_face, sound_face)
            values = (*now[:3], now[6], now[5], now[7])
            lower = [
                pltpu.roll(jnp.where(lane == LANES - 1, a, b), 1, 1) for a, b in zip(left, values)
            ]
            left = values
            flux = block.azimuth_flux(values, lower, root_mid)
            for comp in range(3):
                faces[comp, col, here, :] = flux_r[comp]
                sides[comp, here, at(col)] = flux[comp]
            held[0, here, at(col)] = now[0] + (in_coef * flux_r[0] + az * flux[0])
            held[1, here, at(col)] = (now[1] + (in_coef * flux_r[1] + az * flux[1])) + (
                spin * now[7] - pull * now[0]
            )
            held[2, here, at(col)] = (now[2] + (in_coef * flux_r[2] + az * flux[2])) - spin * now[5]
        values = block.ghost_values(layer, coef, 1, sound_mid)
        lower = [pltpu.roll(a, 1, 1) for a in left]
        for comp, value in enumerate(block.azimuth_flux(values, lower, root_mid)):
            sides[comp, here, at(columns)] = value

    def cell_values(place):
        here, inside = rows_at(place), rows_at(place + 1)
        (sound_mid,) = block.columns_of(side[here, :], (SOUND_MID,))
        for col in range(columns):
            state = [ref[here, at(col)] for ref in fields]
            inv, values = block.radial_state(state)
            vel = state[2] * inv
            values = (*values, jnp.abs(vel), state[2] * vel + sound_mid * state[0])
            for slot, value in enumerate(values):
                cell[slot, col, inside, :] = value

    def iteration(place, carry):
        def clamped(late):
            return jnp.clip(place - late, 0, strips - 1)

        update(clamped(3))
        face_fluxes(clamped(1))
        cell_values(clamped(0))
        return carry

    lax.fori_loop(0, strips + 3, iteration, 0)


def flux_layer(layer, fields, rims, edges, coefs, so_far):
    layers, rows, cells = fields[0].shape
    block = min(rows, 2 * LANES)
    count = rows // block
    per = block // SUB
    main = pl.BlockSpec((None, block, cells), lambda i: (layer, i, 0))
    before = pl.BlockSpec((None, SUB, cells), lambda i: (layer, jnp.maximum(i * per - 1, 0), 0))
    after = pl.BlockSpec(
        (None, SUB, cells), lambda i: (layer, jnp.minimum((i + 1) * per, rows // SUB - 1), 0)
    )
    rim = pl.BlockSpec((None, 3, cells), lambda i: (layer, 0, 0))
    operands = [*fields, *fields, *fields, *rims, coefs, *edges, coefs]
    specs = [main] * 3 + [before] * 3 + [after] * 3 + [
        rim,
        rim,
        pl.BlockSpec((COEFS, block), lambda i: (0, i)),
        pl.BlockSpec((EDGE_ROWS, block), lambda i: (0, i)),
        pl.BlockSpec((EDGE_ROWS, block), lambda i: (0, i)),
        pl.BlockSpec((COEFS, LANES), lambda i: (0, (i + 1) * (block // LANES))),
    ]
    aliases = {}
    if so_far is not None:
        for k, array in enumerate(so_far):
            aliases[len(operands)] = k
            operands.append(array)
            specs.append(pl.BlockSpec(memory_space=pl.ANY))
    scratch = [
        pltpu.VMEM((block, LANES), jnp.float32),
        pltpu.VMEM((CELL_VALUES, cells // LANES, block + SUB, LANES), jnp.float32),
        pltpu.VMEM((3, cells // LANES, block + SUB, LANES), jnp.float32),
        pltpu.VMEM((3, block, cells + LANES), jnp.float32),
        pltpu.VMEM((3, block, cells), jnp.float32),
    ]
    return pl.pallas_call(
        lambda *refs: flux_kernel(layer, count, refs),
        grid=(count,),
        in_specs=specs,
        out_specs=[main] * 3,
        out_shape=[jax.ShapeDtypeStruct(f.shape, f.dtype) for f in fields],
        scratch_shapes=scratch,
        input_output_aliases=aliases,
        compiler_params=pltpu.CompilerParams(vmem_limit_bytes=VMEM_BYTES),
        cost_estimate=pl.CostEstimate(
            flops=100 * rows * cells, bytes_accessed=24 * rows * cells, transcendentals=rows * cells
        ),
        name="flux_layer",
    )(*operands)


def gravity_kernel(steps, refs):
    pot_ref, force_ref, inverse_ref = refs[:3]
    halves = refs[3:5]
    out_r, out_phi, out_pot, table_ref, *buffers, sems = refs[8:]
    density, mom_r, mom_phi = buffers
    rows_here = fetch_rows(refs[5:8], buffers, sems, steps)
    cols, block = pot_ref.shape

    @pl.when(pl.program_id(0) == 0)
    def _():
        table_ref[:cols] = halves[0][...]
        table_ref[cols : 2 * cols] = halves[0][...]
        table_ref[2 * cols :] = halves[1][...]

    pot = pot_ref[...]
    row = lax.broadcasted_iota(jnp.int32, pot.shape, 0)
    even = row % 2 == 0
    mode = (row // 2).astype(jnp.float32)
    swapped = jnp.where(even, pltpu.roll(pot, cols - 1, 0), -pltpu.roll(pot, 1, 0))
    left = jnp.concatenate(
        [pot, 0.1 * force_ref[...], swapped * (mode * inverse_ref[...])], axis=1
    )
    high, low = split_bf16(left)
    grid = lax.dot_general(
        jnp.concatenate([high, low, high], axis=0),
        table_ref[...],
        (((0,), (0,)), ((), ())),
        preferred_element_type=jnp.float32,
    )
    out_pot[...] = grid[:block]
    for layer in range(density.shape[0]):
        here = density[layer, rows_here, :]
        out_r[layer] = mom_r[layer, rows_here, :] + here * grid[block : 2 * block]
        out_phi[layer] = mom_phi[layer, rows_here, :] + here * grid[2 * block :]


def add_gravity(pot, force, inverse_mid, tables, density, mom_r, mom_phi):
    layers, rows, cells = density.shape
    cols = pot.shape[0]
    block = min(rows, 2 * LANES)
    modes_spec = pl.BlockSpec((cols, block), lambda i: (0, i))
    table_spec = pl.BlockSpec((cols, cells), lambda i: (0, 0))

    field = pl.BlockSpec((layers, block, cells), lambda i: (0, i, 0))
    grid_shape = jax.ShapeDtypeStruct(density.shape, density.dtype)
    return pl.pallas_call(
        lambda *refs: gravity_kernel(rows // block, refs),
        grid=(rows // block,),
        in_specs=[
            modes_spec, modes_spec, pl.BlockSpec((1, block), lambda i: (0, i)),
        ] + [table_spec] * 2 + [pl.BlockSpec(memory_space=pl.ANY)] * 3,
        out_specs=[field, field, pl.BlockSpec((block, cells), lambda i: (i, 0))],
        out_shape=[grid_shape, grid_shape, jax.ShapeDtypeStruct((rows, cells), jnp.float32)],
        scratch_shapes=[pltpu.VMEM((3 * cols, cells), jnp.bfloat16)]
        + [pltpu.VMEM(density.shape, density.dtype)] * 3
        + [pltpu.SemaphoreType.DMA((3, rows // block))],
        compiler_params=pltpu.CompilerParams(vmem_limit_bytes=VMEM_BYTES),
        cost_estimate=pl.CostEstimate(
            flops=18 * rows * cells * cols, bytes_accessed=44 * rows * cells, transcendentals=0
        ),
        name="add_gravity",
    )(
        pot, force, inverse_mid, *tables,
        density, mom_r, mom_phi,
    )


def exchange_rims(fields, rad_index, rad_count):
    first = jnp.stack([f[:, 0] for f in fields], axis=1)
    last = jnp.stack([f[:, -1] for f in fields], axis=1)
    if rad_count == 1:
        return first, last
    first_out, last_out = first.astype(jnp.bfloat16), last.astype(jnp.bfloat16)
    if rad_count == 2:
        other = lax.ppermute(
            jnp.where(rad_index == 0, last_out, first_out), "rad", [(0, 1), (1, 0)]
        )
        low = high = other
    else:
        up = [(i, i + 1) for i in range(rad_count - 1)]
        low = lax.ppermute(last_out, "rad", up)
        high = lax.ppermute(first_out, "rad", [(b, a) for a, b in up])
    rim_in = jnp.where(rad_index == 0, first, low.astype(first.dtype))
    rim_out = jnp.where(rad_index == rad_count - 1, last, high.astype(last.dtype))
    return rim_in, rim_out


def exchange_edges(first, last, az_count):
    right = [(i, (i + 1) % az_count) for i in range(az_count)]
    left = [(b, a) for a, b in right]
    return lax.ppermute(last, "az", right), lax.ppermute(first, "az", left)


def local(az_count, rad_count, density, mom_r, mom_phi, potential_kernel, force_kernel):
    layers, rows, cells = density.shape
    mode_count = potential_kernel.shape[0]
    pair_count = 2 * mode_count
    cols = az_count * pair_count
    step = 2.0 * math.pi / (az_count * cells)
    az_index = lax.axis_index("az")
    rad_index = lax.axis_index("rad")
    fields = (density, mom_r, mom_phi)

    azimuth = ((az_index * cells + jnp.arange(cells)).astype(jnp.float32) + 0.5) * step
    row = lax.broadcasted_iota(jnp.int32, (cols, cells), 0)
    mode = (row // 2).astype(jnp.float32)
    angle = azimuth[None, :] * mode
    cosine, sine = jnp.cos(angle), jnp.sin(angle)
    basis = pieces_of(jnp.where(row % 2 == 0, cosine, sine), 3)

    rims = exchange_rims(fields, rad_index, rad_count)
    coefs, inverse_mid = row_coefficients(rad_index * rows, rows, step)

    partial, first, last = surface_modes(fields, basis, 1.0 / (az_count * cells))
    edges = exchange_edges(first, last, az_count)
    partial, edges, rims = lax.optimization_barrier((partial, edges, rims))
    pieces = lax.all_to_all(
        partial.reshape(az_count, pair_count, rows), "az", split_axis=0, concat_axis=0, tiled=True
    )
    results = flux_layer(0, fields, rims, edges, coefs, None)
    pieces, results = lax.optimization_barrier((pieces, results))

    own = jnp.sum(pieces, axis=0).astype(jnp.bfloat16)
    pairs = lax.all_gather(own, "rad", axis=1, tiled=True)
    parts = responses(pairs, potential_kernel, force_kernel, az_count)
    every = lax.all_to_all(parts, "az", split_axis=0, concat_axis=0, tiled=True)
    coefs, parts = lax.optimization_barrier((coefs, parts))
    for layer in range(1, layers):
        results = flux_layer(layer, fields, rims, edges, coefs, results)
    pot = every[:, 0].reshape(cols, rows)
    force = every[:, 1].reshape(cols, rows)

    new_r, new_phi, potential = add_gravity(
        pot,
        force,
        inverse_mid,
        basis[:2],
        density,
        results[1],
        results[2],
    )
    return results[0], new_r, new_phi, potential


def solution(mesh):
    az_count, rad_count = mesh.shape["az"], mesh.shape["rad"]
    field = P(None, "rad", "az")
    kernel = P("az", "rad", None)
    return jax.shard_map(
        lambda *args: local(az_count, rad_count, *args),
        mesh=mesh,
        in_specs=(field, field, field, kernel, kernel),
        out_specs=(field, field, field, P("rad", "az")),
        check_vma=False,
    )
```

```python
import math

import jax
import jax.numpy as jnp
from jax import lax
from jax.experimental import pallas as pl
from jax.experimental.pallas import tpu as pltpu
from jax.sharding import PartitionSpec as P

aspect_sq = 0.0025
LANES = 128
SUB = 8
VMEM_BYTES = 60 << 20


def fetch_rows(refs, buffers, sems, steps):
    block = refs[0].shape[1] // steps

    def copy(k, place):
        if isinstance(place, int):
            rows = pl.ds(place * block, block)
        else:
            rows = pl.ds(pl.multiple_of(place * block, block), block)
        return pltpu.make_async_copy(refs[k].at[:, rows], buffers[k].at[:, rows], sems.at[k, place])

    @pl.when(pl.program_id(0) == 0)
    def _():
        for place in range(steps):
            for k in range(len(refs)):
                copy(k, place).start()

    for k in range(len(refs)):
        copy(k, pl.program_id(0)).wait()
    return pl.ds(pl.multiple_of(pl.program_id(0) * block, block), block)


def split_bf16(x):
    high = x.astype(jnp.bfloat16)
    low = (x - high.astype(jnp.float32)).astype(jnp.bfloat16)
    return high, low


def pieces_of(x, count):
    out = []
    for _ in range(count - 1):
        high = lax.reduce_precision(x, 8, 7)
        out.append(high.astype(jnp.bfloat16))
        x = x - high
    return out + [x.astype(jnp.bfloat16)]


EDGE_ROWS = 16


def modes_kernel(scale, steps, refs):
    *tables, out_ref, wide_ref, density, sems = refs[1:]
    thin_ref = tables[2]
    layers = density.shape[0]
    rows_here = fetch_rows(refs[:1], [density], sems, steps)
    cols = thin_ref.shape[0]

    @pl.when(pl.program_id(0) == 0)
    def _():
        wide_ref[:cols] = tables[0][...]
        wide_ref[cols:] = tables[1][...]

    x = density[0, rows_here, :]
    for layer in range(1, layers):
        x = x + density[layer, rows_here, :]
    high = x.astype(jnp.bfloat16)
    x = x - high.astype(jnp.float32)
    mid = x.astype(jnp.bfloat16)
    low = (x - mid.astype(jnp.float32)).astype(jnp.bfloat16)

    def product(a, table):
        return lax.dot_general(
            a, table, (((1,), (1,)), ((), ())), preferred_element_type=jnp.float32
        )

    rows = high.shape[0]
    major = product(jnp.concatenate([high, mid, low], axis=0), wide_ref[...])
    small = major[2 * rows :, :cols] + product(high, thin_ref[...])
    total = major[:rows, :cols] + (
        major[:rows, cols:] + major[rows : 2 * rows, :cols] + (major[rows : 2 * rows, cols:] + small)
    )
    out_ref[...] = (scale * total).T


def edge_kernel(refs):
    firsts, lasts = refs[:3], refs[3:6]
    first_ref, last_ref = refs[6:]
    layers, block, _ = firsts[0].shape
    lane = lax.broadcasted_iota(jnp.int32, (block, LANES), 1)
    edges = jnp.zeros((block, LANES), jnp.float32)
    for layer in range(layers):
        for base, place, tiles in ((0, 0, firsts), (EDGE_ROWS, LANES - 1, lasts)):
            for comp, tile in enumerate(tiles):
                edges = jnp.where(
                    lane == base + 3 * layer + comp,
                    jnp.broadcast_to(tile[layer, :, place : place + 1], (block, LANES)),
                    edges,
                )
    edges = edges.T
    first_ref[...] = edges[:EDGE_ROWS].astype(jnp.bfloat16)
    last_ref[...] = edges[EDGE_ROWS : 2 * EDGE_ROWS].astype(jnp.bfloat16)


def edge_cells(fields):
    layers, rows, cells = fields[0].shape
    block = min(rows, 2 * LANES)
    first = pl.BlockSpec((layers, block, LANES), lambda i: (0, i, 0))
    last = pl.BlockSpec((layers, block, LANES), lambda i: (0, i, cells // LANES - 1))
    edge_spec = pl.BlockSpec((EDGE_ROWS, block), lambda i: (0, i))
    edge_shape = jax.ShapeDtypeStruct((EDGE_ROWS, rows), jnp.bfloat16)
    return pl.pallas_call(
        lambda *refs: edge_kernel(refs),
        grid=(rows // block,),
        in_specs=[first] * 3 + [last] * 3,
        out_specs=[edge_spec, edge_spec],
        out_shape=[edge_shape, edge_shape],
        compiler_params=pltpu.CompilerParams(vmem_limit_bytes=VMEM_BYTES),
        cost_estimate=pl.CostEstimate(
            flops=40 * rows * LANES, bytes_accessed=24 * layers * rows * LANES, transcendentals=0
        ),
        name="edge_cells",
    )(*fields, *fields)


def surface_modes(density, tables, scale):
    layers, rows, cells = density.shape
    cols = tables[0].shape[0]
    block = min(rows, 2 * LANES)
    table_spec = pl.BlockSpec((cols, cells), lambda i: (0, 0))
    return pl.pallas_call(
        lambda *refs: modes_kernel(scale, rows // block, refs),
        grid=(rows // block,),
        in_specs=[pl.BlockSpec(memory_space=pl.ANY)] + [table_spec] * 3,
        out_specs=pl.BlockSpec((cols, block), lambda i: (0, i)),
        out_shape=jax.ShapeDtypeStruct((cols, rows), jnp.float32),
        scratch_shapes=[
            pltpu.VMEM((2 * cols, cells), jnp.bfloat16),
            pltpu.VMEM(density.shape, jnp.float32),
            pltpu.SemaphoreType.DMA((1, rows // block)),
        ],
        compiler_params=pltpu.CompilerParams(vmem_limit_bytes=VMEM_BYTES),
        cost_estimate=pl.CostEstimate(
            flops=12 * rows * cells * cols, bytes_accessed=4 * density.size, transcendentals=0
        ),
        name="surface_modes",
    )(density, *tables)


def response_kernel(steps, refs):
    pairs_ref, pot_ref, force_ref, out_ref, pot_buffer, force_buffer, sems = refs
    pairs = pairs_ref[...]
    buffers = (pot_buffer, force_buffer)
    rows_here = fetch_rows((pot_ref, force_ref), buffers, sems, steps)
    block, cols = out_ref.shape[3], pairs.shape[0]
    mode_of = lax.broadcasted_iota(jnp.int32, (block, cols), 1) // 2
    for place, buffer in enumerate(buffers):
        total = jnp.zeros(mode_of.shape, jnp.float32)
        for mode in range(buffer.shape[0]):
            part = lax.dot_general(
                buffer[mode, rows_here, :],
                pairs,
                (((1,), (1,)), ((), ())),
                preferred_element_type=jnp.float32,
            )
            total = jnp.where(mode_of == mode, part, total)
        out_ref[:, place] = jnp.broadcast_to(total.T[None], (out_ref.shape[0], cols, block))


def responses(pairs, potential_kernel, force_kernel, copies):
    mode_count, rows, count = potential_kernel.shape
    cols = pairs.shape[0]
    block = min(rows, LANES)
    steps = rows // block
    whole = pl.BlockSpec(memory_space=pl.ANY)
    return pl.pallas_call(
        lambda *refs: response_kernel(steps, refs),
        grid=(steps,),
        in_specs=[pl.BlockSpec((cols, count), lambda i: (0, 0)), whole, whole],
        out_specs=pl.BlockSpec((copies, 2, cols, block), lambda i: (0, 0, 0, i)),
        out_shape=jax.ShapeDtypeStruct((copies, 2, cols, rows), jnp.float32),
        scratch_shapes=[
            pltpu.VMEM(potential_kernel.shape, potential_kernel.dtype),
            pltpu.VMEM(force_kernel.shape, force_kernel.dtype),
            pltpu.SemaphoreType.DMA((2, steps)),
        ],
        compiler_params=pltpu.CompilerParams(vmem_limit_bytes=VMEM_BYTES),
        cost_estimate=pl.CostEstimate(
            flops=4 * rows * count * cols * mode_count,
            bytes_accessed=4 * potential_kernel.size,
            transcendentals=0,
        ),
        name="responses",
    )(pairs, potential_kernel, force_kernel)


ROOT_FACE, SOUND_FACE, IN, OUT, ROOT_MID, SOUND_MID, AZ, SPIN, PULL = range(9)
COEFS = 16


def row_coefficients(first_row, rows, step):
    face = jnp.exp((first_row + jnp.arange(rows + LANES + 1)).astype(jnp.float32) * step)
    inner, outer = face[:-1], face[1:]
    mid = 0.5 * (inner + outer)
    area = 0.5 * (outer * outer - inner * inner)
    sound_face = aspect_sq / inner
    sound_mid = aspect_sq / mid
    radial = (0.05 * step) / area
    columns = [
        jnp.sqrt(sound_face),
        sound_face,
        radial * inner,
        radial * outer,
        jnp.sqrt(sound_mid),
        sound_mid,
        0.05 / mid,
        (0.1 * step) / mid,
        (0.1 * step) / (mid * mid),
    ]
    columns += [jnp.zeros_like(mid)] * (COEFS - len(columns))
    return jnp.stack(columns, axis=0), (-0.1 / mid)[None, :rows]


def inverse(x):
    guess = pl.reciprocal(x, approx=True)
    return guess * (2.0 - x * guess)


class FluxBlock:
    def __init__(self, block_count, refs):
        self.fields = refs[0:3]
        self.before = refs[3:6]
        self.after = refs[6:9]
        self.rim_in, self.rim_out, coef_rows, low_rows, high_rows, coef_after = refs[9:15]
        self.block_count = block_count
        self.rows, cells = self.fields[0].shape
        self.columns = cells // LANES
        self.strips = self.rows // SUB
        self.index = pl.program_id(0)
        self.lane = lax.broadcasted_iota(jnp.int32, (SUB, LANES), 1)
        side_rows = jnp.concatenate(
            [coef_rows[...], low_rows[...].astype(jnp.float32), high_rows[...].astype(jnp.float32)], axis=0
        )
        filler = jnp.zeros((LANES - side_rows.shape[0], self.rows), jnp.float32)
        self.side = jnp.concatenate([side_rows, filler], axis=0).T
        self.coef_after = coef_after

    def wide(self, column):
        return jnp.broadcast_to(column, (SUB, LANES))

    def at(self, col):
        return pl.ds(col * LANES, LANES)

    def rows_at(self, place):
        return pl.ds(pl.multiple_of(place * SUB, SUB), SUB)

    def radial_state(self, state):
        density, mom_r, mom_phi = state
        inv = inverse(density)
        vel = mom_r * inv
        return inv, (density, mom_r, mom_phi, jnp.abs(vel), mom_r * vel, mom_phi * vel)

    def radial_flux(self, upper, lower, root, sound):
        speed = jnp.maximum(upper[3], lower[3]) + root
        return (
            (upper[1] + lower[1]) - speed * (upper[0] - lower[0]),
            ((upper[4] + lower[4]) + sound * (upper[0] + lower[0]))
            - speed * (upper[1] - lower[1]),
            (upper[5] + lower[5]) - speed * (upper[2] - lower[2]),
        )

    def azimuth_flux(self, upper, lower, root):
        speed = jnp.maximum(upper[3], lower[3]) + root
        return (
            (upper[2] + lower[2]) - speed * (upper[0] - lower[0]),
            (upper[4] + lower[4]) - speed * (upper[1] - lower[1]),
            (upper[5] + lower[5]) - speed * (upper[2] - lower[2]),
        )

    def azimuth_values(self, state, inv, cross, sound):
        density, mom_r, mom_phi = state
        vel = mom_phi * inv
        return density, mom_r, mom_phi, jnp.abs(vel), cross, mom_phi * vel + sound * density

    def ghost_values(self, layer, coef, side, sound):
        base = COEFS + side * EDGE_ROWS + 3 * layer
        state = [self.wide(coef[:, base + c : base + c + 1]) for c in range(3)]
        inv = inverse(state[0])
        return self.azimuth_values(state, inv, state[1] * state[2] * inv, sound)

    def row_before(self, col):
        return self.edge_row(col, self.index == 0, self.rim_in, self.before, SUB - 1)

    def row_after(self, col):
        return self.edge_row(col, self.index == self.block_count - 1, self.rim_out, self.after, 0)

    def edge_row(self, col, edge, rim, near, row):
        state = []
        for comp in range(3):
            value = jnp.where(
                edge, rim[comp : comp + 1, self.at(col)], near[comp][row : row + 1, self.at(col)]
            )
            state.append(jnp.broadcast_to(value, (SUB, LANES)))
        return self.radial_state(state)[1]

    def columns_of(self, coef, names):
        return [self.wide(coef[:, k : k + 1]) for k in names]


CELL_VALUES = 8


def flux_kernel(together, layer, block_count, refs):
    block = FluxBlock(block_count, refs)
    outs = refs[-8:-5]
    side, cell, faces, sides, held = refs[-5:]
    side[...] = block.side
    lane, at, fields, rows_at = block.lane, block.at, block.fields, block.rows_at
    columns, strips, rows = block.columns, block.strips, block.rows

    after = block.coef_after[...].T
    root_face, sound_face = block.columns_of(after[:SUB], (ROOT_FACE, SOUND_FACE))
    for col in range(columns):
        for slot, value in enumerate(block.row_before(col)):
            cell[slot, col, 0:SUB, :] = value
        last = [
            jnp.broadcast_to(ref[rows - 1 : rows, at(col)], (SUB, LANES)) for ref in fields
        ]
        flux = block.radial_flux(
            block.row_after(col), block.radial_state(last)[1], root_face, sound_face
        )
        for comp in range(3):
            faces[comp, col, rows : rows + SUB, :] = flux[comp]

    def shifted(place, by):
        return pl.ds(pl.multiple_of(place * SUB, SUB) + by, SUB)

    def update(place):
        here, above = rows_at(place), shifted(place, 1)
        out_coef, az = block.columns_of(side[here, :], (OUT, AZ))
        if together:
            side_row, held_row, face_row = sides[:, here, :], held[:, here, :], faces[:, :, above, :]

        for col in range(columns):
            for comp in range(3):
                if together:
                    parts = [
                        row[comp, :, k * LANES : (k + 1) * LANES]
                        for row, k in ((side_row, col + 1), (side_row, col), (held_row, col))
                    ] + [face_row[comp, col]]
                else:
                    parts = [
                        sides[comp, here, at(col + 1)], sides[comp, here, at(col)],
                        held[comp, here, at(col)], faces[comp, col, above, :],
                    ]
                edge = jnp.where(lane == 0, parts[0], parts[1])
                outs[comp][here, at(col)] = parts[2] - (
                    out_coef * parts[3] + az * pltpu.roll(edge, LANES - 1, 1)
                )

    def face_fluxes(place):
        here, inside, below = rows_at(place), rows_at(place + 1), shifted(place, SUB - 1)
        coef = side[here, :]
        root_face, sound_face, in_coef, root_mid, sound_mid, az, spin, pull = block.columns_of(
            coef, (ROOT_FACE, SOUND_FACE, IN, ROOT_MID, SOUND_MID, AZ, SPIN, PULL)
        )
        left = block.ghost_values(layer, coef, 0, sound_mid)
        if together:
            now_row, low_row = cell[:, :, inside, :], cell[:6, :, below, :]
        for col in range(columns):
            if together:
                now = [now_row[slot, col] for slot in range(CELL_VALUES)]
                lower = [low_row[slot, col] for slot in range(6)]
            else:
                now = [cell[slot, col, inside, :] for slot in range(CELL_VALUES)]
                lower = [cell[slot, col, below, :] for slot in range(6)]
            flux_r = block.radial_flux(now[:6], lower, root_face, sound_face)
            values = (*now[:3], now[6], now[5], now[7])
            lower = [
                pltpu.roll(jnp.where(lane == LANES - 1, a, b), 1, 1) for a, b in zip(left, values)
            ]
            left = values
            flux = block.azimuth_flux(values, lower, root_mid)
            for comp in range(3):
                faces[comp, col, here, :] = flux_r[comp]
                sides[comp, here, at(col)] = flux[comp]
            held[0, here, at(col)] = now[0] + (in_coef * flux_r[0] + az * flux[0])
            held[1, here, at(col)] = (now[1] + (in_coef * flux_r[1] + az * flux[1])) + (
                spin * now[7] - pull * now[0]
            )
            held[2, here, at(col)] = (now[2] + (in_coef * flux_r[2] + az * flux[2])) - spin * now[5]
        values = block.ghost_values(layer, coef, 1, sound_mid)
        lower = [pltpu.roll(a, 1, 1) for a in left]
        for comp, value in enumerate(block.azimuth_flux(values, lower, root_mid)):
            sides[comp, here, at(columns)] = value

    def cell_values(place):
        here, inside = rows_at(place), rows_at(place + 1)
        (sound_mid,) = block.columns_of(side[here, :], (SOUND_MID,))
        for col in range(columns):
            state = [ref[here, at(col)] for ref in fields]
            inv, values = block.radial_state(state)
            vel = state[2] * inv
            values = (*values, jnp.abs(vel), state[2] * vel + sound_mid * state[0])
            for slot, value in enumerate(values):
                cell[slot, col, inside, :] = value

    def iteration(place, carry):
        def clamped(late):
            return jnp.clip(place - late, 0, strips - 1)

        update(clamped(3))
        face_fluxes(clamped(1))
        cell_values(clamped(0))
        return carry

    lax.fori_loop(0, strips + 3, iteration, 0)


def flux_layer(layer, together, fields, rims, edges, coefs, so_far):
    layers, rows, cells = fields[0].shape
    block = min(rows, 2 * LANES)
    count = rows // block
    per = block // SUB
    main = pl.BlockSpec((None, block, cells), lambda i: (layer, i, 0))
    before = pl.BlockSpec((None, SUB, cells), lambda i: (layer, jnp.maximum(i * per - 1, 0), 0))
    after = pl.BlockSpec(
        (None, SUB, cells), lambda i: (layer, jnp.minimum((i + 1) * per, rows // SUB - 1), 0)
    )
    rim = pl.BlockSpec((None, 3, cells), lambda i: (layer, 0, 0))
    operands = [*fields, *fields, *fields, *rims, coefs, *edges, coefs]
    specs = [main] * 3 + [before] * 3 + [after] * 3 + [
        rim,
        rim,
        pl.BlockSpec((COEFS, block), lambda i: (0, i)),
        pl.BlockSpec((EDGE_ROWS, block), lambda i: (0, i)),
        pl.BlockSpec((EDGE_ROWS, block), lambda i: (0, i)),
        pl.BlockSpec((COEFS, LANES), lambda i: (0, (i + 1) * (block // LANES))),
    ]
    aliases = {}
    if so_far is not None:
        for k, array in enumerate(so_far):
            aliases[len(operands)] = k
            operands.append(array)
            specs.append(pl.BlockSpec(memory_space=pl.ANY))
    scratch = [
        pltpu.VMEM((block, LANES), jnp.float32),
        pltpu.VMEM((CELL_VALUES, cells // LANES, block + SUB, LANES), jnp.float32),
        pltpu.VMEM((3, cells // LANES, block + SUB, LANES), jnp.float32),
        pltpu.VMEM((3, block, cells + LANES), jnp.float32),
        pltpu.VMEM((3, block, cells), jnp.float32),
    ]
    return pl.pallas_call(
        lambda *refs: flux_kernel(together, layer, count, refs),
        grid=(count,),
        in_specs=specs,
        out_specs=[main] * 3,
        out_shape=[jax.ShapeDtypeStruct(f.shape, f.dtype) for f in fields],
        scratch_shapes=scratch,
        input_output_aliases=aliases,
        compiler_params=pltpu.CompilerParams(vmem_limit_bytes=VMEM_BYTES),
        cost_estimate=pl.CostEstimate(
            flops=100 * rows * cells, bytes_accessed=24 * rows * cells, transcendentals=rows * cells
        ),
        name="flux_layer",
    )(*operands)


def gravity_kernel(steps, refs):
    every_ref, inverse_ref = refs[:2]
    halves = refs[2:4]
    out_r, out_phi, out_pot, table_ref, *buffers, sems = refs[7:]
    density, mom_r, mom_phi = buffers
    rows_here = fetch_rows(refs[4:7], buffers, sems, steps)
    copies, _, part, block = every_ref.shape
    cols = copies * part

    @pl.when(pl.program_id(0) == 0)
    def _():
        table_ref[:cols] = halves[0][...]
        table_ref[cols : 2 * cols] = halves[0][...]
        table_ref[2 * cols :] = halves[1][...]

    pot = every_ref[:, 0].reshape(cols, block)
    force = every_ref[:, 1].reshape(cols, block)
    row = lax.broadcasted_iota(jnp.int32, pot.shape, 0)
    even = row % 2 == 0
    mode = (row // 2).astype(jnp.float32)
    swapped = jnp.where(even, pltpu.roll(pot, cols - 1, 0), -pltpu.roll(pot, 1, 0))
    left = jnp.concatenate(
        [pot, 0.1 * force, swapped * (mode * inverse_ref[...])], axis=1
    )
    high, low = split_bf16(left)
    grid = lax.dot_general(
        jnp.concatenate([high, low, high], axis=0),
        table_ref[...],
        (((0,), (0,)), ((), ())),
        preferred_element_type=jnp.float32,
    )
    out_pot[...] = grid[:block]
    for layer in range(density.shape[0]):
        here = density[layer, rows_here, :]
        out_r[layer] = mom_r[layer, rows_here, :] + here * grid[block : 2 * block]
        out_phi[layer] = mom_phi[layer, rows_here, :] + here * grid[2 * block :]


def add_gravity(every, inverse_mid, tables, density, mom_r, mom_phi):
    layers, rows, cells = density.shape
    cols = every.shape[0] * every.shape[2]
    block = min(rows, 2 * LANES)
    modes_spec = pl.BlockSpec((*every.shape[:3], block), lambda i: (0, 0, 0, i))
    table_spec = pl.BlockSpec((cols, cells), lambda i: (0, 0))

    field = pl.BlockSpec((layers, block, cells), lambda i: (0, i, 0))
    grid_shape = jax.ShapeDtypeStruct(density.shape, density.dtype)
    return pl.pallas_call(
        lambda *refs: gravity_kernel(rows // block, refs),
        grid=(rows // block,),
        in_specs=[
            modes_spec, pl.BlockSpec((1, block), lambda i: (0, i)),
        ] + [table_spec] * 2 + [pl.BlockSpec(memory_space=pl.ANY)] * 3,
        out_specs=[field, field, pl.BlockSpec((block, cells), lambda i: (i, 0))],
        out_shape=[grid_shape, grid_shape, jax.ShapeDtypeStruct((rows, cells), jnp.float32)],
        scratch_shapes=[pltpu.VMEM((3 * cols, cells), jnp.bfloat16)]
        + [pltpu.VMEM(density.shape, density.dtype)] * 3
        + [pltpu.SemaphoreType.DMA((3, rows // block))],
        compiler_params=pltpu.CompilerParams(vmem_limit_bytes=VMEM_BYTES),
        cost_estimate=pl.CostEstimate(
            flops=18 * rows * cells * cols, bytes_accessed=44 * rows * cells, transcendentals=0
        ),
        name="add_gravity",
    )(
        every, inverse_mid, *tables,
        density, mom_r, mom_phi,
    )


def exchange_rims(fields, rad_index, rad_count):
    first = jnp.stack([f[:, 0] for f in fields], axis=1)
    last = jnp.stack([f[:, -1] for f in fields], axis=1)
    if rad_count == 1:
        return first, last
    first_out, last_out = first.astype(jnp.bfloat16), last.astype(jnp.bfloat16)
    if rad_count == 2:
        other = lax.ppermute(
            jnp.where(rad_index == 0, last_out, first_out), "rad", [(0, 1), (1, 0)]
        )
        low = high = other
    else:
        up = [(i, i + 1) for i in range(rad_count - 1)]
        low = lax.ppermute(last_out, "rad", up)
        high = lax.ppermute(first_out, "rad", [(b, a) for a, b in up])
    rim_in = jnp.where(rad_index == 0, first, low.astype(first.dtype))
    rim_out = jnp.where(rad_index == rad_count - 1, last, high.astype(last.dtype))
    return rim_in, rim_out


def exchange_edges(first, last, az_count):
    right = [(i, (i + 1) % az_count) for i in range(az_count)]
    left = [(b, a) for a, b in right]
    return lax.ppermute(last, "az", right), lax.ppermute(first, "az", left)


def local(az_count, rad_count, density, mom_r, mom_phi, potential_kernel, force_kernel):
    layers, rows, cells = density.shape
    mode_count = potential_kernel.shape[0]
    pair_count = 2 * mode_count
    cols = az_count * pair_count
    step = 2.0 * math.pi / (az_count * cells)
    az_index = lax.axis_index("az")
    rad_index = lax.axis_index("rad")
    fields = (density, mom_r, mom_phi)

    azimuth = ((az_index * cells + jnp.arange(cells)).astype(jnp.float32) + 0.5) * step
    row = lax.broadcasted_iota(jnp.int32, (cols, cells), 0)
    mode = (row // 2).astype(jnp.float32)
    angle = azimuth[None, :] * mode
    cosine, sine = jnp.cos(angle), jnp.sin(angle)
    basis = pieces_of(jnp.where(row % 2 == 0, cosine, sine), 3)

    rims = exchange_rims(fields, rad_index, rad_count)
    coefs, inverse_mid = row_coefficients(rad_index * rows, rows, step)

    first, last = edge_cells(fields)
    basis, first, last = lax.optimization_barrier((basis, first, last))
    edges = exchange_edges(first, last, az_count)
    partial = surface_modes(density, basis, 1.0 / (az_count * cells))
    partial, edges, rims = lax.optimization_barrier((partial, edges, rims))
    pieces = lax.all_to_all(
        partial.reshape(az_count, pair_count, rows), "az", split_axis=0, concat_axis=0, tiled=True
    )
    results = flux_layer(0, True, fields, rims, edges, coefs, None)
    pieces, results = lax.optimization_barrier((pieces, results))

    own = jnp.sum(pieces, axis=0).astype(jnp.bfloat16)
    pairs = lax.all_gather(own, "rad", axis=1, tiled=True)
    parts = responses(pairs, potential_kernel, force_kernel, az_count)
    every = lax.all_to_all(parts, "az", split_axis=0, concat_axis=0, tiled=True)
    coefs, parts = lax.optimization_barrier((coefs, parts))
    for layer in range(1, layers):
        results = flux_layer(layer, False, fields, rims, edges, coefs, results)
    if pair_count % SUB:
        every = jnp.swapaxes(every, 0, 1).reshape(1, 2, cols, rows)

    new_r, new_phi, potential = add_gravity(
        every,
        inverse_mid,
        basis[:2],
        density,
        results[1],
        results[2],
    )
    return results[0], new_r, new_phi, potential


def solution(mesh):
    az_count, rad_count = mesh.shape["az"], mesh.shape["rad"]
    field = P(None, "rad", "az")
    kernel = P("az", "rad", None)
    return jax.shard_map(
        lambda *args: local(az_count, rad_count, *args),
        mesh=mesh,
        in_specs=(field, field, field, kernel, kernel),
        out_specs=(field, field, field, P("rad", "az")),
        check_vma=False,
    )
```

```python
import math

import jax
import jax.numpy as jnp
from jax import lax
from jax.experimental import pallas as pl
from jax.experimental.pallas import tpu as pltpu
from jax.sharding import PartitionSpec as P

aspect_sq = 0.0025
LANES = 128
SUB = 8
VMEM_BYTES = 60 << 20


def fetch_rows(refs, buffers, sems, steps):
    block = refs[0].shape[1] // steps

    def copy(k, place):
        if isinstance(place, int):
            rows = pl.ds(place * block, block)
        else:
            rows = pl.ds(pl.multiple_of(place * block, block), block)
        return pltpu.make_async_copy(refs[k].at[:, rows], buffers[k].at[:, rows], sems.at[k, place])

    @pl.when(pl.program_id(0) == 0)
    def _():
        for place in range(steps):
            for k in range(len(refs)):
                copy(k, place).start()

    for k in range(len(refs)):
        copy(k, pl.program_id(0)).wait()
    return pl.ds(pl.multiple_of(pl.program_id(0) * block, block), block)


def split_bf16(x):
    high = x.astype(jnp.bfloat16)
    low = (x - high.astype(jnp.float32)).astype(jnp.bfloat16)
    return high, low


def pieces_of(x, count):
    out = []
    for _ in range(count - 1):
        high = lax.reduce_precision(x, 8, 7)
        out.append(high.astype(jnp.bfloat16))
        x = x - high
    return out + [x.astype(jnp.bfloat16)]


EDGE_ROWS = 16


def modes_kernel(scale, steps, refs):
    *tables, out_ref, wide_ref, density, sems = refs[1:]
    thin_ref = tables[2]
    layers = density.shape[0]
    rows_here = fetch_rows(refs[:1], [density], sems, steps)
    cols = thin_ref.shape[0]

    @pl.when(pl.program_id(0) == 0)
    def _():
        wide_ref[:cols] = tables[0][...]
        wide_ref[cols:] = tables[1][...]

    x = density[0, rows_here, :]
    for layer in range(1, layers):
        x = x + density[layer, rows_here, :]
    high = x.astype(jnp.bfloat16)
    x = x - high.astype(jnp.float32)
    mid = x.astype(jnp.bfloat16)
    low = (x - mid.astype(jnp.float32)).astype(jnp.bfloat16)

    def product(a, table):
        return lax.dot_general(
            a, table, (((1,), (1,)), ((), ())), preferred_element_type=jnp.float32
        )

    rows = high.shape[0]
    major = product(jnp.concatenate([high, mid, low], axis=0), wide_ref[...])
    small = major[2 * rows :, :cols] + product(high, thin_ref[...])
    total = major[:rows, :cols] + (
        major[:rows, cols:] + major[rows : 2 * rows, :cols] + (major[rows : 2 * rows, cols:] + small)
    )
    out_ref[...] = (scale * total).T


def edge_kernel(refs):
    firsts, lasts = refs[:3], refs[3:6]
    first_ref, last_ref = refs[6:]
    layers, block, _ = firsts[0].shape
    lane = lax.broadcasted_iota(jnp.int32, (block, LANES), 1)
    edges = jnp.zeros((block, LANES), jnp.float32)
    for layer in range(layers):
        for base, place, tiles in ((0, 0, firsts), (EDGE_ROWS, LANES - 1, lasts)):
            for comp, tile in enumerate(tiles):
                edges = jnp.where(
                    lane == base + 3 * layer + comp,
                    jnp.broadcast_to(tile[layer, :, place : place + 1], (block, LANES)),
                    edges,
                )
    edges = edges.T
    first_ref[...] = edges[:EDGE_ROWS].astype(jnp.bfloat16)
    last_ref[...] = edges[EDGE_ROWS : 2 * EDGE_ROWS].astype(jnp.bfloat16)


def edge_cells(fields):
    layers, rows, cells = fields[0].shape
    block = min(rows, 2 * LANES)
    first = pl.BlockSpec((layers, block, LANES), lambda i: (0, i, 0))
    last = pl.BlockSpec((layers, block, LANES), lambda i: (0, i, cells // LANES - 1))
    edge_spec = pl.BlockSpec((EDGE_ROWS, block), lambda i: (0, i))
    edge_shape = jax.ShapeDtypeStruct((EDGE_ROWS, rows), jnp.bfloat16)
    return pl.pallas_call(
        lambda *refs: edge_kernel(refs),
        grid=(rows // block,),
        in_specs=[first] * 3 + [last] * 3,
        out_specs=[edge_spec, edge_spec],
        out_shape=[edge_shape, edge_shape],
        compiler_params=pltpu.CompilerParams(vmem_limit_bytes=VMEM_BYTES),
        cost_estimate=pl.CostEstimate(
            flops=40 * rows * LANES, bytes_accessed=24 * layers * rows * LANES, transcendentals=0
        ),
        name="edge_cells",
    )(*fields, *fields)


def surface_modes(density, tables, scale):
    layers, rows, cells = density.shape
    cols = tables[0].shape[0]
    block = min(rows, 2 * LANES)
    table_spec = pl.BlockSpec((cols, cells), lambda i: (0, 0))
    return pl.pallas_call(
        lambda *refs: modes_kernel(scale, rows // block, refs),
        grid=(rows // block,),
        in_specs=[pl.BlockSpec(memory_space=pl.ANY)] + [table_spec] * 3,
        out_specs=pl.BlockSpec((cols, block), lambda i: (0, i)),
        out_shape=jax.ShapeDtypeStruct((cols, rows), jnp.float32),
        scratch_shapes=[
            pltpu.VMEM((2 * cols, cells), jnp.bfloat16),
            pltpu.VMEM(density.shape, jnp.float32),
            pltpu.SemaphoreType.DMA((1, rows // block)),
        ],
        compiler_params=pltpu.CompilerParams(vmem_limit_bytes=VMEM_BYTES),
        cost_estimate=pl.CostEstimate(
            flops=12 * rows * cells * cols, bytes_accessed=4 * density.size, transcendentals=0
        ),
        name="surface_modes",
    )(density, *tables)


def response_kernel(steps, refs):
    pairs_ref, pot_ref, force_ref, out_ref, pot_buffer, force_buffer, sems = refs
    pairs = pairs_ref[...]
    buffers = (pot_buffer, force_buffer)
    rows_here = fetch_rows((pot_ref, force_ref), buffers, sems, steps)
    block, cols = out_ref.shape[3], pairs.shape[0]
    mode_of = lax.broadcasted_iota(jnp.int32, (block, cols), 1) // 2
    for place, buffer in enumerate(buffers):
        total = jnp.zeros(mode_of.shape, jnp.float32)
        for mode in range(buffer.shape[0]):
            part = lax.dot_general(
                buffer[mode, rows_here, :],
                pairs,
                (((1,), (1,)), ((), ())),
                preferred_element_type=jnp.float32,
            )
            total = jnp.where(mode_of == mode, part, total)
        out_ref[:, place] = jnp.broadcast_to(total.T[None], (out_ref.shape[0], cols, block))


def responses(pairs, potential_kernel, force_kernel, copies):
    mode_count, rows, count = potential_kernel.shape
    cols = pairs.shape[0]
    block = min(rows, LANES)
    steps = rows // block
    whole = pl.BlockSpec(memory_space=pl.ANY)
    return pl.pallas_call(
        lambda *refs: response_kernel(steps, refs),
        grid=(steps,),
        in_specs=[pl.BlockSpec((cols, count), lambda i: (0, 0)), whole, whole],
        out_specs=pl.BlockSpec((copies, 2, cols, block), lambda i: (0, 0, 0, i)),
        out_shape=jax.ShapeDtypeStruct((copies, 2, cols, rows), jnp.float32),
        scratch_shapes=[
            pltpu.VMEM(potential_kernel.shape, potential_kernel.dtype),
            pltpu.VMEM(force_kernel.shape, force_kernel.dtype),
            pltpu.SemaphoreType.DMA((2, steps)),
        ],
        compiler_params=pltpu.CompilerParams(vmem_limit_bytes=VMEM_BYTES),
        cost_estimate=pl.CostEstimate(
            flops=4 * rows * count * cols * mode_count,
            bytes_accessed=4 * potential_kernel.size,
            transcendentals=0,
        ),
        name="responses",
    )(pairs, potential_kernel, force_kernel)


ROOT_FACE, SOUND_FACE, IN, OUT, ROOT_MID, SOUND_MID, AZ, SPIN, PULL = range(9)
COEFS = 16


def row_coefficients(first_row, rows, step):
    face = jnp.exp((first_row + jnp.arange(rows + LANES + 1)).astype(jnp.float32) * step)
    inner, outer = face[:-1], face[1:]
    mid = 0.5 * (inner + outer)
    area = 0.5 * (outer * outer - inner * inner)
    sound_face = aspect_sq / inner
    sound_mid = aspect_sq / mid
    radial = (0.05 * step) / area
    columns = [
        jnp.sqrt(sound_face),
        sound_face,
        radial * inner,
        radial * outer,
        jnp.sqrt(sound_mid),
        sound_mid,
        0.05 / mid,
        (0.1 * step) / mid,
        (0.1 * step) / (mid * mid),
    ]
    columns += [jnp.zeros_like(mid)] * (COEFS - len(columns))
    return jnp.stack(columns, axis=0), (-0.1 / mid)[None, :rows]


def inverse(x):
    guess = pl.reciprocal(x, approx=True)
    return guess * (2.0 - x * guess)


class FluxBlock:
    def __init__(self, block_count, refs):
        self.fields = refs[0:3]
        self.before = refs[3:6]
        self.after = refs[6:9]
        self.rim_in, self.rim_out, coef_rows, low_rows, high_rows, coef_after = refs[9:15]
        self.block_count = block_count
        self.rows, cells = self.fields[0].shape
        self.columns = cells // LANES
        self.strips = self.rows // SUB
        self.index = pl.program_id(0)
        self.lane = lax.broadcasted_iota(jnp.int32, (SUB, LANES), 1)
        side_rows = jnp.concatenate(
            [coef_rows[...], low_rows[...].astype(jnp.float32), high_rows[...].astype(jnp.float32)], axis=0
        )
        filler = jnp.zeros((LANES - side_rows.shape[0], self.rows), jnp.float32)
        self.side = jnp.concatenate([side_rows, filler], axis=0).T
        self.coef_after = coef_after

    def wide(self, column):
        return jnp.broadcast_to(column, (SUB, LANES))

    def at(self, col):
        return pl.ds(col * LANES, LANES)

    def rows_at(self, place):
        return pl.ds(pl.multiple_of(place * SUB, SUB), SUB)

    def radial_state(self, state):
        density, mom_r, mom_phi = state
        inv = inverse(density)
        vel = mom_r * inv
        return inv, (density, mom_r, mom_phi, jnp.abs(vel), mom_r * vel, mom_phi * vel)

    def radial_flux(self, upper, lower, root, sound):
        speed = jnp.maximum(upper[3], lower[3]) + root
        return (
            (upper[1] + lower[1]) - speed * (upper[0] - lower[0]),
            ((upper[4] + lower[4]) + sound * (upper[0] + lower[0]))
            - speed * (upper[1] - lower[1]),
            (upper[5] + lower[5]) - speed * (upper[2] - lower[2]),
        )

    def azimuth_flux(self, upper, lower, root):
        speed = jnp.maximum(upper[3], lower[3]) + root
        return (
            (upper[2] + lower[2]) - speed * (upper[0] - lower[0]),
            (upper[4] + lower[4]) - speed * (upper[1] - lower[1]),
            (upper[5] + lower[5]) - speed * (upper[2] - lower[2]),
        )

    def azimuth_values(self, state, inv, cross, sound):
        density, mom_r, mom_phi = state
        vel = mom_phi * inv
        return density, mom_r, mom_phi, jnp.abs(vel), cross, mom_phi * vel + sound * density

    def ghost_values(self, layer, coef, side, sound):
        base = COEFS + side * EDGE_ROWS + 3 * layer
        state = [self.wide(coef[:, base + c : base + c + 1]) for c in range(3)]
        inv = inverse(state[0])
        return self.azimuth_values(state, inv, state[1] * state[2] * inv, sound)

    def row_before(self, col):
        return self.edge_row(col, self.index == 0, self.rim_in, self.before, SUB - 1)

    def row_after(self, col):
        return self.edge_row(col, self.index == self.block_count - 1, self.rim_out, self.after, 0)

    def edge_row(self, col, edge, rim, near, row):
        state = []
        for comp in range(3):
            value = jnp.where(
                edge, rim[comp : comp + 1, self.at(col)], near[comp][row : row + 1, self.at(col)]
            )
            state.append(jnp.broadcast_to(value, (SUB, LANES)))
        return self.radial_state(state)[1]

    def columns_of(self, coef, names):
        return [self.wide(coef[:, k : k + 1]) for k in names]


CELL_VALUES = 8


def flux_kernel(lag, layer, block_count, refs):
    block = FluxBlock(block_count, refs)
    outs = refs[-7:-4]
    side, cell, faces, sides = refs[-4:]
    side[...] = block.side
    lane, at, fields, rows_at = block.lane, block.at, block.fields, block.rows_at
    columns, strips, rows = block.columns, block.strips, block.rows

    after = block.coef_after[...].T
    root_face, sound_face = block.columns_of(after[:SUB], (ROOT_FACE, SOUND_FACE))
    for col in range(columns):
        for slot, value in enumerate(block.row_before(col)):
            cell[slot, col, 0:SUB, :] = value
        last = [
            jnp.broadcast_to(ref[rows - 1 : rows, at(col)], (SUB, LANES)) for ref in fields
        ]
        flux = block.radial_flux(
            block.row_after(col), block.radial_state(last)[1], root_face, sound_face
        )
        for comp in range(3):
            faces[comp, col, rows : rows + SUB, :] = flux[comp]

    def shifted(place, by):
        return pl.ds(pl.multiple_of(place * SUB, SUB) + by, SUB)

    def update(place):
        here, inside, above = rows_at(place), rows_at(place + 1), shifted(place, 1)
        in_coef, out_coef, spin, pull = block.columns_of(side[here, :], (IN, OUT, SPIN, PULL))
        for col in range(columns):
            density, mom_r, mom_phi, cross, push = (
                cell[slot, col, inside, :] for slot in (0, 1, 2, 5, 7)
            )
            base = (
                density, mom_r + (spin * push - pull * density), mom_phi - spin * cross
            )
            for comp in range(3):
                low = sides[comp, here, at(col)]
                edge = jnp.where(lane == 0, sides[comp, here, at(col + 1)], low)
                outs[comp][here, at(col)] = base[comp] + (
                    (in_coef * faces[comp, col, here, :] - out_coef * faces[comp, col, above, :])
                    + (low - pltpu.roll(edge, LANES - 1, 1))
                )

    def face_fluxes(place):
        here, inside, below = rows_at(place), rows_at(place + 1), shifted(place, SUB - 1)
        coef = side[here, :]
        root_face, sound_face, root_mid, sound_mid, az = block.columns_of(
            coef, (ROOT_FACE, SOUND_FACE, ROOT_MID, SOUND_MID, AZ)
        )
        left = block.ghost_values(layer, coef, 0, sound_mid)
        for col in range(columns):
            now = [cell[slot, col, inside, :] for slot in range(CELL_VALUES)]
            lower = [cell[slot, col, below, :] for slot in range(6)]
            flux_r = block.radial_flux(now[:6], lower, root_face, sound_face)
            values = (*now[:3], now[6], now[5], now[7])
            lower = [
                pltpu.roll(jnp.where(lane == LANES - 1, a, b), 1, 1) for a, b in zip(left, values)
            ]
            left = values
            flux = block.azimuth_flux(values, lower, root_mid)
            for comp in range(3):
                faces[comp, col, here, :] = flux_r[comp]
                sides[comp, here, at(col)] = az * flux[comp]
        values = block.ghost_values(layer, coef, 1, sound_mid)
        lower = [pltpu.roll(a, 1, 1) for a in left]
        for comp, value in enumerate(block.azimuth_flux(values, lower, root_mid)):
            sides[comp, here, at(columns)] = az * value

    def cell_values(place):
        here, inside = rows_at(place), rows_at(place + 1)
        (sound_mid,) = block.columns_of(side[here, :], (SOUND_MID,))
        for col in range(columns):
            state = [ref[here, at(col)] for ref in fields]
            inv, values = block.radial_state(state)
            vel = state[2] * inv
            values = (*values, jnp.abs(vel), state[2] * vel + sound_mid * state[0])
            for slot, value in enumerate(values):
                cell[slot, col, inside, :] = value

    def iteration(place, carry):
        def clamped(late):
            return jnp.clip(place - late, 0, strips - 1)

        if lag == 0:
            cell_values(clamped(0))
        face_fluxes(clamped(lag))
        update(clamped(lag + 1))
        if lag > 0:
            cell_values(clamped(0))
        return carry

    lax.fori_loop(0, strips + lag + 1, iteration, 0)


def flux_layer(layer, lag, fields, rims, edges, coefs, so_far):
    layers, rows, cells = fields[0].shape
    block = min(rows, 2 * LANES)
    count = rows // block
    per = block // SUB
    main = pl.BlockSpec((None, block, cells), lambda i: (layer, i, 0))
    before = pl.BlockSpec((None, SUB, cells), lambda i: (layer, jnp.maximum(i * per - 1, 0), 0))
    after = pl.BlockSpec(
        (None, SUB, cells), lambda i: (layer, jnp.minimum((i + 1) * per, rows // SUB - 1), 0)
    )
    rim = pl.BlockSpec((None, 3, cells), lambda i: (layer, 0, 0))
    operands = [*fields, *fields, *fields, *rims, coefs, *edges, coefs]
    specs = [main] * 3 + [before] * 3 + [after] * 3 + [
        rim,
        rim,
        pl.BlockSpec((COEFS, block), lambda i: (0, i)),
        pl.BlockSpec((EDGE_ROWS, block), lambda i: (0, i)),
        pl.BlockSpec((EDGE_ROWS, block), lambda i: (0, i)),
        pl.BlockSpec((COEFS, LANES), lambda i: (0, (i + 1) * (block // LANES))),
    ]
    aliases = {}
    if so_far is not None:
        for k, array in enumerate(so_far):
            aliases[len(operands)] = k
            operands.append(array)
            specs.append(pl.BlockSpec(memory_space=pl.ANY))
    scratch = [
        pltpu.VMEM((block, LANES), jnp.float32),
        pltpu.VMEM((CELL_VALUES, cells // LANES, block + SUB, LANES), jnp.float32),
        pltpu.VMEM((3, cells // LANES, block + SUB, LANES), jnp.float32),
        pltpu.VMEM((3, block, cells + LANES), jnp.float32),
    ]
    return pl.pallas_call(
        lambda *refs: flux_kernel(lag, layer, count, refs),
        grid=(count,),
        in_specs=specs,
        out_specs=[main] * 3,
        out_shape=[jax.ShapeDtypeStruct(f.shape, f.dtype) for f in fields],
        scratch_shapes=scratch,
        input_output_aliases=aliases,
        compiler_params=pltpu.CompilerParams(vmem_limit_bytes=VMEM_BYTES),
        cost_estimate=pl.CostEstimate(
            flops=100 * rows * cells, bytes_accessed=24 * rows * cells, transcendentals=rows * cells
        ),
        name="flux_layer",
    )(*operands)


def gravity_kernel(steps, refs):
    every_ref, inverse_ref = refs[:2]
    halves = refs[2:4]
    out_r, out_phi, out_pot, table_ref, *buffers, sems = refs[7:]
    density, mom_r, mom_phi = buffers
    rows_here = fetch_rows(refs[4:7], buffers, sems, steps)
    copies, _, part, block = every_ref.shape
    cols = copies * part

    @pl.when(pl.program_id(0) == 0)
    def _():
        table_ref[:cols] = halves[0][...]
        table_ref[cols : 2 * cols] = halves[0][...]
        table_ref[2 * cols :] = halves[1][...]

    pot = every_ref[:, 0].reshape(cols, block)
    force = every_ref[:, 1].reshape(cols, block)
    row = lax.broadcasted_iota(jnp.int32, pot.shape, 0)
    even = row % 2 == 0
    mode = (row // 2).astype(jnp.float32)
    swapped = jnp.where(even, pltpu.roll(pot, cols - 1, 0), -pltpu.roll(pot, 1, 0))
    left = jnp.concatenate(
        [pot, 0.1 * force, swapped * (mode * inverse_ref[...])], axis=1
    )
    high, low = split_bf16(left)
    grid = lax.dot_general(
        jnp.concatenate([high, low, high], axis=0),
        table_ref[...],
        (((0,), (0,)), ((), ())),
        preferred_element_type=jnp.float32,
    )
    out_pot[...] = grid[:block]
    for layer in range(density.shape[0]):
        here = density[layer, rows_here, :]
        out_r[layer] = mom_r[layer, rows_here, :] + here * grid[block : 2 * block]
        out_phi[layer] = mom_phi[layer, rows_here, :] + here * grid[2 * block :]


def add_gravity(every, inverse_mid, tables, density, mom_r, mom_phi):
    layers, rows, cells = density.shape
    cols = every.shape[0] * every.shape[2]
    block = min(rows, LANES)
    modes_spec = pl.BlockSpec((*every.shape[:3], block), lambda i: (0, 0, 0, i))
    table_spec = pl.BlockSpec((cols, cells), lambda i: (0, 0))

    field = pl.BlockSpec((layers, block, cells), lambda i: (0, i, 0))
    grid_shape = jax.ShapeDtypeStruct(density.shape, density.dtype)
    return pl.pallas_call(
        lambda *refs: gravity_kernel(rows // block, refs),
        grid=(rows // block,),
        in_specs=[
            modes_spec, pl.BlockSpec((1, block), lambda i: (0, i)),
        ] + [table_spec] * 2 + [pl.BlockSpec(memory_space=pl.ANY)] * 3,
        out_specs=[field, field, pl.BlockSpec((block, cells), lambda i: (i, 0))],
        out_shape=[grid_shape, grid_shape, jax.ShapeDtypeStruct((rows, cells), jnp.float32)],
        scratch_shapes=[pltpu.VMEM((3 * cols, cells), jnp.bfloat16)]
        + [pltpu.VMEM(density.shape, density.dtype)] * 3
        + [pltpu.SemaphoreType.DMA((3, rows // block))],
        compiler_params=pltpu.CompilerParams(vmem_limit_bytes=VMEM_BYTES),
        cost_estimate=pl.CostEstimate(
            flops=18 * rows * cells * cols, bytes_accessed=44 * rows * cells, transcendentals=0
        ),
        name="add_gravity",
    )(
        every, inverse_mid, *tables,
        density, mom_r, mom_phi,
    )


def exchange_rims(fields, rad_index, rad_count):
    first = jnp.stack([f[:, 0] for f in fields], axis=1)
    last = jnp.stack([f[:, -1] for f in fields], axis=1)
    if rad_count == 1:
        return first, last
    first_out, last_out = first.astype(jnp.bfloat16), last.astype(jnp.bfloat16)
    if rad_count == 2:
        other = lax.ppermute(
            jnp.where(rad_index == 0, last_out, first_out), "rad", [(0, 1), (1, 0)]
        )
        low = high = other
    else:
        up = [(i, i + 1) for i in range(rad_count - 1)]
        low = lax.ppermute(last_out, "rad", up)
        high = lax.ppermute(first_out, "rad", [(b, a) for a, b in up])
    rim_in = jnp.where(rad_index == 0, first, low.astype(first.dtype))
    rim_out = jnp.where(rad_index == rad_count - 1, last, high.astype(last.dtype))
    return rim_in, rim_out


def exchange_edges(first, last, az_count):
    right = [(i, (i + 1) % az_count) for i in range(az_count)]
    left = [(b, a) for a, b in right]
    return lax.ppermute(last, "az", right), lax.ppermute(first, "az", left)


def local(az_count, rad_count, density, mom_r, mom_phi, potential_kernel, force_kernel):
    layers, rows, cells = density.shape
    mode_count = potential_kernel.shape[0]
    pair_count = 2 * mode_count
    cols = az_count * pair_count
    step = 2.0 * math.pi / (az_count * cells)
    az_index = lax.axis_index("az")
    rad_index = lax.axis_index("rad")
    fields = (density, mom_r, mom_phi)

    azimuth = ((az_index * cells + jnp.arange(cells)).astype(jnp.float32) + 0.5) * step
    row = lax.broadcasted_iota(jnp.int32, (cols, cells), 0)
    mode = (row // 2).astype(jnp.float32)
    angle = azimuth[None, :] * mode
    cosine, sine = jnp.cos(angle), jnp.sin(angle)
    basis = pieces_of(jnp.where(row % 2 == 0, cosine, sine), 3)

    rims = exchange_rims(fields, rad_index, rad_count)
    coefs, inverse_mid = row_coefficients(rad_index * rows, rows, step)

    first, last = edge_cells(fields)
    basis, first, last = lax.optimization_barrier((basis, first, last))
    edges = exchange_edges(first, last, az_count)
    partial = surface_modes(density, basis, 1.0 / (az_count * cells))
    partial, edges, rims = lax.optimization_barrier((partial, edges, rims))
    pieces = lax.all_to_all(
        partial.reshape(az_count, pair_count, rows), "az", split_axis=0, concat_axis=0, tiled=True
    )
    results = flux_layer(0, 1, fields, rims, edges, coefs, None)
    pieces, results = lax.optimization_barrier((pieces, results))

    own = jnp.sum(pieces, axis=0).astype(jnp.bfloat16)
    pairs = lax.all_gather(own, "rad", axis=1, tiled=True)
    parts = responses(pairs, potential_kernel, force_kernel, az_count)
    every = lax.all_to_all(parts, "az", split_axis=0, concat_axis=0, tiled=True)
    coefs, parts = lax.optimization_barrier((coefs, parts))
    for layer in range(1, layers):
        results = flux_layer(layer, 0, fields, rims, edges, coefs, results)
    if pair_count % SUB:
        every = jnp.swapaxes(every, 0, 1).reshape(1, 2, cols, rows)

    new_r, new_phi, potential = add_gravity(
        every,
        inverse_mid,
        basis[:2],
        density,
        results[1],
        results[2],
    )
    return results[0], new_r, new_phi, potential


def solution(mesh):
    az_count, rad_count = mesh.shape["az"], mesh.shape["rad"]
    field = P(None, "rad", "az")
    kernel = P("az", "rad", None)
    return jax.shard_map(
        lambda *args: local(az_count, rad_count, *args),
        mesh=mesh,
        in_specs=(field, field, field, kernel, kernel),
        out_specs=(field, field, field, P("rad", "az")),
        check_vma=False,
    )
```

```python
import math

import jax
import jax.numpy as jnp
from jax import lax
from jax.experimental import pallas as pl
from jax.experimental.pallas import tpu as pltpu
from jax.sharding import PartitionSpec as P

aspect_sq = 0.0025
LANES = 128
SUB = 8
VMEM_BYTES = 60 << 20


def fetch_rows(refs, buffers, sems, steps):
    block = refs[0].shape[1] // steps

    def copy(k, place):
        if isinstance(place, int):
            rows = pl.ds(place * block, block)
        else:
            rows = pl.ds(pl.multiple_of(place * block, block), block)
        return pltpu.make_async_copy(refs[k].at[:, rows], buffers[k].at[:, rows], sems.at[k, place])

    @pl.when(pl.program_id(0) == 0)
    def _():
        for place in range(steps):
            for k in range(len(refs)):
                copy(k, place).start()

    for k in range(len(refs)):
        copy(k, pl.program_id(0)).wait()
    return pl.ds(pl.multiple_of(pl.program_id(0) * block, block), block)


def split_bf16(x):
    high = x.astype(jnp.bfloat16)
    low = (x - high.astype(jnp.float32)).astype(jnp.bfloat16)
    return high, low


def pieces_of(x, count):
    out = []
    for _ in range(count - 1):
        high = lax.reduce_precision(x, 8, 7)
        out.append(high.astype(jnp.bfloat16))
        x = x - high
    return out + [x.astype(jnp.bfloat16)]


EDGE_ROWS = 16


def modes_kernel(scale, steps, refs):
    *tables, out_ref, wide_ref, density, sems = refs[1:]
    thin_ref = tables[2]
    layers = density.shape[0]
    rows_here = fetch_rows(refs[:1], [density], sems, steps)
    cols = thin_ref.shape[0]

    @pl.when(pl.program_id(0) == 0)
    def _():
        wide_ref[:cols] = tables[0][...]
        wide_ref[cols:] = tables[1][...]

    x = density[0, rows_here, :]
    for layer in range(1, layers):
        x = x + density[layer, rows_here, :]
    high = x.astype(jnp.bfloat16)
    x = x - high.astype(jnp.float32)
    mid = x.astype(jnp.bfloat16)
    low = (x - mid.astype(jnp.float32)).astype(jnp.bfloat16)

    def product(a, table):
        return lax.dot_general(
            a, table, (((1,), (1,)), ((), ())), preferred_element_type=jnp.float32
        )

    rows = high.shape[0]
    major = product(jnp.concatenate([high, mid, low], axis=0), wide_ref[...])
    small = major[2 * rows :, :cols] + product(high, thin_ref[...])
    total = major[:rows, :cols] + (
        major[:rows, cols:] + major[rows : 2 * rows, :cols] + (major[rows : 2 * rows, cols:] + small)
    )
    out_ref[...] = (scale * total).T


def edge_kernel(refs):
    firsts, lasts = refs[:3], refs[3:6]
    first_ref, last_ref = refs[6:]
    layers, block, _ = firsts[0].shape
    lane = lax.broadcasted_iota(jnp.int32, (block, LANES), 1)
    edges = jnp.zeros((block, LANES), jnp.float32)
    for layer in range(layers):
        for base, place, tiles in ((0, 0, firsts), (EDGE_ROWS, LANES - 1, lasts)):
            for comp, tile in enumerate(tiles):
                edges = jnp.where(
                    lane == base + 3 * layer + comp,
                    jnp.broadcast_to(tile[layer, :, place : place + 1], (block, LANES)),
                    edges,
                )
    edges = edges.T
    first_ref[...] = edges[:EDGE_ROWS].astype(jnp.bfloat16)
    last_ref[...] = edges[EDGE_ROWS : 2 * EDGE_ROWS].astype(jnp.bfloat16)


def edge_cells(fields):
    layers, rows, cells = fields[0].shape
    block = min(rows, 4 * LANES)
    first = pl.BlockSpec((layers, block, LANES), lambda i: (0, i, 0))
    last = pl.BlockSpec((layers, block, LANES), lambda i: (0, i, cells // LANES - 1))
    edge_spec = pl.BlockSpec((EDGE_ROWS, block), lambda i: (0, i))
    edge_shape = jax.ShapeDtypeStruct((EDGE_ROWS, rows), jnp.bfloat16)
    return pl.pallas_call(
        lambda *refs: edge_kernel(refs),
        grid=(rows // block,),
        in_specs=[first] * 3 + [last] * 3,
        out_specs=[edge_spec, edge_spec],
        out_shape=[edge_shape, edge_shape],
        compiler_params=pltpu.CompilerParams(vmem_limit_bytes=VMEM_BYTES),
        cost_estimate=pl.CostEstimate(
            flops=40 * rows * LANES, bytes_accessed=24 * layers * rows * LANES, transcendentals=0
        ),
        name="edge_cells",
    )(*fields, *fields)


def surface_modes(density, tables, scale):
    layers, rows, cells = density.shape
    cols = tables[0].shape[0]
    block = min(rows, 2 * LANES)
    table_spec = pl.BlockSpec((cols, cells), lambda i: (0, 0))
    return pl.pallas_call(
        lambda *refs: modes_kernel(scale, rows // block, refs),
        grid=(rows // block,),
        in_specs=[pl.BlockSpec(memory_space=pl.ANY)] + [table_spec] * 3,
        out_specs=pl.BlockSpec((cols, block), lambda i: (0, i)),
        out_shape=jax.ShapeDtypeStruct((cols, rows), jnp.float32),
        scratch_shapes=[
            pltpu.VMEM((2 * cols, cells), jnp.bfloat16),
            pltpu.VMEM(density.shape, jnp.float32),
            pltpu.SemaphoreType.DMA((1, rows // block)),
        ],
        compiler_params=pltpu.CompilerParams(vmem_limit_bytes=VMEM_BYTES),
        cost_estimate=pl.CostEstimate(
            flops=12 * rows * cells * cols, bytes_accessed=4 * density.size, transcendentals=0
        ),
        name="surface_modes",
    )(density, *tables)


def response_kernel(steps, refs):
    pairs_ref, pot_ref, force_ref, out_ref, pot_buffer, force_buffer, sems = refs
    pairs = pairs_ref[...]
    buffers = (pot_buffer, force_buffer)
    rows_here = fetch_rows((pot_ref, force_ref), buffers, sems, steps)
    block, cols = out_ref.shape[3], pairs.shape[0]
    mode_of = lax.broadcasted_iota(jnp.int32, (block, cols), 1) // 2
    for place, buffer in enumerate(buffers):
        total = jnp.zeros(mode_of.shape, jnp.float32)
        for mode in range(buffer.shape[0]):
            part = lax.dot_general(
                buffer[mode, rows_here, :],
                pairs,
                (((1,), (1,)), ((), ())),
                preferred_element_type=jnp.float32,
            )
            total = jnp.where(mode_of == mode, part, total)
        out_ref[:, place] = jnp.broadcast_to(total.T[None], (out_ref.shape[0], cols, block))


def responses(pairs, potential_kernel, force_kernel, copies):
    mode_count, rows, count = potential_kernel.shape
    cols = pairs.shape[0]
    block = min(rows, LANES)
    steps = rows // block
    whole = pl.BlockSpec(memory_space=pl.ANY)
    return pl.pallas_call(
        lambda *refs: response_kernel(steps, refs),
        grid=(steps,),
        in_specs=[pl.BlockSpec((cols, count), lambda i: (0, 0)), whole, whole],
        out_specs=pl.BlockSpec((copies, 2, cols, block), lambda i: (0, 0, 0, i)),
        out_shape=jax.ShapeDtypeStruct((copies, 2, cols, rows), jnp.float32),
        scratch_shapes=[
            pltpu.VMEM(potential_kernel.shape, potential_kernel.dtype),
            pltpu.VMEM(force_kernel.shape, force_kernel.dtype),
            pltpu.SemaphoreType.DMA((2, steps)),
        ],
        compiler_params=pltpu.CompilerParams(vmem_limit_bytes=VMEM_BYTES),
        cost_estimate=pl.CostEstimate(
            flops=4 * rows * count * cols * mode_count,
            bytes_accessed=4 * potential_kernel.size,
            transcendentals=0,
        ),
        name="responses",
    )(pairs, potential_kernel, force_kernel)


ROOT_FACE, SOUND_FACE, IN, OUT, ROOT_MID, SOUND_MID, AZ, SPIN, PULL = range(9)
COEFS = 16


def row_coefficients(first_row, rows, step):
    face = jnp.exp((first_row + jnp.arange(rows + LANES + 1)).astype(jnp.float32) * step)
    inner, outer = face[:-1], face[1:]
    mid = 0.5 * (inner + outer)
    area = 0.5 * (outer * outer - inner * inner)
    sound_face = aspect_sq / inner
    sound_mid = aspect_sq / mid
    radial = (0.05 * step) / area
    columns = [
        jnp.sqrt(sound_face),
        sound_face,
        radial * inner,
        radial * outer,
        jnp.sqrt(sound_mid),
        sound_mid,
        0.05 / mid,
        (0.1 * step) / mid,
        (0.1 * step) / (mid * mid),
    ]
    columns += [jnp.zeros_like(mid)] * (COEFS - len(columns))
    return jnp.stack(columns, axis=0), (-0.1 / mid)[None, :rows]


def inverse(x):
    guess = pl.reciprocal(x, approx=True)
    return guess * (2.0 - x * guess)


class FluxBlock:
    def __init__(self, block_count, refs):
        self.fields = refs[0:3]
        self.before = refs[3:6]
        self.after = refs[6:9]
        self.rim_in, self.rim_out, coef_rows, low_rows, high_rows, coef_after = refs[9:15]
        self.block_count = block_count
        self.rows, cells = self.fields[0].shape
        self.columns = cells // LANES
        self.strips = self.rows // SUB
        self.index = pl.program_id(0)
        self.lane = lax.broadcasted_iota(jnp.int32, (SUB, LANES), 1)
        side_rows = jnp.concatenate(
            [coef_rows[...], low_rows[...].astype(jnp.float32), high_rows[...].astype(jnp.float32)], axis=0
        )
        filler = jnp.zeros((LANES - side_rows.shape[0], self.rows), jnp.float32)
        self.side = jnp.concatenate([side_rows, filler], axis=0).T
        self.coef_after = coef_after

    def wide(self, column):
        return jnp.broadcast_to(column, (SUB, LANES))

    def at(self, col):
        return pl.ds(col * LANES, LANES)

    def rows_at(self, place):
        return pl.ds(pl.multiple_of(place * SUB, SUB), SUB)

    def radial_state(self, state):
        density, mom_r, mom_phi = state
        inv = inverse(density)
        vel = mom_r * inv
        return inv, (density, mom_r, mom_phi, jnp.abs(vel), mom_r * vel, mom_phi * vel)

    def radial_flux(self, upper, lower, root, sound):
        speed = jnp.maximum(upper[3], lower[3]) + root
        return (
            (upper[1] + lower[1]) - speed * (upper[0] - lower[0]),
            ((upper[4] + lower[4]) + sound * (upper[0] + lower[0]))
            - speed * (upper[1] - lower[1]),
            (upper[5] + lower[5]) - speed * (upper[2] - lower[2]),
        )

    def azimuth_flux(self, upper, lower, root):
        speed = jnp.maximum(upper[3], lower[3]) + root
        return (
            (upper[2] + lower[2]) - speed * (upper[0] - lower[0]),
            (upper[4] + lower[4]) - speed * (upper[1] - lower[1]),
            (upper[5] + lower[5]) - speed * (upper[2] - lower[2]),
        )

    def azimuth_values(self, state, inv, cross, sound):
        density, mom_r, mom_phi = state
        vel = mom_phi * inv
        return density, mom_r, mom_phi, jnp.abs(vel), cross, mom_phi * vel + sound * density

    def ghost_values(self, layer, coef, side, sound):
        base = COEFS + side * EDGE_ROWS + 3 * layer
        state = [self.wide(coef[:, base + c : base + c + 1]) for c in range(3)]
        inv = inverse(state[0])
        return self.azimuth_values(state, inv, state[1] * state[2] * inv, sound)

    def row_before(self, col):
        return self.edge_row(col, self.index == 0, self.rim_in, self.before, SUB - 1)

    def row_after(self, col):
        return self.edge_row(col, self.index == self.block_count - 1, self.rim_out, self.after, 0)

    def edge_row(self, col, edge, rim, near, row):
        state = []
        for comp in range(3):
            value = jnp.where(
                edge, rim[comp : comp + 1, self.at(col)], near[comp][row : row + 1, self.at(col)]
            )
            state.append(jnp.broadcast_to(value, (SUB, LANES)))
        return self.radial_state(state)[1]

    def columns_of(self, coef, names):
        return [self.wide(coef[:, k : k + 1]) for k in names]


CELL_VALUES = 8


def flux_kernel(unroll, layer, block_count, refs):
    block = FluxBlock(block_count, refs)
    outs = refs[-8:-5]
    side, cell, faces, sides, held = refs[-5:]
    side[...] = block.side
    lane, at, fields, rows_at = block.lane, block.at, block.fields, block.rows_at
    columns, strips, rows = block.columns, block.strips, block.rows

    after = block.coef_after[...].T
    root_face, sound_face = block.columns_of(after[:SUB], (ROOT_FACE, SOUND_FACE))
    for col in range(columns):
        for slot, value in enumerate(block.row_before(col)):
            cell[slot, col, 0:SUB, :] = value
        last = [
            jnp.broadcast_to(ref[rows - 1 : rows, at(col)], (SUB, LANES)) for ref in fields
        ]
        flux = block.radial_flux(
            block.row_after(col), block.radial_state(last)[1], root_face, sound_face
        )
        for comp in range(3):
            faces[comp, col, rows : rows + SUB, :] = flux[comp]

    def shifted(place, by):
        return pl.ds(pl.multiple_of(place * SUB, SUB) + by, SUB)

    def update(place):
        here, above = rows_at(place), shifted(place, 1)
        out_coef, az = block.columns_of(side[here, :], (OUT, AZ))
        for comp in range(3):
            low = sides[comp, here, at(0)]
            for col in range(columns):
                beyond = sides[comp, here, at(col + 1)]
                edge = jnp.where(lane == 0, beyond, low)
                low = beyond
                outs[comp][here, at(col)] = held[comp, here, at(col)] - (
                    out_coef * faces[comp, col, above, :] + az * pltpu.roll(edge, LANES - 1, 1)
                )

    def face_fluxes(place):
        here, inside, below = rows_at(place), rows_at(place + 1), shifted(place, SUB - 1)
        coef = side[here, :]
        root_face, sound_face, in_coef, root_mid, sound_mid, az, spin, pull = block.columns_of(
            coef, (ROOT_FACE, SOUND_FACE, IN, ROOT_MID, SOUND_MID, AZ, SPIN, PULL)
        )
        left = block.ghost_values(layer, coef, 0, sound_mid)
        for col in range(columns):
            now = [cell[slot, col, inside, :] for slot in range(CELL_VALUES)]
            lower = [cell[slot, col, below, :] for slot in range(6)]
            flux_r = block.radial_flux(now[:6], lower, root_face, sound_face)
            values = (*now[:3], now[6], now[5], now[7])
            lower = [
                pltpu.roll(jnp.where(lane == LANES - 1, a, b), 1, 1) for a, b in zip(left, values)
            ]
            left = values
            flux = block.azimuth_flux(values, lower, root_mid)
            for comp in range(3):
                faces[comp, col, here, :] = flux_r[comp]
                sides[comp, here, at(col)] = flux[comp]
            held[0, here, at(col)] = now[0] + (in_coef * flux_r[0] + az * flux[0])
            held[1, here, at(col)] = (now[1] + (in_coef * flux_r[1] + az * flux[1])) + (
                spin * now[7] - pull * now[0]
            )
            held[2, here, at(col)] = (now[2] + (in_coef * flux_r[2] + az * flux[2])) - spin * now[5]
        values = block.ghost_values(layer, coef, 1, sound_mid)
        lower = [pltpu.roll(a, 1, 1) for a in left]
        for comp, value in enumerate(block.azimuth_flux(values, lower, root_mid)):
            sides[comp, here, at(columns)] = value

    def cell_values(place):
        here, inside = rows_at(place), rows_at(place + 1)
        (sound_mid,) = block.columns_of(side[here, :], (SOUND_MID,))
        for col in range(columns):
            state = [ref[here, at(col)] for ref in fields]
            inv, values = block.radial_state(state)
            vel = state[2] * inv
            values = (*values, jnp.abs(vel), state[2] * vel + sound_mid * state[0])
            for slot, value in enumerate(values):
                cell[slot, col, inside, :] = value

    def iteration(place, carry):
        for stage, late in ((update, 3), (face_fluxes, 1), (cell_values, 0)):
            first = jnp.clip(place - late, 0, strips // unroll - 1) * unroll
            for k in range(unroll):
                stage(first + k)
        return carry

    lax.fori_loop(0, strips // unroll + 3, iteration, 0)


def flux_layer(layer, unroll, fields, rims, edges, coefs, so_far):
    layers, rows, cells = fields[0].shape
    block = min(rows, 2 * LANES)
    count = rows // block
    per = block // SUB
    main = pl.BlockSpec((None, block, cells), lambda i: (layer, i, 0))
    before = pl.BlockSpec((None, SUB, cells), lambda i: (layer, jnp.maximum(i * per - 1, 0), 0))
    after = pl.BlockSpec(
        (None, SUB, cells), lambda i: (layer, jnp.minimum((i + 1) * per, rows // SUB - 1), 0)
    )
    rim = pl.BlockSpec((None, 3, cells), lambda i: (layer, 0, 0))
    operands = [*fields, *fields, *fields, *rims, coefs, *edges, coefs]
    specs = [main] * 3 + [before] * 3 + [after] * 3 + [
        rim,
        rim,
        pl.BlockSpec((COEFS, block), lambda i: (0, i)),
        pl.BlockSpec((EDGE_ROWS, block), lambda i: (0, i)),
        pl.BlockSpec((EDGE_ROWS, block), lambda i: (0, i)),
        pl.BlockSpec((COEFS, LANES), lambda i: (0, (i + 1) * (block // LANES))),
    ]
    aliases = {}
    if so_far is not None:
        for k, array in enumerate(so_far):
            aliases[len(operands)] = k
            operands.append(array)
            specs.append(pl.BlockSpec(memory_space=pl.ANY))
    scratch = [
        pltpu.VMEM((block, LANES), jnp.float32),
        pltpu.VMEM((CELL_VALUES, cells // LANES, block + SUB, LANES), jnp.float32),
        pltpu.VMEM((3, cells // LANES, block + SUB, LANES), jnp.float32),
        pltpu.VMEM((3, block, cells + LANES), jnp.float32),
        pltpu.VMEM((3, block, cells), jnp.float32),
    ]
    return pl.pallas_call(
        lambda *refs: flux_kernel(unroll, layer, count, refs),
        grid=(count,),
        in_specs=specs,
        out_specs=[main] * 3,
        out_shape=[jax.ShapeDtypeStruct(f.shape, f.dtype) for f in fields],
        scratch_shapes=scratch,
        input_output_aliases=aliases,
        compiler_params=pltpu.CompilerParams(vmem_limit_bytes=VMEM_BYTES),
        cost_estimate=pl.CostEstimate(
            flops=100 * rows * cells, bytes_accessed=24 * rows * cells, transcendentals=rows * cells
        ),
        name="flux_layer",
    )(*operands)


def gravity_kernel(steps, refs):
    every_ref, inverse_ref = refs[:2]
    halves = refs[2:4]
    out_r, out_phi, out_pot, table_ref, *buffers, sems = refs[7:]
    density, mom_r, mom_phi = buffers
    rows_here = fetch_rows(refs[4:7], buffers, sems, steps)
    copies, _, part, block = every_ref.shape
    cols = copies * part

    @pl.when(pl.program_id(0) == 0)
    def _():
        table_ref[:cols] = halves[0][...]
        table_ref[cols : 2 * cols] = halves[0][...]
        table_ref[2 * cols :] = halves[1][...]

    pot = every_ref[:, 0].reshape(cols, block)
    force = every_ref[:, 1].reshape(cols, block)
    row = lax.broadcasted_iota(jnp.int32, pot.shape, 0)
    even = row % 2 == 0
    mode = (row // 2).astype(jnp.float32)
    swapped = jnp.where(even, pltpu.roll(pot, cols - 1, 0), -pltpu.roll(pot, 1, 0))
    left = jnp.concatenate(
        [pot, 0.1 * force, swapped * (mode * inverse_ref[...])], axis=1
    )
    high, low = split_bf16(left)
    grid = lax.dot_general(
        jnp.concatenate([high, low, high], axis=0),
        table_ref[...],
        (((0,), (0,)), ((), ())),
        preferred_element_type=jnp.float32,
    )
    out_pot[...] = grid[:block]
    for layer in range(density.shape[0]):
        here = density[layer, rows_here, :]
        out_r[layer] = mom_r[layer, rows_here, :] + here * grid[block : 2 * block]
        out_phi[layer] = mom_phi[layer, rows_here, :] + here * grid[2 * block :]


def add_gravity(every, inverse_mid, tables, density, mom_r, mom_phi):
    layers, rows, cells = density.shape
    cols = every.shape[0] * every.shape[2]
    block = min(rows, 2 * LANES)
    modes_spec = pl.BlockSpec((*every.shape[:3], block), lambda i: (0, 0, 0, i))
    table_spec = pl.BlockSpec((cols, cells), lambda i: (0, 0))

    field = pl.BlockSpec((layers, block, cells), lambda i: (0, i, 0))
    grid_shape = jax.ShapeDtypeStruct(density.shape, density.dtype)
    return pl.pallas_call(
        lambda *refs: gravity_kernel(rows // block, refs),
        grid=(rows // block,),
        in_specs=[
            modes_spec, pl.BlockSpec((1, block), lambda i: (0, i)),
        ] + [table_spec] * 2 + [pl.BlockSpec(memory_space=pl.ANY)] * 3,
        out_specs=[field, field, pl.BlockSpec((block, cells), lambda i: (i, 0))],
        out_shape=[grid_shape, grid_shape, jax.ShapeDtypeStruct((rows, cells), jnp.float32)],
        scratch_shapes=[pltpu.VMEM((3 * cols, cells), jnp.bfloat16)]
        + [pltpu.VMEM(density.shape, density.dtype)] * 3
        + [pltpu.SemaphoreType.DMA((3, rows // block))],
        compiler_params=pltpu.CompilerParams(vmem_limit_bytes=VMEM_BYTES),
        cost_estimate=pl.CostEstimate(
            flops=18 * rows * cells * cols, bytes_accessed=44 * rows * cells, transcendentals=0
        ),
        name="add_gravity",
    )(
        every, inverse_mid, *tables,
        density, mom_r, mom_phi,
    )


def exchange_rims(fields, rad_index, rad_count):
    first = jnp.stack([f[:, 0] for f in fields], axis=1)
    last = jnp.stack([f[:, -1] for f in fields], axis=1)
    if rad_count == 1:
        return first, last
    first_out, last_out = first.astype(jnp.bfloat16), last.astype(jnp.bfloat16)
    if rad_count == 2:
        other = lax.ppermute(
            jnp.where(rad_index == 0, last_out, first_out), "rad", [(0, 1), (1, 0)]
        )
        low = high = other
    else:
        up = [(i, i + 1) for i in range(rad_count - 1)]
        low = lax.ppermute(last_out, "rad", up)
        high = lax.ppermute(first_out, "rad", [(b, a) for a, b in up])
    rim_in = jnp.where(rad_index == 0, first, low.astype(first.dtype))
    rim_out = jnp.where(rad_index == rad_count - 1, last, high.astype(last.dtype))
    return rim_in, rim_out


def exchange_edges(first, last, az_count):
    right = [(i, (i + 1) % az_count) for i in range(az_count)]
    left = [(b, a) for a, b in right]
    return lax.ppermute(last, "az", right), lax.ppermute(first, "az", left)


def local(az_count, rad_count, density, mom_r, mom_phi, potential_kernel, force_kernel):
    layers, rows, cells = density.shape
    mode_count = potential_kernel.shape[0]
    pair_count = 2 * mode_count
    cols = az_count * pair_count
    step = 2.0 * math.pi / (az_count * cells)
    az_index = lax.axis_index("az")
    rad_index = lax.axis_index("rad")
    fields = (density, mom_r, mom_phi)

    azimuth = ((az_index * cells + jnp.arange(cells)).astype(jnp.float32) + 0.5) * step
    row = lax.broadcasted_iota(jnp.int32, (cols, cells), 0)
    mode = (row // 2).astype(jnp.float32)
    angle = azimuth[None, :] * mode
    cosine, sine = jnp.cos(angle), jnp.sin(angle)
    basis = pieces_of(jnp.where(row % 2 == 0, cosine, sine), 3)

    rims = exchange_rims(fields, rad_index, rad_count)
    coefs, inverse_mid = row_coefficients(rad_index * rows, rows, step)

    first, last = edge_cells(fields)
    basis, first, last = lax.optimization_barrier((basis, first, last))
    edges = exchange_edges(first, last, az_count)
    partial = surface_modes(density, basis, 1.0 / (az_count * cells))
    partial, edges, rims = lax.optimization_barrier((partial, edges, rims))
    pieces = lax.all_to_all(
        partial.reshape(az_count, pair_count, rows), "az", split_axis=0, concat_axis=0, tiled=True
    )
    results = flux_layer(0, 1, fields, rims, edges, coefs, None)
    pieces, results = lax.optimization_barrier((pieces, results))

    own = jnp.sum(pieces, axis=0).astype(jnp.bfloat16)
    pairs = lax.all_gather(own, "rad", axis=1, tiled=True)
    parts = responses(pairs, potential_kernel, force_kernel, az_count)
    every = lax.all_to_all(parts, "az", split_axis=0, concat_axis=0, tiled=True)
    coefs, parts = lax.optimization_barrier((coefs, parts))
    for layer in range(1, layers):
        results = flux_layer(layer, 2, fields, rims, edges, coefs, results)
    if pair_count % SUB:
        every = jnp.swapaxes(every, 0, 1).reshape(1, 2, cols, rows)

    new_r, new_phi, potential = add_gravity(
        every,
        inverse_mid,
        basis[:2],
        density,
        results[1],
        results[2],
    )
    return results[0], new_r, new_phi, potential


def solution(mesh):
    az_count, rad_count = mesh.shape["az"], mesh.shape["rad"]
    field = P(None, "rad", "az")
    kernel = P("az", "rad", None)
    return jax.shard_map(
        lambda *args: local(az_count, rad_count, *args),
        mesh=mesh,
        in_specs=(field, field, field, kernel, kernel),
        out_specs=(field, field, field, P("rad", "az")),
        check_vma=False,
    )
```

```python
import math

import jax
import jax.numpy as jnp
from jax import lax
from jax.experimental import pallas as pl
from jax.experimental.pallas import tpu as pltpu
from jax.sharding import PartitionSpec as P

aspect_sq = 0.0025
LANES = 128
SUB = 8
VMEM_BYTES = 60 << 20


def fetch_rows(refs, buffers, sems, steps):
    block = refs[0].shape[1] // steps

    def copy(k, place):
        if isinstance(place, int):
            rows = pl.ds(place * block, block)
        else:
            rows = pl.ds(pl.multiple_of(place * block, block), block)
        return pltpu.make_async_copy(refs[k].at[:, rows], buffers[k].at[:, rows], sems.at[k, place])

    @pl.when(pl.program_id(0) == 0)
    def _():
        for place in range(steps):
            for k in range(len(refs)):
                copy(k, place).start()

    for k in range(len(refs)):
        copy(k, pl.program_id(0)).wait()
    return pl.ds(pl.multiple_of(pl.program_id(0) * block, block), block)


def split_bf16(x):
    high = x.astype(jnp.bfloat16)
    low = (x - high.astype(jnp.float32)).astype(jnp.bfloat16)
    return high, low


def pieces_of(x, count):
    out = []
    for _ in range(count - 1):
        high = lax.reduce_precision(x, 8, 7)
        out.append(high.astype(jnp.bfloat16))
        x = x - high
    return out + [x.astype(jnp.bfloat16)]


EDGE_ROWS = 16


def modes_kernel(scale, steps, refs):
    *tables, out_ref, wide_ref, density, sems = refs[1:]
    thin_ref = tables[2]
    layers = density.shape[0]
    rows_here = fetch_rows(refs[:1], [density], sems, steps)
    cols = thin_ref.shape[0]

    @pl.when(pl.program_id(0) == 0)
    def _():
        wide_ref[:cols] = tables[0][...]
        wide_ref[cols:] = tables[1][...]

    x = density[0, rows_here, :]
    for layer in range(1, layers):
        x = x + density[layer, rows_here, :]
    high = x.astype(jnp.bfloat16)
    x = x - high.astype(jnp.float32)
    mid = x.astype(jnp.bfloat16)
    low = (x - mid.astype(jnp.float32)).astype(jnp.bfloat16)

    def product(a, table):
        return lax.dot_general(
            a, table, (((1,), (1,)), ((), ())), preferred_element_type=jnp.float32
        )

    rows = high.shape[0]
    major = product(jnp.concatenate([high, mid, low], axis=0), wide_ref[...])
    small = major[2 * rows :, :cols] + product(high, thin_ref[...])
    total = major[:rows, :cols] + (
        major[:rows, cols:] + major[rows : 2 * rows, :cols] + (major[rows : 2 * rows, cols:] + small)
    )
    out_ref[...] = (scale * total).T


def edge_kernel(refs):
    firsts, lasts = refs[:3], refs[3:6]
    first_ref, last_ref = refs[6:]
    layers, block, _ = firsts[0].shape
    lane = lax.broadcasted_iota(jnp.int32, (block, LANES), 1)
    edges = jnp.zeros((block, LANES), jnp.float32)
    for layer in range(layers):
        for base, place, tiles in ((0, 0, firsts), (EDGE_ROWS, LANES - 1, lasts)):
            for comp, tile in enumerate(tiles):
                edges = jnp.where(
                    lane == base + 3 * layer + comp,
                    jnp.broadcast_to(tile[layer, :, place : place + 1], (block, LANES)),
                    edges,
                )
    edges = edges.T
    first_ref[...] = edges[:EDGE_ROWS].astype(jnp.bfloat16)
    last_ref[...] = edges[EDGE_ROWS : 2 * EDGE_ROWS].astype(jnp.bfloat16)


def edge_cells(fields):
    layers, rows, cells = fields[0].shape
    block = min(rows, 4 * LANES)
    first = pl.BlockSpec((layers, block, LANES), lambda i: (0, i, 0))
    last = pl.BlockSpec((layers, block, LANES), lambda i: (0, i, cells // LANES - 1))
    edge_spec = pl.BlockSpec((EDGE_ROWS, block), lambda i: (0, i))
    edge_shape = jax.ShapeDtypeStruct((EDGE_ROWS, rows), jnp.bfloat16)
    return pl.pallas_call(
        lambda *refs: edge_kernel(refs),
        grid=(rows // block,),
        in_specs=[first] * 3 + [last] * 3,
        out_specs=[edge_spec, edge_spec],
        out_shape=[edge_shape, edge_shape],
        compiler_params=pltpu.CompilerParams(vmem_limit_bytes=VMEM_BYTES),
        cost_estimate=pl.CostEstimate(
            flops=40 * rows * LANES, bytes_accessed=24 * layers * rows * LANES, transcendentals=0
        ),
        name="edge_cells",
    )(*fields, *fields)


def surface_modes(density, tables, scale):
    layers, rows, cells = density.shape
    cols = tables[0].shape[0]
    block = min(rows, 2 * LANES)
    table_spec = pl.BlockSpec((cols, cells), lambda i: (0, 0))
    return pl.pallas_call(
        lambda *refs: modes_kernel(scale, rows // block, refs),
        grid=(rows // block,),
        in_specs=[pl.BlockSpec(memory_space=pl.ANY)] + [table_spec] * 3,
        out_specs=pl.BlockSpec((cols, block), lambda i: (0, i)),
        out_shape=jax.ShapeDtypeStruct((cols, rows), jnp.float32),
        scratch_shapes=[
            pltpu.VMEM((2 * cols, cells), jnp.bfloat16),
            pltpu.VMEM(density.shape, jnp.float32),
            pltpu.SemaphoreType.DMA((1, rows // block)),
        ],
        compiler_params=pltpu.CompilerParams(vmem_limit_bytes=VMEM_BYTES),
        cost_estimate=pl.CostEstimate(
            flops=12 * rows * cells * cols, bytes_accessed=4 * density.size, transcendentals=0
        ),
        name="surface_modes",
    )(density, *tables)


def response_kernel(steps, refs):
    pairs_ref, pot_ref, force_ref, out_ref, pot_buffer, force_buffer, sems = refs
    pairs = pairs_ref[...]
    buffers = (pot_buffer, force_buffer)
    rows_here = fetch_rows((pot_ref, force_ref), buffers, sems, steps)
    block, cols = out_ref.shape[3], pairs.shape[0]
    mode_of = lax.broadcasted_iota(jnp.int32, (block, cols), 1) // 2
    for place, buffer in enumerate(buffers):
        total = jnp.zeros(mode_of.shape, jnp.float32)
        for mode in range(buffer.shape[0]):
            part = lax.dot_general(
                buffer[mode, rows_here, :],
                pairs,
                (((1,), (1,)), ((), ())),
                preferred_element_type=jnp.float32,
            )
            total = jnp.where(mode_of == mode, part, total)
        out_ref[:, place] = jnp.broadcast_to(total.T[None], (out_ref.shape[0], cols, block))


def responses(pairs, potential_kernel, force_kernel, copies):
    mode_count, rows, count = potential_kernel.shape
    cols = pairs.shape[0]
    block = min(rows, LANES)
    steps = rows // block
    whole = pl.BlockSpec(memory_space=pl.ANY)
    return pl.pallas_call(
        lambda *refs: response_kernel(steps, refs),
        grid=(steps,),
        in_specs=[pl.BlockSpec((cols, count), lambda i: (0, 0)), whole, whole],
        out_specs=pl.BlockSpec((copies, 2, cols, block), lambda i: (0, 0, 0, i)),
        out_shape=jax.ShapeDtypeStruct((copies, 2, cols, rows), jnp.float32),
        scratch_shapes=[
            pltpu.VMEM(potential_kernel.shape, potential_kernel.dtype),
            pltpu.VMEM(force_kernel.shape, force_kernel.dtype),
            pltpu.SemaphoreType.DMA((2, steps)),
        ],
        compiler_params=pltpu.CompilerParams(vmem_limit_bytes=VMEM_BYTES),
        cost_estimate=pl.CostEstimate(
            flops=4 * rows * count * cols * mode_count,
            bytes_accessed=4 * potential_kernel.size,
            transcendentals=0,
        ),
        name="responses",
    )(pairs, potential_kernel, force_kernel)


ROOT_FACE, SOUND_FACE, IN, OUT, ROOT_MID, SOUND_MID, AZ, SPIN, PULL = range(9)
COEFS = 16


def row_coefficients(first_row, rows, step):
    face = jnp.exp((first_row + jnp.arange(rows + LANES + 1)).astype(jnp.float32) * step)
    inner, outer = face[:-1], face[1:]
    mid = 0.5 * (inner + outer)
    area = 0.5 * (outer * outer - inner * inner)
    sound_face = aspect_sq / inner
    sound_mid = aspect_sq / mid
    radial = (0.05 * step) / area
    columns = [
        jnp.sqrt(sound_face),
        sound_face,
        radial * inner,
        radial * outer,
        jnp.sqrt(sound_mid),
        sound_mid,
        0.05 / mid,
        (0.1 * step) / mid,
        (0.1 * step) / (mid * mid),
    ]
    columns += [jnp.zeros_like(mid)] * (COEFS - len(columns))
    return jnp.stack(columns, axis=0), (-0.1 / mid)[None, :rows]


def inverse(x):
    guess = pl.reciprocal(x, approx=True)
    return guess * (2.0 - x * guess)


class FluxBlock:
    def __init__(self, block_count, refs):
        self.fields = refs[0:3]
        self.before = refs[3:6]
        self.after = refs[6:9]
        self.rim_in, self.rim_out, coef_rows, low_rows, high_rows, coef_after = refs[9:15]
        self.block_count = block_count
        self.rows, cells = self.fields[0].shape
        self.columns = cells // LANES
        self.strips = self.rows // SUB
        self.index = pl.program_id(0)
        self.lane = lax.broadcasted_iota(jnp.int32, (SUB, LANES), 1)
        side_rows = jnp.concatenate(
            [coef_rows[...], low_rows[...].astype(jnp.float32), high_rows[...].astype(jnp.float32)], axis=0
        )
        filler = jnp.zeros((LANES - side_rows.shape[0], self.rows), jnp.float32)
        self.side = jnp.concatenate([side_rows, filler], axis=0).T
        self.coef_after = coef_after

    def wide(self, column):
        return jnp.broadcast_to(column, (SUB, LANES))

    def at(self, col):
        return pl.ds(col * LANES, LANES)

    def rows_at(self, place):
        if isinstance(place, int):
            return pl.ds(place * SUB, SUB)
        return pl.ds(pl.multiple_of(place * SUB, SUB), SUB)

    def radial_state(self, state):
        density, mom_r, mom_phi = state
        inv = inverse(density)
        vel = mom_r * inv
        return inv, (density, mom_r, mom_phi, jnp.abs(vel), mom_r * vel, mom_phi * vel)

    def radial_flux(self, upper, lower, root, sound):
        speed = jnp.maximum(upper[3], lower[3]) + root
        return (
            (upper[1] + lower[1]) - speed * (upper[0] - lower[0]),
            ((upper[4] + lower[4]) + sound * (upper[0] + lower[0]))
            - speed * (upper[1] - lower[1]),
            (upper[5] + lower[5]) - speed * (upper[2] - lower[2]),
        )

    def azimuth_flux(self, upper, lower, root):
        speed = jnp.maximum(upper[3], lower[3]) + root
        return (
            (upper[2] + lower[2]) - speed * (upper[0] - lower[0]),
            (upper[4] + lower[4]) - speed * (upper[1] - lower[1]),
            (upper[5] + lower[5]) - speed * (upper[2] - lower[2]),
        )

    def azimuth_values(self, state, inv, cross, sound):
        density, mom_r, mom_phi = state
        vel = mom_phi * inv
        return density, mom_r, mom_phi, jnp.abs(vel), cross, mom_phi * vel + sound * density

    def ghost_values(self, layer, coef, side, sound):
        base = COEFS + side * EDGE_ROWS + 3 * layer
        state = [self.wide(coef[:, base + c : base + c + 1]) for c in range(3)]
        inv = inverse(state[0])
        return self.azimuth_values(state, inv, state[1] * state[2] * inv, sound)

    def row_before(self, col):
        return self.edge_row(col, self.index == 0, self.rim_in, self.before, SUB - 1)

    def row_after(self, col):
        return self.edge_row(col, self.index == self.block_count - 1, self.rim_out, self.after, 0)

    def edge_row(self, col, edge, rim, near, row):
        state = []
        for comp in range(3):
            value = jnp.where(
                edge, rim[comp : comp + 1, self.at(col)], near[comp][row : row + 1, self.at(col)]
            )
            state.append(jnp.broadcast_to(value, (SUB, LANES)))
        return self.radial_state(state)[1]

    def columns_of(self, coef, names):
        return [self.wide(coef[:, k : k + 1]) for k in names]


CELL_VALUES = 8


def flux_kernel(unroll, layer, block_count, refs):
    block = FluxBlock(block_count, refs)
    outs = refs[-8:-5]
    side, cell, faces, sides, held = refs[-5:]
    side[...] = block.side
    lane, at, fields, rows_at = block.lane, block.at, block.fields, block.rows_at
    columns, strips, rows = block.columns, block.strips, block.rows

    after = block.coef_after[...].T
    root_face, sound_face = block.columns_of(after[:SUB], (ROOT_FACE, SOUND_FACE))
    for col in range(columns):
        for slot, value in enumerate(block.row_before(col)):
            cell[slot, col, 0:SUB, :] = value
        last = [
            jnp.broadcast_to(ref[rows - 1 : rows, at(col)], (SUB, LANES)) for ref in fields
        ]
        flux = block.radial_flux(
            block.row_after(col), block.radial_state(last)[1], root_face, sound_face
        )
        for comp in range(3):
            faces[comp, col, rows : rows + SUB, :] = flux[comp]

    def shifted(place, by):
        if isinstance(place, int):
            return pl.ds(place * SUB + by, SUB)
        return pl.ds(pl.multiple_of(place * SUB, SUB) + by, SUB)

    def update(place):
        here, above = rows_at(place), shifted(place, 1)
        out_coef, az = block.columns_of(side[here, :], (OUT, AZ))
        for comp in range(3):
            low = sides[comp, here, at(0)]
            for col in range(columns):
                beyond = sides[comp, here, at(col + 1)]
                edge = jnp.where(lane == 0, beyond, low)
                low = beyond
                outs[comp][here, at(col)] = held[comp, here, at(col)] - (
                    out_coef * faces[comp, col, above, :] + az * pltpu.roll(edge, LANES - 1, 1)
                )

    def face_fluxes(place):
        here, inside, below = rows_at(place), rows_at(place + 1), shifted(place, SUB - 1)
        coef = side[here, :]
        root_face, sound_face, in_coef, root_mid, sound_mid, az, spin, pull = block.columns_of(
            coef, (ROOT_FACE, SOUND_FACE, IN, ROOT_MID, SOUND_MID, AZ, SPIN, PULL)
        )
        left = block.ghost_values(layer, coef, 0, sound_mid)
        for col in range(columns):
            now = [cell[slot, col, inside, :] for slot in range(CELL_VALUES)]
            lower = [cell[slot, col, below, :] for slot in range(6)]
            flux_r = block.radial_flux(now[:6], lower, root_face, sound_face)
            values = (*now[:3], now[6], now[5], now[7])
            lower = [
                pltpu.roll(jnp.where(lane == LANES - 1, a, b), 1, 1) for a, b in zip(left, values)
            ]
            left = values
            flux = block.azimuth_flux(values, lower, root_mid)
            for comp in range(3):
                faces[comp, col, here, :] = flux_r[comp]
                sides[comp, here, at(col)] = flux[comp]
            held[0, here, at(col)] = now[0] + (in_coef * flux_r[0] + az * flux[0])
            held[1, here, at(col)] = (now[1] + (in_coef * flux_r[1] + az * flux[1])) + (
                spin * now[7] - pull * now[0]
            )
            held[2, here, at(col)] = (now[2] + (in_coef * flux_r[2] + az * flux[2])) - spin * now[5]
        values = block.ghost_values(layer, coef, 1, sound_mid)
        lower = [pltpu.roll(a, 1, 1) for a in left]
        for comp, value in enumerate(block.azimuth_flux(values, lower, root_mid)):
            sides[comp, here, at(columns)] = value

    def cell_values(place):
        here, inside = rows_at(place), rows_at(place + 1)
        (sound_mid,) = block.columns_of(side[here, :], (SOUND_MID,))
        for col in range(columns):
            state = [ref[here, at(col)] for ref in fields]
            inv, values = block.radial_state(state)
            vel = state[2] * inv
            values = (*values, jnp.abs(vel), state[2] * vel + sound_mid * state[0])
            for slot, value in enumerate(values):
                cell[slot, col, inside, :] = value

    groups = strips // unroll

    def run(stage, group):
        for k in range(unroll):
            stage(group * unroll + k)

    def iteration(group, carry):
        run(update, group - 3)
        run(face_fluxes, group - 1)
        run(cell_values, group)
        return carry

    run(cell_values, 0)
    for group in (1, 2):
        run(face_fluxes, group - 1)
        run(cell_values, group)
    lax.fori_loop(3, groups, iteration, 0)
    run(update, groups - 3)
    run(face_fluxes, groups - 1)
    run(update, groups - 2)
    run(update, groups - 1)


def flux_layer(layer, unroll, fields, rims, edges, coefs, so_far):
    layers, rows, cells = fields[0].shape
    block = min(rows, 2 * LANES)
    count = rows // block
    per = block // SUB
    main = pl.BlockSpec((None, block, cells), lambda i: (layer, i, 0))
    before = pl.BlockSpec((None, SUB, cells), lambda i: (layer, jnp.maximum(i * per - 1, 0), 0))
    after = pl.BlockSpec(
        (None, SUB, cells), lambda i: (layer, jnp.minimum((i + 1) * per, rows // SUB - 1), 0)
    )
    rim = pl.BlockSpec((None, 3, cells), lambda i: (layer, 0, 0))
    operands = [*fields, *fields, *fields, *rims, coefs, *edges, coefs]
    specs = [main] * 3 + [before] * 3 + [after] * 3 + [
        rim,
        rim,
        pl.BlockSpec((COEFS, block), lambda i: (0, i)),
        pl.BlockSpec((EDGE_ROWS, block), lambda i: (0, i)),
        pl.BlockSpec((EDGE_ROWS, block), lambda i: (0, i)),
        pl.BlockSpec((COEFS, LANES), lambda i: (0, (i + 1) * (block // LANES))),
    ]
    aliases = {}
    if so_far is not None:
        for k, array in enumerate(so_far):
            aliases[len(operands)] = k
            operands.append(array)
            specs.append(pl.BlockSpec(memory_space=pl.ANY))
    scratch = [
        pltpu.VMEM((block, LANES), jnp.float32),
        pltpu.VMEM((CELL_VALUES, cells // LANES, block + SUB, LANES), jnp.float32),
        pltpu.VMEM((3, cells // LANES, block + SUB, LANES), jnp.float32),
        pltpu.VMEM((3, block, cells + LANES), jnp.float32),
        pltpu.VMEM((3, block, cells), jnp.float32),
    ]
    return pl.pallas_call(
        lambda *refs: flux_kernel(unroll, layer, count, refs),
        grid=(count,),
        in_specs=specs,
        out_specs=[main] * 3,
        out_shape=[jax.ShapeDtypeStruct(f.shape, f.dtype) for f in fields],
        scratch_shapes=scratch,
        input_output_aliases=aliases,
        compiler_params=pltpu.CompilerParams(vmem_limit_bytes=VMEM_BYTES),
        cost_estimate=pl.CostEstimate(
            flops=100 * rows * cells, bytes_accessed=24 * rows * cells, transcendentals=rows * cells
        ),
        name="flux_layer",
    )(*operands)


def gravity_kernel(steps, refs):
    every_ref, inverse_ref = refs[:2]
    halves = refs[2:4]
    out_r, out_phi, out_pot, table_ref, *buffers, sems = refs[7:]
    density, mom_r, mom_phi = buffers
    rows_here = fetch_rows(refs[4:7], buffers, sems, steps)
    copies, _, part, block = every_ref.shape
    cols = copies * part

    @pl.when(pl.program_id(0) == 0)
    def _():
        table_ref[:cols] = halves[0][...]
        table_ref[cols : 2 * cols] = halves[0][...]
        table_ref[2 * cols :] = halves[1][...]

    pot = every_ref[:, 0].reshape(cols, block)
    force = every_ref[:, 1].reshape(cols, block)
    row = lax.broadcasted_iota(jnp.int32, pot.shape, 0)
    even = row % 2 == 0
    mode = (row // 2).astype(jnp.float32)
    swapped = jnp.where(even, pltpu.roll(pot, cols - 1, 0), -pltpu.roll(pot, 1, 0))
    left = jnp.concatenate(
        [pot, 0.1 * force, swapped * (mode * inverse_ref[...])], axis=1
    )
    high, low = split_bf16(left)
    grid = lax.dot_general(
        jnp.concatenate([high, low, high], axis=0),
        table_ref[...],
        (((0,), (0,)), ((), ())),
        preferred_element_type=jnp.float32,
    )
    out_pot[...] = grid[:block]
    for layer in range(density.shape[0]):
        here = density[layer, rows_here, :]
        out_r[layer] = mom_r[layer, rows_here, :] + here * grid[block : 2 * block]
        out_phi[layer] = mom_phi[layer, rows_here, :] + here * grid[2 * block :]


def add_gravity(every, inverse_mid, tables, density, mom_r, mom_phi):
    layers, rows, cells = density.shape
    cols = every.shape[0] * every.shape[2]
    block = min(rows, 2 * LANES)
    modes_spec = pl.BlockSpec((*every.shape[:3], block), lambda i: (0, 0, 0, i))
    table_spec = pl.BlockSpec((cols, cells), lambda i: (0, 0))

    field = pl.BlockSpec((layers, block, cells), lambda i: (0, i, 0))
    grid_shape = jax.ShapeDtypeStruct(density.shape, density.dtype)
    return pl.pallas_call(
        lambda *refs: gravity_kernel(rows // block, refs),
        grid=(rows // block,),
        in_specs=[
            modes_spec, pl.BlockSpec((1, block), lambda i: (0, i)),
        ] + [table_spec] * 2 + [pl.BlockSpec(memory_space=pl.ANY)] * 3,
        out_specs=[field, field, pl.BlockSpec((block, cells), lambda i: (i, 0))],
        out_shape=[grid_shape, grid_shape, jax.ShapeDtypeStruct((rows, cells), jnp.float32)],
        scratch_shapes=[pltpu.VMEM((3 * cols, cells), jnp.bfloat16)]
        + [pltpu.VMEM(density.shape, density.dtype)] * 3
        + [pltpu.SemaphoreType.DMA((3, rows // block))],
        compiler_params=pltpu.CompilerParams(vmem_limit_bytes=VMEM_BYTES),
        cost_estimate=pl.CostEstimate(
            flops=18 * rows * cells * cols, bytes_accessed=44 * rows * cells, transcendentals=0
        ),
        name="add_gravity",
    )(
        every, inverse_mid, *tables,
        density, mom_r, mom_phi,
    )


def exchange_rims(fields, rad_index, rad_count):
    first = jnp.stack([f[:, 0] for f in fields], axis=1)
    last = jnp.stack([f[:, -1] for f in fields], axis=1)
    if rad_count == 1:
        return first, last
    first_out, last_out = first.astype(jnp.bfloat16), last.astype(jnp.bfloat16)
    if rad_count == 2:
        other = lax.ppermute(
            jnp.where(rad_index == 0, last_out, first_out), "rad", [(0, 1), (1, 0)]
        )
        low = high = other
    else:
        up = [(i, i + 1) for i in range(rad_count - 1)]
        low = lax.ppermute(last_out, "rad", up)
        high = lax.ppermute(first_out, "rad", [(b, a) for a, b in up])
    rim_in = jnp.where(rad_index == 0, first, low.astype(first.dtype))
    rim_out = jnp.where(rad_index == rad_count - 1, last, high.astype(last.dtype))
    return rim_in, rim_out


def exchange_edges(first, last, az_count):
    right = [(i, (i + 1) % az_count) for i in range(az_count)]
    left = [(b, a) for a, b in right]
    return lax.ppermute(last, "az", right), lax.ppermute(first, "az", left)


def local(az_count, rad_count, density, mom_r, mom_phi, potential_kernel, force_kernel):
    layers, rows, cells = density.shape
    mode_count = potential_kernel.shape[0]
    pair_count = 2 * mode_count
    cols = az_count * pair_count
    step = 2.0 * math.pi / (az_count * cells)
    az_index = lax.axis_index("az")
    rad_index = lax.axis_index("rad")
    fields = (density, mom_r, mom_phi)

    azimuth = ((az_index * cells + jnp.arange(cells)).astype(jnp.float32) + 0.5) * step
    row = lax.broadcasted_iota(jnp.int32, (cols, cells), 0)
    mode = (row // 2).astype(jnp.float32)
    angle = azimuth[None, :] * mode
    cosine, sine = jnp.cos(angle), jnp.sin(angle)
    basis = pieces_of(jnp.where(row % 2 == 0, cosine, sine), 3)

    rims = exchange_rims(fields, rad_index, rad_count)
    coefs, inverse_mid = row_coefficients(rad_index * rows, rows, step)

    first, last = edge_cells(fields)
    basis, first, last = lax.optimization_barrier((basis, first, last))
    edges = exchange_edges(first, last, az_count)
    partial = surface_modes(density, basis, 1.0 / (az_count * cells))
    partial, edges, rims = lax.optimization_barrier((partial, edges, rims))
    pieces = lax.all_to_all(
        partial.reshape(az_count, pair_count, rows), "az", split_axis=0, concat_axis=0, tiled=True
    )
    results = flux_layer(0, 2, fields, rims, edges, coefs, None)
    pieces, results = lax.optimization_barrier((pieces, results))

    own = jnp.sum(pieces, axis=0).astype(jnp.bfloat16)
    pairs = lax.all_gather(own, "rad", axis=1, tiled=True)
    parts = responses(pairs, potential_kernel, force_kernel, az_count)
    every = lax.all_to_all(parts, "az", split_axis=0, concat_axis=0, tiled=True)
    coefs, parts = lax.optimization_barrier((coefs, parts))
    for layer in range(1, layers):
        results = flux_layer(layer, 2, fields, rims, edges, coefs, results)
    if pair_count % SUB:
        every = jnp.swapaxes(every, 0, 1).reshape(1, 2, cols, rows)

    new_r, new_phi, potential = add_gravity(
        every,
        inverse_mid,
        basis[:2],
        density,
        results[1],
        results[2],
    )
    return results[0], new_r, new_phi, potential


def solution(mesh):
    az_count, rad_count = mesh.shape["az"], mesh.shape["rad"]
    field = P(None, "rad", "az")
    kernel = P("az", "rad", None)
    return jax.shard_map(
        lambda *args: local(az_count, rad_count, *args),
        mesh=mesh,
        in_specs=(field, field, field, kernel, kernel),
        out_specs=(field, field, field, P("rad", "az")),
        check_vma=False,
    )
```
